32 devices in a mesh: dp: 8 (over y, x, core), tensor: 4 (over z).
Axes of the slice: x: 2, y: 2, z: 4, core: 2. Of those that a mesh axis runs over, the one named last changes fastest.
Arguments:
- frames: bfloat16 [16, 1024, 1024], P('dp', 'tensor'), may hold values from -6 to 6
- cotangent: bfloat16 [16, 1024, 1024], P('dp', 'tensor'), may hold values from -6 to 6
- clip_valid: int32 [16], P('dp'), may hold values 0 or 1
- frame_counts: int32 [16], P('dp'), may hold values from 256 to 1024, as said below
- rel_rows: int32 [73], replicated, may hold values from 0 to 72, each once
- first_up: bfloat16 [1024, 4096], P('dp', 'tensor'), may hold values from -0.1875 to 0.1875
- first_down: bfloat16 [4096, 1024], P('tensor', 'dp'), may hold values from -0.1875 to 0.1875
- attend_in: bfloat16 [3, 1024, 1024], P(None, 'dp', 'tensor'), may hold values from -0.1875 to 0.1875
- attend_out: bfloat16 [1024, 1024], P('tensor', 'dp'), may hold values from -1.5 to 1.5
- pointwise_in: bfloat16 [2, 1024, 1024], P(None, 'dp', 'tensor'), may hold values from -0.1875 to 0.1875
- pointwise_out: bfloat16 [1024, 1024], P('tensor', 'dp'), may hold values from -0.25 to 0.25
- second_up: bfloat16 [1024, 4096], P('dp', 'tensor'), may hold values from -0.1875 to 0.1875
- second_down: bfloat16 [4096, 1024], P('tensor', 'dp'), may hold values from -0.1875 to 0.1875
- vectors: bfloat16 [56, 1024], P(None, 'dp')
- distance: bfloat16 [73, 64], replicated, may hold values from -6 to 6
Outputs:
- frames_out: bfloat16 [16, 1024, 1024], P('dp', 'tensor')
- frames_grad: bfloat16 [16, 1024, 1024], P('dp', 'tensor')
- grad_first_up: float32 [1024, 4096], P('dp', 'tensor')
- grad_first_down: float32 [4096, 1024], P('tensor', 'dp')
- grad_attend_in: float32 [3, 1024, 1024], P(None, 'dp', 'tensor')
- grad_attend_out: float32 [1024, 1024], P('tensor', 'dp')
- grad_pointwise_in: float32 [2, 1024, 1024], P(None, 'dp', 'tensor')
- grad_pointwise_out: float32 [1024, 1024], P('tensor', 'dp')
- grad_second_up: float32 [1024, 4096], P('dp', 'tensor')
- grad_second_down: float32 [4096, 1024], P('tensor', 'dp')
- grad_vectors: float32 [56, 1024], P(None, ('dp', 'tensor'))
- grad_distance: float32 [73, 64], replicated
The draws below stay inside these ranges and needn't reach their ends.
Inputs may be any that keep to these rules, and one draw needn't show every extreme that they name: `frame_counts`: in each aligned run of 2 slots (those of one index of dp) at least one has all 1024 frames. `rel_rows`: names each row of distance once.
All inputs are finite; a program needn't handle non-finite values. No bound on the sum of `clip_valid` on one device may be relied on, other than what follows from the above.
Results may differ from the reference program's by a relative error of at most 0.035.
Values may be sent and summed in bfloat16 or wider, within the bound.
No kernel may reach another device: no remote copies, remote signals or barrier semaphores. Data moves between devices by JAX's collectives and lax.ppermute only.
A program may use at most 256 MiB of HBM per device.

```python
import jax
import jax.numpy as jnp
from jax import lax

D = 1024
HEADS = 16
HEAD_DIM = 64
FF = 4096
KERNEL = 31
LEFT = 64
OFFSETS = 73
SLOT = 1024
MICRO = 2
CLIPS = 16
NVEC = 56


def draw_frame_counts(key, part):
    key = jax.random.fold_in(key, 11)
    key_lengths, key_choice = jax.random.split(key)
    lengths = jax.random.randint(key_lengths, (CLIPS,), SLOT // 4, SLOT + 1)
    chosen = jax.random.randint(key_choice, (CLIPS // MICRO,), 0, MICRO)
    places = jnp.arange(CLIPS) % MICRO
    groups = jnp.arange(CLIPS) // MICRO
    full_slot = places == chosen[groups]
    return jnp.where(full_slot, SLOT, lengths).astype(jnp.int32)


def draw_vectors(key, part):
    key = jax.random.fold_in(key, 23)
    key_bias, key_gain, key_taps = jax.random.split(key, 3)
    ratio_rows = FF // D
    attend_base = 3 + ratio_rows
    conv_base = attend_base + 5
    second_base = conv_base + 4
    final_base = second_base + 3 + ratio_rows
    taps_base = final_base + 2
    row_ids = jnp.arange(NVEC)[:, None]
    biases = 0.3 * jax.random.normal(key_bias, (NVEC, D), jnp.float32)
    gain_values = jax.random.uniform(key_gain, (NVEC, D), jnp.float32, 0.5, 1.5)
    tap_values = jax.random.normal(key_taps, (NVEC, D), jnp.float32) * KERNEL ** (-0.5)
    is_gain = (row_ids == 0) | (row_ids == attend_base) | (row_ids == conv_base) | (row_ids == conv_base + 2) | (row_ids == second_base) | (row_ids == final_base)
    is_tap = row_ids >= taps_base
    return jnp.where(is_gain, gain_values, jnp.where(is_tap, tap_values, biases)).astype(jnp.bfloat16)


def plant(drawn, stream_key, low, high):
    shape = drawn.shape
    index_at = [jax.random.randint(jax.random.fold_in(stream_key, axis), (), 0, shape[axis]) for axis in range(len(shape))]
    drawn = drawn.at[tuple(index_at)].set(low)
    longest = shape.index(max(shape))
    index_at[longest] = (index_at[longest] + 1) % shape[longest]
    return drawn.at[tuple(index_at)].set(high)


def steps_of(own_key, extent, cuts, low, high):
    factor_of, own = 1.0, jax.random.fold_in(own_key, 6)
    for dim, shards_of in cuts:
        draws = jnp.exp(jax.random.uniform(jax.random.fold_in(own, dim), (shards_of,), jnp.float32, low / len(cuts), high / len(cuts)))
        factor_of = factor_of * jnp.repeat(draws, extent[dim] // shards_of).reshape([-1 if axis == dim else 1 for axis in range(len(extent))])
    return factor_of


def scatter_about(own_key, dims, width, bound, cuts=(), kind=jnp.bfloat16):
    values = width * jax.random.normal(own_key, dims, jnp.float32)
    if cuts:
        values = values * steps_of(own_key, dims, cuts, -0.22, 0.18)
    return jnp.clip(values, -bound, bound).astype(kind)


def setup_inputs(seed: int = 0) -> dict:
    arg_keys = jax.random.split(jax.random.key(seed), 16)
    return {
        "frames": scatter_about(arg_keys[0], (CLIPS, SLOT, D), 1.0, 6.0, ((0, 8), (1, 4))),
        "cotangent": scatter_about(arg_keys[1], (CLIPS, SLOT, D), 1.0, 6.0, ((0, 8), (1, 4))),
        "clip_valid": plant((jax.random.randint(arg_keys[2], (CLIPS,), 0, 4) < 3).astype(jnp.int32), jax.random.fold_in(arg_keys[2], 1), 0, 1),
        "frame_counts": draw_frame_counts(jax.random.fold_in(arg_keys[15], 71), 0),
        "rel_rows": jax.random.permutation(arg_keys[4], OFFSETS).astype(jnp.int32),
        "first_up": scatter_about(arg_keys[5], (D, FF), D ** -0.5, 0.1875, ((0, 8), (1, 4))),
        "first_down": scatter_about(arg_keys[6], (FF, D), (FF // 4) ** -0.5, 0.1875, ((0, 4), (1, 8))),
        "attend_in": scatter_about(arg_keys[7], (3, D, D), D ** -0.5, 0.1875, ((1, 8), (2, 4))),
        "attend_out": scatter_about(arg_keys[8], (D, D), (max(D // 64, 2)) ** -0.5, 1.5, ((0, 4), (1, 8))),
        "pointwise_in": scatter_about(arg_keys[9], (2, D, D), D ** -0.5, 0.1875, ((1, 8), (2, 4))),
        "pointwise_out": scatter_about(arg_keys[10], (D, D), (D // 2) ** -0.5, 0.25, ((0, 4), (1, 8))),
        "second_up": scatter_about(arg_keys[11], (D, FF), D ** -0.5, 0.1875, ((0, 8), (1, 4))),
        "second_down": scatter_about(arg_keys[12], (FF, D), (FF // 4) ** -0.5, 0.1875, ((0, 4), (1, 8))),
        "vectors": draw_vectors(jax.random.fold_in(arg_keys[15], 71), 0),
        "distance": scatter_about(arg_keys[14], (OFFSETS, HEAD_DIM), 1.0, 6.0),
    }


@jax.custom_vjp
def low(v):
    return lax.optimization_barrier(v.astype(jnp.bfloat16)).astype(jnp.float32)

@jax.custom_vjp
def low_back(v):
    return v

def low_keep(v):
    return (low(v), None)

def low_pass(kept, grad):
    return (grad,)

def back_keep(v):
    return (v, None)

def back_low(kept, grad):
    return (low(grad),)
low.defvjp(low_keep, low_pass)
low_back.defvjp(back_keep, back_low)
EPSILON = 1e-05

def precise(left_side, right_side):
    return jnp.dot(left_side, right_side, precision=lax.Precision.HIGHEST)

def apply_swish(values):
    return values * jax.nn.sigmoid(values)

def layer_norm(values, gain_row, shift_row):
    centred = values - lax.optimization_barrier(jnp.mean(values, axis=-1, keepdims=True))
    variance = lax.optimization_barrier(jnp.mean(centred * centred, axis=-1, keepdims=True))
    return centred * lax.rsqrt(variance + EPSILON) * gain_row + shift_row

def feed_forward(inputs, up_weight, down_weight, vectors, base_row):
    ratio_rows = FF // D
    normed = low(layer_norm(inputs, vectors[base_row], vectors[base_row + 1]))
    upper_rows = low_back(precise(normed, up_weight) + vectors[base_row + 2:base_row + 2 + ratio_rows].reshape(FF))
    hidden = low(apply_swish(upper_rows))
    return low_back(precise(hidden, down_weight) + vectors[base_row + 2 + ratio_rows])

def split_heads(block_in):
    return block_in.reshape(SLOT, HEADS, HEAD_DIM).transpose(1, 0, 2)

def attention(inputs, mix_weight, back_weight, vectors, base_row, rel_table, live_mask, offsets):
    normed = low(layer_norm(inputs, vectors[base_row], vectors[base_row + 1]))
    queries = split_heads(low_back(low(precise(normed, mix_weight[0]) + vectors[base_row + 2])))
    key_rows = split_heads(low_back(low(precise(normed, mix_weight[1]))))
    value_rows = split_heads(low_back(low(precise(normed, mix_weight[2]) + vectors[base_row + 3])))
    query_table = low_back(low(jnp.einsum('hid,od->hio', queries, rel_table, precision=lax.Precision.HIGHEST)))
    relative = jnp.take_along_axis(query_table, jnp.broadcast_to(offsets, (HEADS, SLOT, SLOT)), axis=2)
    direct = jnp.einsum('hid,hjd->hij', queries, key_rows, precision=lax.Precision.HIGHEST)
    scores = low_back((direct + relative) * HEAD_DIM ** (-0.5))
    masked = jnp.where(live_mask[None, None, :] > 0, scores, -1e+30)
    row_peak = lax.optimization_barrier(jnp.max(masked, axis=-1, keepdims=True))
    exp_rows = jnp.exp(masked - row_peak)
    shares = exp_rows / lax.optimization_barrier(jnp.sum(exp_rows, axis=-1, keepdims=True))
    context = low_back(low(jnp.einsum('hij,hjd->hid', low(shares), value_rows, precision=lax.Precision.HIGHEST)))
    context = context.transpose(1, 0, 2).reshape(SLOT, D)
    return low_back(precise(context, back_weight) + vectors[base_row + 4])

def convolution(inputs, mix_weight, back_weight, vectors, base_row, taps_row, live_mask):
    normed = low(layer_norm(inputs, vectors[base_row], vectors[base_row + 1]))
    linear = low_back(precise(normed, mix_weight[0]))
    gate_rows = low_back(precise(normed, mix_weight[1]))
    gated_rows = linear * jax.nn.sigmoid(gate_rows) * live_mask[:, None]
    padded = jnp.pad(gated_rows, ((KERNEL - 1, 0), (0, 0)))
    depth_out = jnp.zeros_like(gated_rows)
    for offset in range(KERNEL):
        depth_out = depth_out + vectors[taps_row + offset] * padded[offset:offset + SLOT]
    activated = low(apply_swish(layer_norm(depth_out, vectors[base_row + 2], vectors[base_row + 3])))
    return low_back(precise(activated, back_weight))

def clip_layer(params, clip_in, frame_total, rel_rows, offsets):
    first_up, first_down, attend_in, attend_out, pointwise_in, pointwise_out, second_up, second_down, vectors, distance = params
    ratio_rows = FF // D
    attend_base = 3 + ratio_rows
    conv_base = attend_base + 5
    second_base = conv_base + 4
    final_base = second_base + 3 + ratio_rows
    taps_base = final_base + 2
    live_mask = (jnp.arange(SLOT) < frame_total).astype(jnp.float32)
    rel_table = jnp.take(distance, rel_rows, axis=0)
    after_one = clip_in + 0.5 * feed_forward(clip_in, first_up, first_down, vectors, 0)
    after_two = after_one + attention(after_one, attend_in, attend_out, vectors, attend_base, rel_table, live_mask, offsets)
    after_three = after_two + convolution(after_two, pointwise_in, pointwise_out, vectors, conv_base, taps_base, live_mask)
    after_four = after_three + 0.5 * feed_forward(after_three, second_up, second_down, vectors, second_base)
    return layer_norm(after_four, vectors[final_base], vectors[final_base + 1])

def reference(frames, cotangent, clip_valid, frame_counts, rel_rows, first_up, first_down, attend_in, attend_out, pointwise_in, pointwise_out, second_up, second_down, vectors, distance):
    params = tuple((weight.astype(jnp.float32) for weight in (first_up, first_down, attend_in, attend_out, pointwise_in, pointwise_out, second_up, second_down, vectors, distance)))
    positions = jnp.arange(SLOT).astype(jnp.int32)
    offsets = jnp.clip(positions[None, :] - positions[:, None] + LEFT, 0, OFFSETS - 1).astype(jnp.int32)

    def one_clip(totals, inputs):
        clip_in, clip_cot, valid_flag, frame_total = inputs
        clip_wide = clip_in.astype(jnp.float32)

        def forward(weights, rows_in):
            final_rows = clip_layer(weights, rows_in, frame_total, rel_rows, offsets)
            return jnp.where(valid_flag > 0, final_rows, rows_in)
        result, pullback = jax.vjp(forward, params, clip_wide)
        grad_params, grad_rows = pullback(clip_cot.astype(jnp.float32))
        totals = jax.tree.map(jnp.add, totals, grad_params)
        return (totals, (result.astype(jnp.bfloat16), grad_rows.astype(jnp.bfloat16)))
    initial = jax.tree.map(jnp.zeros_like, params)
    totals, (outputs, grads) = lax.scan(one_clip, initial, (frames, cotangent, clip_valid, frame_counts))
    return (outputs, grads, totals[0], totals[1], totals[2], totals[3], totals[4], totals[5], totals[6], totals[7], totals[8], totals[9])
```

```python
import jax
import jax.numpy as jnp
from jax import lax
from jax.experimental import pallas as pl
from jax.experimental.pallas import tpu as pltpu
from jax.sharding import Mesh
from jax.sharding import PartitionSpec as P

HEADS = 16
HEAD_DIM = 64
FF = 4096
KERNEL = 31
LEFT = 64
OFFSETS = 73
EPSILON = 1e-05

LANES = 128
RIGHT = OFFSETS - 1 - LEFT
NT = (((1,), (1,)), ((), ()))
NN = (((1,), (0,)), ((), ()))
TN = (((0,), (0,)), ((), ()))


def dot_f32(left_side, right_side, dims):
    return lax.dot_general(left_side, right_side, dims, preferred_element_type=jnp.float32)


def band_distance():
    shape = (LANES, 3 * LANES)
    return (
        lax.broadcasted_iota(jnp.int32, shape, 1)
        - LANES
        - lax.broadcasted_iota(jnp.int32, shape, 0)
    )


def add_relative(score_ref, source, live_row, distance, block, number, key_blocks):
    rows = slice(number * LANES, (number + 1) * LANES)
    own = source[rows]
    left_col = own[:, 2 * LANES - LEFT : 2 * LANES - LEFT + 1]
    right_col = own[:, RIGHT : RIGHT + 1]
    rolled = pltpu.roll(own, LANES, 1, stride=1, stride_axis=0)
    rolled = jnp.concatenate([rolled, rolled[:, :LANES]], axis=1)
    band = jnp.where(
        distance <= -LEFT, left_col, jnp.where(distance >= RIGHT, right_col, rolled)
    )
    lanes = lax.broadcasted_iota(jnp.int32, (LANES, 3 * LANES), 1)
    band = band - jnp.where(lanes < LANES, left_col, right_col)
    window = pl.ds(pl.multiple_of(block * LANES, LANES), 3 * LANES)
    score_ref[rows, window] += band
    base = jnp.concatenate(
        [
            jnp.broadcast_to(jnp.where(place < block, left_col, right_col), (LANES, LANES))
            for place in range(key_blocks)
        ],
        axis=1,
    )
    return score_ref[rows, LANES : LANES + key_blocks * LANES] + base + live_row


def live_keys(meta_ref, key_count):
    places = lax.broadcasted_iota(jnp.int32, (1, key_count), 1)
    return jnp.where(places < meta_ref[1], 0.0, -1e30).astype(jnp.float32)


def attend_kernel(meta_ref, q_ref, k_ref, v_ref, e_ref, c_ref, lse_ref, score_ref, share_ref):
    row_count, key_count = q_ref.shape[0], k_ref.shape[0]
    pair = pl.program_id(0)
    lanes = lax.broadcasted_iota(jnp.int32, (row_count, LANES), 1)
    live_row = live_keys(meta_ref, key_count)
    distance = band_distance()
    result = None
    for half in range(2):
        mine = (lanes < HEAD_DIM) if half == 0 else (lanes >= HEAD_DIM)
        q_half = jnp.where(mine, q_ref[...], 0)
        score_ref[:, LANES : LANES + key_count] = dot_f32(q_half, k_ref[...], NT)
        source = dot_f32(q_half, e_ref[...], NT).astype(jnp.bfloat16).astype(jnp.float32)
        for number in range(row_count // LANES):
            rows = slice(number * LANES, (number + 1) * LANES)
            scores = add_relative(
                score_ref, source, live_row, distance, meta_ref[0] + number, number,
                key_count // LANES,
            )
            peak = jnp.max(scores, axis=1, keepdims=True)
            grown = jnp.exp(scores - peak)
            total = jnp.sum(grown, axis=1, keepdims=True)
            share_ref[rows] = (grown * (1.0 / total)).astype(jnp.bfloat16)
            lse_ref[rows] = jnp.where(
                lanes[rows] == 2 * pair + half, peak + jnp.log(total), lse_ref[rows]
            )
        context = dot_f32(share_ref[...], v_ref[...], NN)
        result = context if half == 0 else jnp.where(mine, context, result)
    c_ref[...] = result.astype(jnp.bfloat16)


def attend_back_kernel(
    meta_ref, q_ref, k_ref, v_ref, e_ref, dc_ref, c_ref, lse_ref,
    dq_ref, dk_ref, dv_ref, de_ref,
    score_ref, grad_ref, share_ref, slope_ref, source_ref, wide_ref,
):
    row_count, key_count = q_ref.shape[0], k_ref.shape[0]
    key_blocks = key_count // LANES
    pair = pl.program_id(0)
    lanes = lax.broadcasted_iota(jnp.int32, (row_count, LANES), 1)
    live_row = live_keys(meta_ref, key_count)
    distance = band_distance()
    inside = (distance > -LEFT) & (distance < RIGHT)
    square = (LANES, LANES)
    flip = (
        lax.broadcasted_iota(jnp.int32, square, 0) + lax.broadcasted_iota(jnp.int32, square, 1)
        == LANES - 1
    ).astype(jnp.float32).astype(jnp.bfloat16)
    spots = lax.broadcasted_iota(jnp.int32, (LANES, 2 * LANES), 1)

    @pl.when(pair == 0)
    def _():
        shape = (key_count, LANES)
        before = lax.broadcasted_iota(jnp.int32, shape, 0) < LANES * lax.broadcasted_iota(
            jnp.int32, shape, 1
        )
        wide_ref[:, LANES:] = before.astype(jnp.float32).astype(jnp.bfloat16)
        slope_ref[:, :LANES] = jnp.zeros((row_count, LANES), jnp.bfloat16)
        slope_ref[:, LANES + key_count :] = jnp.zeros((row_count, LANES), jnp.bfloat16)
        de_ref[...] = jnp.zeros(de_ref.shape, jnp.float32)

    wide_ref[:, :LANES] = k_ref[...]
    inner_all = dc_ref[...].astype(jnp.float32) * c_ref[...].astype(jnp.float32)
    grad_q = grad_k = grad_v = None
    for half in range(2):
        mine = (lanes < HEAD_DIM) if half == 0 else (lanes >= HEAD_DIM)
        q_half = jnp.where(mine, q_ref[...], 0)
        dc_half = jnp.where(mine, dc_ref[...], 0)
        score_ref[:, LANES : LANES + key_count] = dot_f32(q_half, k_ref[...], NT)
        grad_ref[...] = dot_f32(dc_half, v_ref[...], NT)
        source = dot_f32(q_half, e_ref[...], NT).astype(jnp.bfloat16).astype(jnp.float32)
        inner = jnp.sum(jnp.where(mine, inner_all, 0.0), axis=1, keepdims=True)
        level = jnp.sum(
            jnp.where(lanes == 2 * pair + half, lse_ref[...], 0.0), axis=1, keepdims=True
        )
        for number in range(row_count // LANES):
            rows = slice(number * LANES, (number + 1) * LANES)
            scores = add_relative(
                score_ref, source, live_row, distance, meta_ref[0] + number, number, key_blocks
            )
            shares = jnp.exp(scores - level[rows])
            share_ref[rows] = shares.astype(jnp.bfloat16)
            slope_ref[rows, LANES : LANES + key_count] = (
                shares * (grad_ref[rows] - inner[rows])
            ).astype(jnp.bfloat16)
        slopes = slope_ref[:, LANES : LANES + key_count]
        wide = dot_f32(slopes, wide_ref[...], NN)
        before = wide[:, LANES:]
        for number in range(row_count // LANES):
            rows = slice(number * LANES, (number + 1) * LANES)
            block = meta_ref[0] + number
            window = pl.ds(pl.multiple_of(block * LANES, LANES), 3 * LANES)
            seen = slope_ref[rows, window].astype(jnp.float32)
            sums, spot = before[rows], lanes[rows]
            far_left = jnp.sum(
                jnp.where(spot == jnp.maximum(block - 1, 0), sums, 0.0), axis=1, keepdims=True
            ) + jnp.sum(jnp.where(distance <= -LEFT, seen, 0.0), axis=1, keepdims=True)
            far_right = jnp.sum(
                jnp.where(spot == key_blocks, sums, 0.0)
                - jnp.where(spot == jnp.minimum(block + 2, key_blocks), sums, 0.0),
                axis=1,
                keepdims=True,
            ) + jnp.sum(jnp.where(distance >= RIGHT, seen, 0.0), axis=1, keepdims=True)
            band = jnp.where(inside, seen, 0.0)
            band = jnp.concatenate(
                [band[:, :LANES] + band[:, 2 * LANES :], band[:, LANES : 2 * LANES]], axis=1
            )
            turned = dot_f32(flip, band.astype(jnp.bfloat16), NN)
            turned = pltpu.roll(turned, 1, 1, stride=1, stride_axis=0)
            turned = dot_f32(flip, turned.astype(jnp.bfloat16), NN)
            turned = jnp.where(
                spots == 2 * LANES - LEFT, far_left, jnp.where(spots == RIGHT, far_right, turned)
            )
            source_ref[rows] = turned.astype(jnp.bfloat16)
        q_part = wide[:, :LANES] + dot_f32(source_ref[...], e_ref[...], NN)
        k_part = dot_f32(q_half, slopes, TN)
        v_part = dot_f32(dc_half, share_ref[...], TN)
        de_ref[...] += dot_f32(q_half, source_ref[...], TN)
        grad_q = q_part if half == 0 else jnp.where(mine, q_part, grad_q)
        grad_k = k_part if half == 0 else grad_k + k_part
        grad_v = v_part if half == 0 else grad_v + v_part
    dq_ref[...] = (grad_q * HEAD_DIM ** (-0.5)).astype(jnp.bfloat16)
    dk_ref[...] = grad_k.T.astype(jnp.bfloat16)
    dv_ref[...] = grad_v.T.astype(jnp.bfloat16)


def pair_spec(row_count):
    return pl.BlockSpec((row_count, LANES), lambda pair, meta: (0, pair))


def fixed_spec(row_count, column_count):
    return pl.BlockSpec((row_count, column_count), lambda pair, meta: (0, 0))


def attend(meta, queries, key_rows, value_rows, table):
    row_count, width = queries.shape
    key_count = key_rows.shape[0]
    return pl.pallas_call(
        attend_kernel,
        grid_spec=pltpu.PrefetchScalarGridSpec(
            num_scalar_prefetch=1,
            grid=(width // LANES,),
            in_specs=[
                pair_spec(row_count),
                pair_spec(key_count),
                pair_spec(key_count),
                fixed_spec(2 * LANES, LANES),
            ],
            out_specs=[pair_spec(row_count), fixed_spec(row_count, LANES)],
            scratch_shapes=[
                pltpu.VMEM((row_count, key_count + 2 * LANES), jnp.float32),
                pltpu.VMEM((row_count, key_count), jnp.bfloat16),
            ],
        ),
        out_shape=[
            jax.ShapeDtypeStruct((row_count, width), jnp.bfloat16),
            jax.ShapeDtypeStruct((row_count, LANES), jnp.float32),
        ],
        compiler_params=pltpu.CompilerParams(vmem_limit_bytes=48 * 2**20),
        name="attend",
    )(meta, queries, key_rows, value_rows, table)


def attend_back(meta, queries, key_rows, value_rows, table, grad_context, context, levels):
    row_count, width = queries.shape
    key_count = key_rows.shape[0]
    return pl.pallas_call(
        attend_back_kernel,
        grid_spec=pltpu.PrefetchScalarGridSpec(
            num_scalar_prefetch=1,
            grid=(width // LANES,),
            in_specs=[
                pair_spec(row_count),
                pair_spec(key_count),
                pair_spec(key_count),
                fixed_spec(2 * LANES, LANES),
                pair_spec(row_count),
                pair_spec(row_count),
                fixed_spec(row_count, LANES),
            ],
            out_specs=[
                pair_spec(row_count),
                pair_spec(key_count),
                pair_spec(key_count),
                fixed_spec(LANES, 2 * LANES),
            ],
            scratch_shapes=[
                pltpu.VMEM((row_count, key_count + 2 * LANES), jnp.float32),
                pltpu.VMEM((row_count, key_count), jnp.float32),
                pltpu.VMEM((row_count, key_count), jnp.bfloat16),
                pltpu.VMEM((row_count, key_count + 2 * LANES), jnp.bfloat16),
                pltpu.VMEM((row_count, 2 * LANES), jnp.bfloat16),
                pltpu.VMEM((key_count, 2 * LANES), jnp.bfloat16),
            ],
        ),
        out_shape=[
            jax.ShapeDtypeStruct((row_count, width), jnp.bfloat16),
            jax.ShapeDtypeStruct((key_count, width), jnp.bfloat16),
            jax.ShapeDtypeStruct((key_count, width), jnp.bfloat16),
            jax.ShapeDtypeStruct((LANES, 2 * LANES), jnp.float32),
        ],
        compiler_params=pltpu.CompilerParams(vmem_limit_bytes=48 * 2**20),
        name="attend_back",
    )(meta, queries, key_rows, value_rows, table, grad_context, context, levels)


def wide_table(table_low):
    places = jnp.arange(2 * LANES)
    offsets = jnp.clip(jnp.where(places < LANES, places, places - 2 * LANES) + LEFT, 0, OFFSETS - 1)
    rows = table_low[offsets]
    return jnp.concatenate([rows, rows], axis=1)


def table_grad(wide_grad):
    folded = (wide_grad[:HEAD_DIM] + wide_grad[HEAD_DIM:]).T
    return jnp.concatenate([folded[2 * LANES - LEFT :], folded[: RIGHT + 1]], axis=0)


def apply_swish(values):
    return values * jax.nn.sigmoid(values)


def swish_slope(values):
    logistic = jax.nn.sigmoid(values)
    return logistic + values * logistic * (1.0 - logistic)


def matmul(left_side, right_side):
    return dot_f32(left_side, right_side, NN)


def norm_rows(values, gain_row, shift_row):
    centred = values - jnp.mean(values, axis=-1, keepdims=True)
    variance = jnp.mean(centred * centred, axis=-1, keepdims=True)
    inverse = lax.rsqrt(variance + EPSILON)
    normal = centred * inverse
    return (normal * gain_row + shift_row, normal, inverse)


def norm_back(grad_out, normal, inverse, gain_row):
    grad_normal = grad_out * gain_row
    grad_in = inverse * (
        grad_normal
        - jnp.mean(grad_normal, axis=-1, keepdims=True)
        - normal * jnp.mean(grad_normal * normal, axis=-1, keepdims=True)
    )
    return (grad_in, jnp.sum(grad_out * normal, axis=0), jnp.sum(grad_out, axis=0))


TENSOR = ("far", "z")


class Place:
    def __init__(self):
        self.count = {axis: lax.axis_size(axis) for axis in ("y", "x", "core", "far", "z")}
        self.index = {axis: lax.axis_index(axis) for axis in ("y", "x", "core", "far", "z")}
        self.count["t"] = self.count["far"] * self.count["z"]
        self.index["t"] = self.index["far"] * self.count["z"] + self.index["z"]
        self.count["seq"] = self.count["far"] * 2
        self.index["seq"] = self.index["far"] * 2 + self.index["core"]
        self.names = {"t": TENSOR, "seq": ("core", "far")}

    def seq_pair(self, start, end):
        far = self.count["far"]
        return ((start % 2) * far + start // 2, (end % 2) * far + end // 2)

    def turn(self, block, axis, step):
        size = self.count[axis]
        pairs = [(start, (start + step) % size) for start in range(size)]
        if axis == "seq":
            pairs = [self.seq_pair(*pair) for pair in pairs]
        return lax.ppermute(block, self.names.get(axis, axis), pairs)

    def after(self, axis, step):
        return lax.rem(self.index[axis] + step, self.count[axis])


def steps(place, axis):
    return range(1, place.count[axis])


def halves_of(shard, by_rows):
    row_dim = 1 if by_rows else 0
    half = shard.shape[row_dim] // 2
    return [lax.slice_in_dim(shard, number * half, (number + 1) * half, axis=row_dim) for number in range(2)]


def gather_half(place, block, order):
    stack = jnp.stack([block] + [place.turn(block, "t", step) for step in steps(place, "t")])
    pieces = {(0, 0, 0): stack}
    for axis in order:
        where = ("y", "x", "core").index(axis)
        for key, piece in list(pieces.items()):
            for step in steps(place, axis):
                new_key = key[:where] + (step,) + key[where + 1 :]
                pieces[new_key] = place.turn(piece, axis, step)
    return pieces


ORDERS = (("x", "y", "core"), ("y", "x", "core"))


def assemble(place, halves, by_rows):
    keys = [(number, key) for number, pieces in enumerate(halves) for key in pieces]
    arrays = [halves[number][key] for number, key in keys]
    counts = place.count
    tensor_count = counts["t"]
    dp_count = counts["y"] * counts["x"] * counts["core"]
    dtype = arrays[0].dtype
    if by_rows:
        _, depth, half_rows, columns = arrays[0].shape
        shard_rows = half_rows * len(halves)
        out_shape = (depth, shard_rows * dp_count, columns * tensor_count)
    else:
        _, half_rows, columns = arrays[0].shape
        shard_rows = half_rows * len(halves)
        aligned = columns % LANES == 0
        if aligned:
            out_shape = (shard_rows * tensor_count, columns * dp_count)
        else:
            out_shape = (dp_count, shard_rows * tensor_count, columns)

    def kernel(meta_ref, *refs):
        piece_refs, out_ref, sem = refs[: len(keys)], refs[len(keys)], refs[len(keys) + 1]
        copies = []
        for (number, key), piece_ref in zip(keys, piece_refs):
            spot = [
                lax.rem(meta_ref[i] - key[i] + counts[axis], counts[axis])
                for i, axis in enumerate(("y", "x", "core"))
            ]
            dp_spot = (spot[0] * counts["x"] + spot[1]) * counts["core"] + spot[2]
            for step in range(tensor_count):
                t_spot = lax.rem(meta_ref[3] - step + tensor_count, tensor_count)
                if by_rows:
                    rows = pl.ds(
                        pl.multiple_of(dp_spot * shard_rows + number * half_rows, half_rows), half_rows
                    )
                    target = out_ref.at[:, rows, pl.ds(pl.multiple_of(t_spot * columns, columns), columns)]
                else:
                    rows = pl.ds(
                        pl.multiple_of(t_spot * shard_rows + number * half_rows, half_rows), half_rows
                    )
                    if aligned:
                        target = out_ref.at[rows, pl.ds(pl.multiple_of(dp_spot * columns, columns), columns)]
                    else:
                        target = out_ref.at[dp_spot, rows, :]
                copy = pltpu.make_async_copy(piece_ref.at[step], target, sem.at[len(copies)])
                copy.start()
                copies.append(copy)
        for copy in copies:
            copy.wait()

    meta = jnp.stack([place.index[axis] for axis in ("y", "x", "core", "t")]).astype(jnp.int32)
    whole = pl.pallas_call(
        kernel,
        grid_spec=pltpu.PrefetchScalarGridSpec(
            num_scalar_prefetch=1,
            grid=(),
            in_specs=[pl.BlockSpec(memory_space=pl.ANY)] * len(keys),
            out_specs=pl.BlockSpec(memory_space=pltpu.VMEM),
            scratch_shapes=[pltpu.SemaphoreType.DMA((len(keys) * tensor_count,))],
        ),
        out_shape=jax.ShapeDtypeStruct(out_shape, dtype),
        compiler_params=pltpu.CompilerParams(vmem_limit_bytes=20 * 2**20),
        name="assemble",
    )(meta, *arrays)
    if not by_rows and not aligned:
        whole = whole.transpose(1, 0, 2).reshape(shard_rows * tensor_count, columns * dp_count)
    return whole


def fetch(place, shard, by_rows):
    halves = [
        gather_half(place, half, order) for half, order in zip(halves_of(shard, by_rows), ORDERS)
    ]
    return assemble(place, halves, by_rows)


class Part:
    def __init__(self, array, by_rows, spans):
        self.array, self.by_rows, self.spans = array, by_rows, spans

    def pick(self, axis, index):
        spans = dict(self.spans)
        count = spans[axis]
        if count == 1:
            return self
        spans[axis] = 1
        array = self.array
        if self.by_rows:
            if axis == "t":
                width = array.shape[-1] // count
                array = lax.dynamic_slice_in_dim(array, index * width, width, axis=4)
            else:
                array = lax.dynamic_slice_in_dim(array, index, 1, axis={"y": 1, "x": 2}[axis])
        elif axis == "t":
            array = lax.dynamic_slice_in_dim(array, index, 1, axis=0)
        else:
            width = array.shape[-1] // (self.spans["y"] * self.spans["x"])
            if axis == "y":
                width = width * self.spans["x"]
                array = lax.dynamic_slice_in_dim(array, index * width, width, axis=2)
            else:
                array = jnp.concatenate(
                    [
                        lax.dynamic_slice_in_dim(array, (row * count + index) * width, width, axis=2)
                        for row in range(self.spans["y"])
                    ],
                    axis=2,
                )
        return Part(array, self.by_rows, spans)


def added(parts):
    total = parts[0].array.astype(jnp.float32)
    for part in parts[1:]:
        total = total + part.array.astype(jnp.float32)
    return total


def reduce_half(place, parts, order):
    for axis in order:
        arrived = []
        for step in steps(place, axis):
            picked = [part.pick(axis, place.after(axis, step)) for part in parts]
            message = place.turn(added(picked).astype(jnp.bfloat16), axis, step)
            arrived.append(Part(message, picked[0].by_rows, picked[0].spans))
        parts = [part.pick(axis, place.index[axis]) for part in parts] + arrived
    return added(parts)


BACK_ORDERS = (("y", "x", "t"), ("x", "y", "t"))


def reduce_weight(place, product, by_rows, depth):
    counts = place.count
    spans = {"y": counts["y"], "x": counts["x"], "t": counts["t"]}
    other = place.turn(product(1 - place.index["core"]), "core", 1)
    mine = product(place.index["core"])
    results = []
    for number, order in enumerate(BACK_ORDERS):
        parts = []
        for array in (mine, other):
            if by_rows:
                block = array.reshape(
                    depth, counts["y"], counts["x"], 2, -1, array.shape[-1]
                )[:, :, :, number]
            else:
                block = array.reshape(counts["t"], 2, -1, array.shape[-1])[:, number]
            parts.append(Part(block, by_rows, spans))
        results.append(reduce_half(place, parts, order))
    if by_rows:
        return jnp.concatenate([one[:, 0, 0] for one in results], axis=1)
    return jnp.concatenate([one[0] for one in results], axis=0)


def core_columns(place, rows_in, core):
    blocks = place.count["y"] * place.count["x"]
    width = rows_in.shape[-1] // (2 * blocks)
    return jnp.concatenate(
        [
            lax.dynamic_slice_in_dim(rows_in, (2 * block + core) * width, width, axis=-1)
            for block in range(blocks)
        ],
        axis=-1,
    )


def grad_by_rows(place, inputs, grads):
    def product(core):
        left_side = core_columns(place, inputs, core)
        return jnp.stack([dot_f32(left_side, grad, TN).astype(jnp.bfloat16) for grad in grads])

    return reduce_weight(place, product, True, len(grads))


def grad_by_columns(place, inputs, grad):
    def product(core):
        return dot_f32(inputs, core_columns(place, grad, core), TN).astype(jnp.bfloat16)

    return reduce_weight(place, product, False, 1)


def to_clip(place, blocks):
    micro, z_count = blocks.shape[0], place.count["z"]
    z_here = place.index["z"]
    arrived = []
    for step in range(micro):
        block = lax.dynamic_index_in_dim(blocks, lax.rem(z_here + step, micro), 0, keepdims=False)
        arrived.append(lax.ppermute(block, ("core", "z"), clip_pairs(micro, z_count, step)))
    stack = jnp.stack(arrived)
    ordered = [
        lax.dynamic_index_in_dim(stack, lax.rem(z_here - spot + micro, micro), 0, keepdims=False)
        for spot in range(micro)
    ]
    return jnp.concatenate(ordered, axis=0)


def clip_pairs(micro, z_count, step):
    return [
        (core * z_count + z, (z // micro) * z_count + micro * core + (step + z) % micro)
        for core in range(2)
        for z in range(z_count)
    ]


def from_clip(place, rows_in, micro):
    z_count, z_here = place.count["z"], place.index["z"]
    blocks = rows_in.reshape(micro, -1, rows_in.shape[-1])
    arrived = []
    for step in range(micro):
        spot = lax.rem(z_here - step + micro, micro)
        block = lax.dynamic_index_in_dim(blocks, spot, 0, keepdims=False)
        pairs = [(end, start) for start, end in clip_pairs(micro, z_count, step)]
        arrived.append(lax.ppermute(block, ("core", "z"), pairs))
    stack = jnp.stack(arrived)
    return jnp.stack(
        [
            lax.dynamic_index_in_dim(stack, lax.rem(number - z_here % micro + micro, micro), 0, keepdims=False)
            for number in range(micro)
        ]
    )


def all_rows(place, own):
    count = place.count["seq"]
    whole = jnp.zeros((count,) + own.shape, own.dtype)
    for step in range(count):
        block = own if step == 0 else place.turn(own, "seq", step)
        spot = lax.rem(place.index["seq"] - step + count, count)
        whole = lax.dynamic_update_index_in_dim(whole, block, spot, 0)
    return whole.reshape((count * own.shape[0],) + own.shape[1:])


def own_sum(place, partial):
    count = place.count["seq"]
    blocks = partial.reshape(count, -1, partial.shape[-1])
    total = lax.dynamic_index_in_dim(blocks, place.index["seq"], 0, keepdims=False).astype(jnp.float32)
    for step in range(1, count):
        message = lax.dynamic_index_in_dim(blocks, place.after("seq", step), 0, keepdims=False)
        total = total + place.turn(message, "seq", step).astype(jnp.float32)
    return total


def neighbour_rows(place, rows_in, step):
    count = place.count["seq"]
    pairs = [
        place.seq_pair(start, start + step) for start in range(count) if 0 <= start + step < count
    ]
    return lax.ppermute(rows_in, place.names["seq"], pairs)


def feed_forward(inputs, up_weight, down_weight, up_bias, down_bias, gain_row, shift_row):
    normed, normal, inverse = norm_rows(inputs, gain_row, shift_row)
    normed = normed.astype(jnp.bfloat16)
    upper_rows = matmul(normed, up_weight) + up_bias
    hidden = apply_swish(upper_rows).astype(jnp.bfloat16)
    result = matmul(hidden, down_weight) + down_bias
    return (result, (normal, inverse, normed, upper_rows.astype(jnp.bfloat16), hidden))


def feed_back(place, grad_result, stored, up_weight, down_weight, gain_row):
    normal, inverse, normed, upper_rows, hidden = stored
    grad_low = grad_result.astype(jnp.bfloat16)
    grad_down = grad_by_columns(place, hidden, grad_low)
    grad_hidden = dot_f32(grad_low, down_weight, NT)
    grad_upper = (grad_hidden * swish_slope(upper_rows.astype(jnp.float32))).astype(jnp.bfloat16)
    grad_up = grad_by_rows(place, normed, [grad_upper])[0]
    grad_normed = dot_f32(grad_upper, up_weight, NT)
    grad_in, grad_gain, grad_shift = norm_back(grad_normed, normal, inverse, gain_row)
    up_bias_grad = jnp.sum(grad_upper.astype(jnp.float32), axis=0)
    down_bias_grad = jnp.sum(grad_low.astype(jnp.float32), axis=0)
    return (grad_in, (grad_up, grad_down), (grad_gain, grad_shift, up_bias_grad, down_bias_grad))


def body(
    frames,
    cotangent,
    clip_valid,
    frame_counts,
    rel_rows,
    first_up,
    first_down,
    attend_in,
    attend_out,
    pointwise_in,
    pointwise_out,
    second_up,
    second_down,
    vectors,
    distance,
):
    place = Place()
    micro, _, width = frames.shape
    ratio_rows = FF // width
    attend_base = 3 + ratio_rows
    conv_base = attend_base + 5
    second_base = conv_base + 4
    final_base = second_base + 3 + ratio_rows
    taps_base = final_base + 2
    scale = HEAD_DIM ** (-0.5)

    rows_low = to_clip(place, frames)
    vector_wide = lax.all_gather(vectors, ("y", "x", "core"), axis=1, tiled=True).astype(jnp.float32)
    up_one = fetch(place, first_up[None], True)[0]
    down_one = fetch(place, first_down, False)
    attend_mix = fetch(place, attend_in, True)
    attend_back_weight = fetch(place, attend_out, False)
    point_mix = fetch(place, pointwise_in, True)
    point_back = fetch(place, pointwise_out, False)
    up_two = fetch(place, second_up[None], True)[0]
    down_two = fetch(place, second_down, False)
    cot_low = to_clip(place, cotangent)

    row_count = rows_low.shape[0]
    slot_len = row_count * place.count["seq"]
    z_here = place.index["z"]
    own_facts = jnp.stack([clip_valid, frame_counts])
    other_facts = place.turn(own_facts, "core", 1)
    facts = jnp.where(z_here // micro == place.index["core"], own_facts, other_facts)
    facts = lax.dynamic_index_in_dim(facts, lax.rem(z_here, micro), 1, keepdims=False)
    valid_flag = (facts[0] > 0).astype(jnp.float32)
    first_row = place.index["seq"] * row_count
    live = ((first_row + jnp.arange(row_count)) < facts[1]).astype(jnp.float32)[:, None]
    meta = jnp.stack([place.index["seq"] * (row_count // LANES), facts[1]]).astype(jnp.int32)
    pick_rows = (rel_rows[:, None] == jnp.arange(OFFSETS)[None, :]).astype(jnp.bfloat16)
    table = wide_table(matmul(pick_rows, distance).astype(jnp.bfloat16))

    rows_in = rows_low.astype(jnp.float32)
    rows_cot = cot_low.astype(jnp.float32)
    one_out, one_kept = feed_forward(
        rows_in,
        up_one,
        down_one,
        vector_wide[2 : 2 + ratio_rows].reshape(FF),
        vector_wide[2 + ratio_rows],
        vector_wide[0],
        vector_wide[1],
    )
    after_one = rows_in + 0.5 * one_out

    attend_normed, attend_normal, attend_inverse = norm_rows(
        after_one, vector_wide[attend_base], vector_wide[attend_base + 1]
    )
    attend_normed = attend_normed.astype(jnp.bfloat16)
    queries = (matmul(attend_normed, attend_mix[0]) + vector_wide[attend_base + 2]).astype(jnp.bfloat16)
    queries = (queries.astype(jnp.float32) * scale).astype(jnp.bfloat16)
    own_keys = matmul(attend_normed, attend_mix[1]).astype(jnp.bfloat16)
    own_values = (matmul(attend_normed, attend_mix[2]) + vector_wide[attend_base + 3]).astype(jnp.bfloat16)
    key_rows, value_rows = all_rows(place, own_keys), all_rows(place, own_values)
    context, levels = attend(meta, queries, key_rows, value_rows, table)
    after_two = after_one + matmul(context, attend_back_weight) + vector_wide[attend_base + 4]

    conv_normed, conv_normal, conv_inverse = norm_rows(
        after_two, vector_wide[conv_base], vector_wide[conv_base + 1]
    )
    conv_normed = conv_normed.astype(jnp.bfloat16)
    linear = matmul(conv_normed, point_mix[0])
    logistic = jax.nn.sigmoid(matmul(conv_normed, point_mix[1]))
    gated = linear * logistic * live
    taps = vector_wide[taps_base : taps_base + KERNEL]
    reach = KERNEL - 1
    padded = jnp.concatenate([neighbour_rows(place, gated[-reach:], 1), gated], axis=0)
    depth_out = jnp.zeros_like(gated)
    for offset in range(KERNEL):
        depth_out = depth_out + taps[offset] * padded[offset : offset + row_count]
    deep_gain = vector_wide[conv_base + 2]
    deep_norm, deep_normal, deep_inverse = norm_rows(depth_out, deep_gain, vector_wide[conv_base + 3])
    activated = apply_swish(deep_norm).astype(jnp.bfloat16)
    after_three = after_two + matmul(activated, point_back)

    two_out, two_kept = feed_forward(
        after_three,
        up_two,
        down_two,
        vector_wide[second_base + 2 : second_base + 2 + ratio_rows].reshape(FF),
        vector_wide[second_base + 2 + ratio_rows],
        vector_wide[second_base],
        vector_wide[second_base + 1],
    )
    after_four = after_three + 0.5 * two_out
    final_rows, final_normal, final_inverse = norm_rows(
        after_four, vector_wide[final_base], vector_wide[final_base + 1]
    )
    frames_out = from_clip(
        place, jnp.where(valid_flag > 0, final_rows, rows_in).astype(jnp.bfloat16), micro
    )

    grad_four, final_gain_grad, final_shift_grad = norm_back(
        rows_cot * valid_flag, final_normal, final_inverse, vector_wide[final_base]
    )
    grad_two_in, two_weights, two_parts = feed_back(
        place, 0.5 * grad_four, two_kept, up_two, down_two, vector_wide[second_base]
    )
    grad_three = grad_four + grad_two_in

    conv_low = grad_three.astype(jnp.bfloat16)
    grad_point_back = grad_by_columns(place, activated, conv_low)
    grad_deep = dot_f32(conv_low, point_back, NT) * swish_slope(deep_norm)
    grad_depth, deep_gain_grad, deep_shift_grad = norm_back(
        grad_deep, deep_normal, deep_inverse, deep_gain
    )
    extended = jnp.concatenate([grad_depth, neighbour_rows(place, grad_depth[:reach], -1)], axis=0)
    grad_gated = jnp.zeros_like(grad_depth)
    tap_grads = []
    for offset in range(KERNEL):
        tap_grads.append(jnp.sum(padded[offset : offset + row_count] * grad_depth, axis=0))
        grad_gated = grad_gated + taps[offset] * extended[reach - offset : reach - offset + row_count]
    grad_gated = grad_gated * live
    grad_linear = (grad_gated * logistic).astype(jnp.bfloat16)
    grad_gate = (grad_gated * linear * logistic * (1.0 - logistic)).astype(jnp.bfloat16)
    grad_point_mix = grad_by_rows(place, conv_normed, [grad_linear, grad_gate])
    grad_conv_normed = dot_f32(grad_linear, point_mix[0], NT) + dot_f32(grad_gate, point_mix[1], NT)
    grad_conv_in, conv_gain_grad, conv_shift_grad = norm_back(
        grad_conv_normed, conv_normal, conv_inverse, vector_wide[conv_base]
    )
    grad_two = grad_three + grad_conv_in

    attend_low = grad_two.astype(jnp.bfloat16)
    grad_attend_back = grad_by_columns(place, context, attend_low)
    grad_context = dot_f32(attend_low, attend_back_weight, NT).astype(jnp.bfloat16)
    grad_queries, part_keys, part_values, grad_table = attend_back(
        meta, queries, key_rows, value_rows, table, grad_context, context, levels
    )
    grad_keys = own_sum(place, part_keys).astype(jnp.bfloat16)
    grad_values = own_sum(place, part_values).astype(jnp.bfloat16)
    grad_attend_mix = grad_by_rows(place, attend_normed, [grad_queries, grad_keys, grad_values])
    grad_attend_normed = (
        dot_f32(grad_queries, attend_mix[0], NT)
        + dot_f32(grad_keys, attend_mix[1], NT)
        + dot_f32(grad_values, attend_mix[2], NT)
    )
    grad_attend_in, attend_gain_grad, attend_shift_grad = norm_back(
        grad_attend_normed, attend_normal, attend_inverse, vector_wide[attend_base]
    )
    grad_one = grad_two + grad_attend_in

    grad_one_in, one_weights, one_parts = feed_back(
        place, 0.5 * grad_one, one_kept, up_one, down_one, vector_wide[0]
    )
    grad_rows = grad_one + grad_one_in + (1.0 - valid_flag) * rows_cot
    frames_grad = from_clip(place, grad_rows.astype(jnp.bfloat16), micro)

    def column_sum(rows):
        return jnp.sum(rows.astype(jnp.float32), axis=0)

    vector_part = jnp.concatenate(
        [
            jnp.stack([one_parts[0], one_parts[1]]),
            one_parts[2].reshape(ratio_rows, width),
            jnp.stack(
                [
                    one_parts[3],
                    attend_gain_grad,
                    attend_shift_grad,
                    column_sum(grad_queries),
                    column_sum(grad_values),
                    column_sum(attend_low),
                    conv_gain_grad,
                    conv_shift_grad,
                    deep_gain_grad,
                    deep_shift_grad,
                    two_parts[0],
                    two_parts[1],
                ]
            ),
            two_parts[2].reshape(ratio_rows, width),
            jnp.stack([two_parts[3], final_gain_grad, final_shift_grad]),
            jnp.stack(tap_grads),
        ],
        axis=0,
    )
    everywhere = ("y", "x", "core", "far", "z")
    grad_vectors = lax.psum_scatter(vector_part, everywhere, scatter_dimension=1, tiled=True)
    local_distance = jnp.dot(
        pick_rows.astype(jnp.float32).T, table_grad(grad_table), precision=lax.Precision.HIGHEST
    )
    grad_distance = lax.psum(local_distance, everywhere)
    return (
        frames_out,
        frames_grad,
        one_weights[0],
        one_weights[1],
        grad_attend_mix,
        grad_attend_back,
        grad_point_mix,
        grad_point_back,
        two_weights[0],
        two_weights[1],
        grad_vectors,
        grad_distance,
    )


def solution(mesh):
    dp_count, tensor_count = mesh.shape["dp"], mesh.shape["tensor"]

    def program(*arrays):
        group = 2 * (arrays[0].shape[0] // dp_count)
        parted = Mesh(
            mesh.devices.reshape(dp_count // 4, 2, 2, tensor_count // group, group),
            ("y", "x", "core", "far", "z"),
        )
        dp, tensor = ("y", "x", "core"), TENSOR
        return jax.shard_map(
            body,
            mesh=parted,
            in_specs=(
                P(dp, tensor, None),
                P(dp, tensor, None),
                P(dp),
                P(dp),
                P(),
                P(dp, tensor),
                P(tensor, dp),
                P(None, dp, tensor),
                P(tensor, dp),
                P(None, dp, tensor),
                P(tensor, dp),
                P(dp, tensor),
                P(tensor, dp),
                P(None, dp),
                P(),
            ),
            out_specs=(
                P(dp, tensor, None),
                P(dp, tensor, None),
                P(dp, tensor),
                P(tensor, dp),
                P(None, dp, tensor),
                P(tensor, dp),
                P(None, dp, tensor),
                P(tensor, dp),
                P(dp, tensor),
                P(tensor, dp),
                P(None, dp + tensor),
                P(),
            ),
            check_vma=False,
        )(*arrays)

    return program
```

```python
import jax
import jax.numpy as jnp
from jax import lax
from jax.experimental import pallas as pl
from jax.experimental.pallas import tpu as pltpu
from jax.sharding import Mesh
from jax.sharding import PartitionSpec as P

HEADS = 16
HEAD_DIM = 64
FF = 4096
KERNEL = 31
LEFT = 64
OFFSETS = 73
EPSILON = 1e-05

LANES = 128
RIGHT = OFFSETS - 1 - LEFT
NT = (((1,), (1,)), ((), ()))
NN = (((1,), (0,)), ((), ()))
TN = (((0,), (0,)), ((), ()))


def dot_f32(left_side, right_side, dims):
    return lax.dot_general(left_side, right_side, dims, preferred_element_type=jnp.float32)


def band_distance():
    shape = (LANES, 3 * LANES)
    return (
        lax.broadcasted_iota(jnp.int32, shape, 1)
        - LANES
        - lax.broadcasted_iota(jnp.int32, shape, 0)
    )


def add_relative(score_ref, source, live_row, distance, block, number, key_blocks):
    rows = slice(number * LANES, (number + 1) * LANES)
    own = source[rows]
    left_col = own[:, 2 * LANES - LEFT : 2 * LANES - LEFT + 1]
    right_col = own[:, RIGHT : RIGHT + 1]
    rolled = pltpu.roll(own, LANES, 1, stride=1, stride_axis=0)
    rolled = jnp.concatenate([rolled, rolled[:, :LANES]], axis=1)
    band = jnp.where(
        distance <= -LEFT, left_col, jnp.where(distance >= RIGHT, right_col, rolled)
    )
    lanes = lax.broadcasted_iota(jnp.int32, (LANES, 3 * LANES), 1)
    band = band - jnp.where(lanes < LANES, left_col, right_col)
    window = pl.ds(pl.multiple_of(block * LANES, LANES), 3 * LANES)
    score_ref[rows, window] += band
    base = jnp.concatenate(
        [
            jnp.broadcast_to(jnp.where(place < block, left_col, right_col), (LANES, LANES))
            for place in range(key_blocks)
        ],
        axis=1,
    )
    return score_ref[rows, LANES : LANES + key_blocks * LANES] + base + live_row


def live_keys(meta_ref, key_count):
    places = lax.broadcasted_iota(jnp.int32, (1, key_count), 1)
    return jnp.where(places < meta_ref[1], 0.0, -1e30).astype(jnp.float32)


def attend_kernel(meta_ref, q_ref, k_ref, v_ref, e_ref, c_ref, lse_ref, score_ref, share_ref):
    row_count, key_count = q_ref.shape[0], k_ref.shape[0]
    pair = pl.program_id(0)
    lanes = lax.broadcasted_iota(jnp.int32, (row_count, LANES), 1)
    live_row = live_keys(meta_ref, key_count)
    distance = band_distance()
    result = None
    for half in range(2):
        mine = (lanes < HEAD_DIM) if half == 0 else (lanes >= HEAD_DIM)
        q_half = jnp.where(mine, q_ref[...], 0)
        score_ref[:, LANES : LANES + key_count] = dot_f32(q_half, k_ref[...], NT)
        source = dot_f32(q_half, e_ref[...], NT).astype(jnp.bfloat16).astype(jnp.float32)
        for number in range(row_count // LANES):
            rows = slice(number * LANES, (number + 1) * LANES)
            scores = add_relative(
                score_ref, source, live_row, distance, meta_ref[0] + number, number,
                key_count // LANES,
            )
            peak = jnp.max(scores, axis=1, keepdims=True)
            grown = jnp.exp(scores - peak)
            total = jnp.sum(grown, axis=1, keepdims=True)
            share_ref[rows] = (grown * (1.0 / total)).astype(jnp.bfloat16)
            lse_ref[rows] = jnp.where(
                lanes[rows] == 2 * pair + half, peak + jnp.log(total), lse_ref[rows]
            )
        context = dot_f32(share_ref[...], v_ref[...], NN)
        result = context if half == 0 else jnp.where(mine, context, result)
    c_ref[...] = result.astype(jnp.bfloat16)


def attend_back_kernel(
    meta_ref, q_ref, k_ref, v_ref, e_ref, dc_ref, c_ref, lse_ref,
    dq_ref, dk_ref, dv_ref, de_ref,
    score_ref, grad_ref, share_ref, slope_ref, source_ref, wide_ref,
):
    row_count, key_count = q_ref.shape[0], k_ref.shape[0]
    key_blocks = key_count // LANES
    pair = pl.program_id(0)
    lanes = lax.broadcasted_iota(jnp.int32, (row_count, LANES), 1)
    live_row = live_keys(meta_ref, key_count)
    distance = band_distance()
    inside = (distance > -LEFT) & (distance < RIGHT)
    square = (LANES, LANES)
    flip = (
        lax.broadcasted_iota(jnp.int32, square, 0) + lax.broadcasted_iota(jnp.int32, square, 1)
        == LANES - 1
    ).astype(jnp.float32).astype(jnp.bfloat16)
    spots = lax.broadcasted_iota(jnp.int32, (LANES, 2 * LANES), 1)

    @pl.when(pair == 0)
    def _():
        shape = (key_count, LANES)
        before = lax.broadcasted_iota(jnp.int32, shape, 0) < LANES * lax.broadcasted_iota(
            jnp.int32, shape, 1
        )
        wide_ref[:, LANES:] = before.astype(jnp.float32).astype(jnp.bfloat16)
        slope_ref[:, :LANES] = jnp.zeros((row_count, LANES), jnp.bfloat16)
        slope_ref[:, LANES + key_count :] = jnp.zeros((row_count, LANES), jnp.bfloat16)
        de_ref[...] = jnp.zeros(de_ref.shape, jnp.float32)

    wide_ref[:, :LANES] = k_ref[...]
    inner_all = dc_ref[...].astype(jnp.float32) * c_ref[...].astype(jnp.float32)
    grad_q = grad_k = grad_v = None
    for half in range(2):
        mine = (lanes < HEAD_DIM) if half == 0 else (lanes >= HEAD_DIM)
        q_half = jnp.where(mine, q_ref[...], 0)
        dc_half = jnp.where(mine, dc_ref[...], 0)
        score_ref[:, LANES : LANES + key_count] = dot_f32(q_half, k_ref[...], NT)
        grad_ref[...] = dot_f32(dc_half, v_ref[...], NT)
        source = dot_f32(q_half, e_ref[...], NT).astype(jnp.bfloat16).astype(jnp.float32)
        inner = jnp.sum(jnp.where(mine, inner_all, 0.0), axis=1, keepdims=True)
        level = jnp.sum(
            jnp.where(lanes == 2 * pair + half, lse_ref[...], 0.0), axis=1, keepdims=True
        )
        for number in range(row_count // LANES):
            rows = slice(number * LANES, (number + 1) * LANES)
            scores = add_relative(
                score_ref, source, live_row, distance, meta_ref[0] + number, number, key_blocks
            )
            shares = jnp.exp(scores - level[rows])
            share_ref[rows] = shares.astype(jnp.bfloat16)
            slope_ref[rows, LANES : LANES + key_count] = (
                shares * (grad_ref[rows] - inner[rows])
            ).astype(jnp.bfloat16)
        slopes = slope_ref[:, LANES : LANES + key_count]
        wide = dot_f32(slopes, wide_ref[...], NN)
        before = wide[:, LANES:]
        for number in range(row_count // LANES):
            rows = slice(number * LANES, (number + 1) * LANES)
            block = meta_ref[0] + number
            window = pl.ds(pl.multiple_of(block * LANES, LANES), 3 * LANES)
            seen = slope_ref[rows, window].astype(jnp.float32)
            sums, spot = before[rows], lanes[rows]
            far_left = jnp.sum(
                jnp.where(spot == jnp.maximum(block - 1, 0), sums, 0.0), axis=1, keepdims=True
            ) + jnp.sum(jnp.where(distance <= -LEFT, seen, 0.0), axis=1, keepdims=True)
            far_right = jnp.sum(
                jnp.where(spot == key_blocks, sums, 0.0)
                - jnp.where(spot == jnp.minimum(block + 2, key_blocks), sums, 0.0),
                axis=1,
                keepdims=True,
            ) + jnp.sum(jnp.where(distance >= RIGHT, seen, 0.0), axis=1, keepdims=True)
            band = jnp.where(inside, seen, 0.0)
            band = jnp.concatenate(
                [band[:, :LANES] + band[:, 2 * LANES :], band[:, LANES : 2 * LANES]], axis=1
            )
            turned = dot_f32(flip, band.astype(jnp.bfloat16), NN)
            turned = pltpu.roll(turned, 1, 1, stride=1, stride_axis=0)
            turned = dot_f32(flip, turned.astype(jnp.bfloat16), NN)
            turned = jnp.where(
                spots == 2 * LANES - LEFT, far_left, jnp.where(spots == RIGHT, far_right, turned)
            )
            source_ref[rows] = turned.astype(jnp.bfloat16)
        q_part = wide[:, :LANES] + dot_f32(source_ref[...], e_ref[...], NN)
        k_part = dot_f32(q_half, slopes, TN)
        v_part = dot_f32(dc_half, share_ref[...], TN)
        de_ref[...] += dot_f32(q_half, source_ref[...], TN)
        grad_q = q_part if half == 0 else jnp.where(mine, q_part, grad_q)
        grad_k = k_part if half == 0 else grad_k + k_part
        grad_v = v_part if half == 0 else grad_v + v_part
    dq_ref[...] = (grad_q * HEAD_DIM ** (-0.5)).astype(jnp.bfloat16)
    dk_ref[...] = grad_k.T.astype(jnp.bfloat16)
    dv_ref[...] = grad_v.T.astype(jnp.bfloat16)


def pair_spec(row_count):
    return pl.BlockSpec((row_count, LANES), lambda pair, meta: (0, pair))


def fixed_spec(row_count, column_count):
    return pl.BlockSpec((row_count, column_count), lambda pair, meta: (0, 0))


def attend(meta, queries, key_rows, value_rows, table):
    row_count, width = queries.shape
    key_count = key_rows.shape[0]
    return pl.pallas_call(
        attend_kernel,
        grid_spec=pltpu.PrefetchScalarGridSpec(
            num_scalar_prefetch=1,
            grid=(width // LANES,),
            in_specs=[
                pair_spec(row_count),
                pair_spec(key_count),
                pair_spec(key_count),
                fixed_spec(2 * LANES, LANES),
            ],
            out_specs=[pair_spec(row_count), fixed_spec(row_count, LANES)],
            scratch_shapes=[
                pltpu.VMEM((row_count, key_count + 2 * LANES), jnp.float32),
                pltpu.VMEM((row_count, key_count), jnp.bfloat16),
            ],
        ),
        out_shape=[
            jax.ShapeDtypeStruct((row_count, width), jnp.bfloat16),
            jax.ShapeDtypeStruct((row_count, LANES), jnp.float32),
        ],
        compiler_params=pltpu.CompilerParams(vmem_limit_bytes=48 * 2**20),
        name="attend",
    )(meta, queries, key_rows, value_rows, table)


def attend_back(meta, queries, key_rows, value_rows, table, grad_context, context, levels):
    row_count, width = queries.shape
    key_count = key_rows.shape[0]
    return pl.pallas_call(
        attend_back_kernel,
        grid_spec=pltpu.PrefetchScalarGridSpec(
            num_scalar_prefetch=1,
            grid=(width // LANES,),
            in_specs=[
                pair_spec(row_count),
                pair_spec(key_count),
                pair_spec(key_count),
                fixed_spec(2 * LANES, LANES),
                pair_spec(row_count),
                pair_spec(row_count),
                fixed_spec(row_count, LANES),
            ],
            out_specs=[
                pair_spec(row_count),
                pair_spec(key_count),
                pair_spec(key_count),
                fixed_spec(LANES, 2 * LANES),
            ],
            scratch_shapes=[
                pltpu.VMEM((row_count, key_count + 2 * LANES), jnp.float32),
                pltpu.VMEM((row_count, key_count), jnp.float32),
                pltpu.VMEM((row_count, key_count), jnp.bfloat16),
                pltpu.VMEM((row_count, key_count + 2 * LANES), jnp.bfloat16),
                pltpu.VMEM((row_count, 2 * LANES), jnp.bfloat16),
                pltpu.VMEM((key_count, 2 * LANES), jnp.bfloat16),
            ],
        ),
        out_shape=[
            jax.ShapeDtypeStruct((row_count, width), jnp.bfloat16),
            jax.ShapeDtypeStruct((key_count, width), jnp.bfloat16),
            jax.ShapeDtypeStruct((key_count, width), jnp.bfloat16),
            jax.ShapeDtypeStruct((LANES, 2 * LANES), jnp.float32),
        ],
        compiler_params=pltpu.CompilerParams(vmem_limit_bytes=48 * 2**20),
        name="attend_back",
    )(meta, queries, key_rows, value_rows, table, grad_context, context, levels)


def wide_table(table_low):
    places = jnp.arange(2 * LANES)
    offsets = jnp.clip(jnp.where(places < LANES, places, places - 2 * LANES) + LEFT, 0, OFFSETS - 1)
    rows = table_low[offsets]
    return jnp.concatenate([rows, rows], axis=1)


def table_grad(wide_grad):
    folded = (wide_grad[:HEAD_DIM] + wide_grad[HEAD_DIM:]).T
    return jnp.concatenate([folded[2 * LANES - LEFT :], folded[: RIGHT + 1]], axis=0)


def apply_swish(values):
    return values * jax.nn.sigmoid(values)


def swish_slope(values):
    logistic = jax.nn.sigmoid(values)
    return logistic + values * logistic * (1.0 - logistic)


def matmul(left_side, right_side):
    return dot_f32(left_side, right_side, NN)


def norm_rows(values, gain_row, shift_row):
    centred = values - jnp.mean(values, axis=-1, keepdims=True)
    variance = jnp.mean(centred * centred, axis=-1, keepdims=True)
    inverse = lax.rsqrt(variance + EPSILON)
    normal = centred * inverse
    return (normal * gain_row + shift_row, normal, inverse)


def norm_back(grad_out, normal, inverse, gain_row):
    grad_normal = grad_out * gain_row
    grad_in = inverse * (
        grad_normal
        - jnp.mean(grad_normal, axis=-1, keepdims=True)
        - normal * jnp.mean(grad_normal * normal, axis=-1, keepdims=True)
    )
    return (grad_in, jnp.sum(grad_out * normal, axis=0), jnp.sum(grad_out, axis=0))


def fence(*values):
    return lax.optimization_barrier(values)


TENSOR = ("far", "z")


class Place:
    def __init__(self):
        axes = ("y", "x", "core", "far", "z")
        self.count = {axis: lax.axis_size(axis) for axis in axes}
        self.index = {axis: lax.axis_index(axis) for axis in axes}
        count, index = self.count, self.index
        count["t"] = count["far"] * count["z"]
        index["t"] = index["far"] * count["z"] + index["z"]
        count["seq"] = count["far"] * 2
        index["seq"] = index["far"] * 2 + index["core"]
        count["a"], count["b"] = count["x"], count["y"]
        self.mixed = count["x"] == count["y"]
        self.swapped = (index["core"] == 1) if self.mixed else jnp.zeros((), bool)
        index["a"] = jnp.where(self.swapped, index["y"], index["x"])
        index["b"] = jnp.where(self.swapped, index["x"], index["y"])
        self.names = {"t": TENSOR, "seq": ("core", "far")}
        self.dp_count = count["y"] * count["x"] * 2

    def seq_pair(self, start, end):
        far = self.count["far"]
        return ((start % 2) * far + start // 2, (end % 2) * far + end // 2)

    def turn(self, block, axis, step):
        size = self.count[axis]
        pairs = [(start, (start + step) % size) for start in range(size)]
        if axis == "seq":
            pairs = [self.seq_pair(*pair) for pair in pairs]
        if axis in ("a", "b"):
            y_count, x_count = self.count["y"], self.count["x"]
            pairs = []
            for y in range(y_count):
                for x in range(x_count):
                    for core in range(2):
                        along_x = (axis == "a") != (self.mixed and core == 1)
                        new_y = y if along_x else (y + step) % y_count
                        new_x = (x + step) % x_count if along_x else x
                        pairs.append(
                            ((y * x_count + x) * 2 + core, (new_y * x_count + new_x) * 2 + core)
                        )
            return lax.ppermute(block, ("y", "x", "core"), pairs)
        return lax.ppermute(block, self.names.get(axis, axis), pairs)

    def after(self, axis, step):
        return lax.rem(self.index[axis] + step, self.count[axis])

    def block(self, a_index, b_index):
        x_count = self.count["x"]
        return jnp.where(self.swapped, a_index * x_count + b_index, b_index * x_count + a_index)

    def steps(self, axis):
        return range(1, self.count[axis])


def packed(shard):
    rows, columns = shard.shape
    blocks = shard.reshape(rows // columns, columns, columns)
    return blocks.transpose(1, 0, 2).reshape(columns, rows)


def unpacked(block):
    columns, rows = block.shape
    blocks = block.reshape(columns, rows // columns, columns)
    return blocks.transpose(1, 0, 2).reshape(rows, columns)


def gather_t(place, shard):
    return jnp.stack([shard] + [place.turn(shard, "t", step) for step in place.steps("t")])


def gather_a(place, stack):
    return jnp.concatenate([stack] + [place.turn(stack, "a", step) for step in place.steps("a")])


def gather_b(place, stack):
    return [stack] + [place.turn(stack, "b", step) for step in place.steps("b")]


def gather_core(place, stacks):
    return stacks + [place.turn(stack, "core", 1) for stack in stacks]


def assemble(place, stacks, targets):
    counts, dp_count, t_count = place.count, place.dp_count, place.count["t"]
    dtype = stacks[0].dtype
    shard_shape = stacks[0].shape[1:]
    rows, columns = shard_shape[-2:]
    shapes, copy_counts = [], 0
    for target in targets:
        if target[0] == "rows":
            shapes.append((target[2], target[3] * dp_count, columns * t_count))
            copy_counts += dp_count * t_count
        elif target[0] == "columns":
            aligned = columns % LANES == 0
            shape = (rows * t_count, columns * dp_count)
            shapes.append(shape if aligned else (dp_count, rows * t_count, columns))
            copy_counts += dp_count * t_count
        elif target[0] == "packed":
            aligned = rows % LANES == 0
            shape = (columns * t_count, rows * dp_count)
            shapes.append(shape if aligned else (dp_count, t_count, rows, columns))
            copy_counts += dp_count * t_count * (columns // rows if aligned else 1)
        else:
            shapes.append((dp_count, target[2], columns))
            copy_counts += dp_count

    def kernel(meta_ref, *refs):
        stack_refs = refs[: len(stacks)]
        out_refs = refs[len(stacks) : len(stacks) + len(targets)]
        sem = refs[-1]
        copies = []

        def send(source, target):
            copy = pltpu.make_async_copy(source, target, sem.at[len(copies)])
            copy.start()
            copies.append(copy)

        b_count = counts["b"]
        for number, stack_ref in enumerate(stack_refs):
            other, b_step = number // b_count, number % b_count
            core = lax.rem(meta_ref[2] + other, 2)
            for a_step in range(counts["a"]):
                y_spot = lax.rem(meta_ref[0] - b_step + counts["y"], counts["y"])
                x_spot = lax.rem(meta_ref[1] - a_step + counts["x"], counts["x"])
                if place.mixed:
                    y_other = lax.rem(meta_ref[0] - a_step + counts["y"], counts["y"])
                    x_other = lax.rem(meta_ref[1] - b_step + counts["x"], counts["x"])
                    y_spot = jnp.where(core == 1, y_other, y_spot)
                    x_spot = jnp.where(core == 1, x_other, x_spot)
                dp_spot = (y_spot * counts["x"] + x_spot) * 2 + core
                for t_step in range(t_count):
                    t_spot = lax.rem(meta_ref[3] - t_step + t_count, t_count)
                    shard_ref = stack_ref.at[a_step * t_count + t_step]
                    for target, out_ref in zip(targets, out_refs):
                        t_columns = pl.ds(pl.multiple_of(t_spot * columns, columns), columns)
                        if target[0] == "rows":
                            first, depth, count = target[1:]
                            source = shard_ref.at[first : first + depth, 0:count, :]
                            here = pl.ds(pl.multiple_of(dp_spot * count, count), count)
                            send(source, out_ref.at[:, here, t_columns])
                        elif target[0] == "columns":
                            here = pl.ds(pl.multiple_of(t_spot * rows, rows), rows)
                            if columns % LANES == 0:
                                there = pl.ds(pl.multiple_of(dp_spot * columns, columns), columns)
                                send(shard_ref, out_ref.at[here, there])
                            else:
                                send(shard_ref, out_ref.at[dp_spot, here, :])
                        elif target[0] == "packed":
                            if rows % LANES == 0:
                                there = pl.ds(pl.multiple_of(dp_spot * rows, rows), rows)
                                for part in range(columns // rows):
                                    here = pl.ds(
                                        pl.multiple_of(t_spot * columns + part * rows, rows), rows
                                    )
                                    send(
                                        shard_ref.at[target[1], :, part * rows : (part + 1) * rows],
                                        out_ref.at[here, there],
                                    )
                            else:
                                send(shard_ref.at[target[1]], out_ref.at[dp_spot, t_spot])
                        elif t_step == 0:
                            first_row, count = target[1:]
                            send(shard_ref.at[0, first_row : first_row + count, :], out_ref.at[dp_spot])
        for copy in copies:
            copy.wait()

    meta = jnp.stack([place.index[axis] for axis in ("y", "x", "core", "t")]).astype(jnp.int32)
    results = pl.pallas_call(
        kernel,
        grid_spec=pltpu.PrefetchScalarGridSpec(
            num_scalar_prefetch=1,
            grid=(),
            in_specs=[pl.BlockSpec(memory_space=pl.ANY)] * len(stacks),
            out_specs=[pl.BlockSpec(memory_space=pltpu.VMEM)] * len(targets),
            scratch_shapes=[pltpu.SemaphoreType.DMA((copy_counts,))],
        ),
        out_shape=[jax.ShapeDtypeStruct(shape, dtype) for shape in shapes],
        compiler_params=pltpu.CompilerParams(vmem_limit_bytes=20 * 2**20),
        name="assemble",
    )(meta, *stacks)
    finished = []
    for target, whole in zip(targets, results):
        if target[0] == "columns" and columns % LANES:
            whole = whole.transpose(1, 0, 2).reshape(rows * t_count, columns * dp_count)
        if target[0] == "packed" and rows % LANES:
            whole = whole.reshape(dp_count, t_count, rows, columns // rows, rows)
            whole = whole.transpose(1, 3, 2, 0, 4).reshape(columns * t_count, rows * dp_count)
        finished.append(whole)
    return finished


def pick_blocks(array, numbers, count):
    if array.ndim == 4:
        return jnp.concatenate([lax.dynamic_slice_in_dim(array, one, 1, axis=1) for one in numbers], axis=1)
    width = array.shape[1] // count
    return jnp.concatenate(
        [lax.dynamic_slice_in_dim(array, one * width, width, axis=1) for one in numbers], axis=1
    )


def pick_t(array, number, count):
    axis = 3 if array.ndim == 4 else 0
    width = array.shape[axis] // count
    return lax.dynamic_slice_in_dim(array, number * width, width, axis=axis)


def added(arrays):
    total = arrays[0].astype(jnp.float32)
    for array in arrays[1:]:
        total = total + array.astype(jnp.float32)
    return total


def reduce_core(place, product):
    other = place.turn(product(1 - place.index["core"]), "core", 1)
    return [product(place.index["core"]), other]


def reduce_b(place, parts):
    blocks = place.count["a"] * place.count["b"]
    arrived = []
    for step in place.steps("b"):
        numbers = [
            place.block(number, place.after("b", step)) for number in range(place.count["a"])
        ]
        message = added([pick_blocks(part, numbers, blocks) for part in parts])
        arrived.append(place.turn(message.astype(parts[0].dtype), "b", step))
    return (parts, arrived)


def reduce_a(place, state):
    parts, from_b = state
    blocks, a_count = place.count["a"] * place.count["b"], place.count["a"]
    arrived = []
    for step in place.steps("a"):
        there = place.after("a", step)
        number = place.block(there, place.index["b"])
        message = added(
            [pick_blocks(part, [number], blocks) for part in parts]
            + [pick_blocks(part, [there], a_count) for part in from_b]
        )
        arrived.append(place.turn(message.astype(parts[0].dtype), "a", step))
    return (parts, from_b, arrived)


def reduce_t(place, state):
    parts, from_b, from_a = state
    blocks, a_count, t_count = place.count["a"] * place.count["b"], place.count["a"], place.count["t"]
    number = place.block(place.index["a"], place.index["b"])
    mine = [pick_blocks(part, [number], blocks) for part in parts]
    mine += [pick_blocks(part, [place.index["a"]], a_count) for part in from_b]
    mine += from_a
    arrived = []
    for step in place.steps("t"):
        message = added([pick_t(part, place.after("t", step), t_count) for part in mine])
        arrived.append(place.turn(message.astype(parts[0].dtype), "t", step))
    return ([pick_t(part, place.index["t"], t_count) for part in mine], arrived)


def reduce_end(state):
    total = added(state[0] + state[1])
    return total[:, 0] if total.ndim == 4 else total


def core_columns(place, rows_in, core):
    blocks = place.count["y"] * place.count["x"]
    width = rows_in.shape[-1] // (2 * blocks)
    return jnp.concatenate(
        [
            lax.dynamic_slice_in_dim(rows_in, (2 * block + core) * width, width, axis=-1)
            for block in range(blocks)
        ],
        axis=-1,
    )


def term_by_rows(place, inputs, grads, extra=None):
    blocks = place.count["y"] * place.count["x"]

    def product(core):
        left_side = core_columns(place, inputs, core)
        terms = [dot_f32(left_side, grad, TN).astype(jnp.bfloat16) for grad in grads]
        terms = [term.reshape(blocks, -1, term.shape[-1]) for term in terms]
        if extra is not None:
            term = dot_f32(extra[0], core_columns(place, extra[1], core), TN).astype(jnp.bfloat16)
            width = term.shape[1] // blocks
            term = term.reshape(-1, width, blocks, width).transpose(2, 1, 0, 3)
            terms.append(term.reshape(blocks, width, -1))
        return jnp.stack(terms)

    return product


def term_by_columns(place, inputs, grad):
    def product(core):
        return dot_f32(inputs, core_columns(place, grad, core), TN).astype(jnp.bfloat16)

    return product


def term_of_vectors(place, rows_in):
    blocks = place.count["y"] * place.count["x"]

    def product(core):
        mine = core_columns(place, rows_in, core)
        return mine.reshape(rows_in.shape[0], blocks, -1).transpose(1, 0, 2)[None]

    return product


def clip_pairs(micro, z_count, step):
    return [
        (core * z_count + z, (z // micro) * z_count + micro * core + (step + z) % micro)
        for core in range(2)
        for z in range(z_count)
    ]


def to_clip(place, blocks):
    micro, z_count = blocks.shape[0], place.count["z"]
    z_here = place.index["z"]
    arrived = []
    for step in range(micro):
        block = lax.dynamic_index_in_dim(blocks, lax.rem(z_here + step, micro), 0, keepdims=False)
        arrived.append(lax.ppermute(block, ("core", "z"), clip_pairs(micro, z_count, step)))
    return arrived


def ordered_clip(place, arrived):
    micro, z_here = len(arrived), place.index["z"]
    stack = jnp.stack(arrived)
    ordered = [
        lax.dynamic_index_in_dim(stack, lax.rem(z_here - spot + micro, micro), 0, keepdims=False)
        for spot in range(micro)
    ]
    return jnp.concatenate(ordered, axis=0)


def from_clip(place, rows_in, micro):
    z_count, z_here = place.count["z"], place.index["z"]
    blocks = rows_in.reshape(micro, -1, rows_in.shape[-1])
    arrived = []
    for step in range(micro):
        spot = lax.rem(z_here - step + micro, micro)
        block = lax.dynamic_index_in_dim(blocks, spot, 0, keepdims=False)
        pairs = [(end, start) for start, end in clip_pairs(micro, z_count, step)]
        arrived.append(lax.ppermute(block, ("core", "z"), pairs))
    return arrived


def own_clips(place, arrived):
    micro, z_here = len(arrived), place.index["z"]
    stack = jnp.stack(arrived)
    return jnp.stack(
        [
            lax.dynamic_index_in_dim(
                stack, lax.rem(number - lax.rem(z_here, micro) + micro, micro), 0, keepdims=False
            )
            for number in range(micro)
        ]
    )


def all_rows(place, own):
    count = place.count["seq"]
    whole = jnp.zeros((count,) + own.shape, own.dtype)
    for step in range(count):
        block = own if step == 0 else place.turn(own, "seq", step)
        spot = lax.rem(place.index["seq"] - step + count, count)
        whole = lax.dynamic_update_index_in_dim(whole, block, spot, 0)
    return whole.reshape((count * own.shape[0],) + own.shape[1:])


def own_sum(place, partial):
    count = place.count["seq"]
    blocks = partial.reshape(count, -1, partial.shape[-1])
    total = lax.dynamic_index_in_dim(blocks, place.index["seq"], 0, keepdims=False).astype(jnp.float32)
    for step in range(1, count):
        message = lax.dynamic_index_in_dim(blocks, place.after("seq", step), 0, keepdims=False)
        total = total + place.turn(message, "seq", step).astype(jnp.float32)
    return total


def neighbour_rows(place, rows_in, step):
    count = place.count["seq"]
    pairs = [
        place.seq_pair(start, start + step) for start in range(count) if 0 <= start + step < count
    ]
    return lax.ppermute(rows_in, place.names["seq"], pairs)


def feed_up(inputs, up_weight, up_bias, gain_row, shift_row):
    normed, normal, inverse = norm_rows(inputs, gain_row, shift_row)
    normed = normed.astype(jnp.bfloat16)
    upper_rows = matmul(normed, up_weight) + up_bias
    hidden = apply_swish(upper_rows).astype(jnp.bfloat16)
    return (hidden, (normal, inverse, normed, upper_rows.astype(jnp.bfloat16)))


def feed_back_down(grad_result, stored, down_weight):
    upper_rows = stored[3]
    grad_low = grad_result.astype(jnp.bfloat16)
    grad_hidden = dot_f32(grad_low, down_weight, NT)
    grad_upper = (grad_hidden * swish_slope(upper_rows.astype(jnp.float32))).astype(jnp.bfloat16)
    up_bias_grad = jnp.sum(grad_upper.astype(jnp.float32), axis=0)
    down_bias_grad = jnp.sum(grad_low.astype(jnp.float32), axis=0)
    return (grad_low, grad_upper, up_bias_grad, down_bias_grad)


def body(
    frames,
    cotangent,
    clip_valid,
    frame_counts,
    rel_rows,
    first_up,
    first_down,
    attend_in,
    attend_out,
    pointwise_in,
    pointwise_out,
    second_up,
    second_down,
    vectors,
    distance,
):
    place = Place()
    micro, _, width = frames.shape
    ratio_rows = FF // width
    attend_base = 3 + ratio_rows
    conv_base = attend_base + 5
    second_base = conv_base + 4
    final_base = second_base + 3 + ratio_rows
    taps_base = final_base + 2
    scale = HEAD_DIM ** (-0.5)

    up_rows, up_columns = first_up.shape
    vector_rows = 16
    vector_parts = up_columns // vectors.shape[1]
    padded_vectors = jnp.pad(vectors, ((0, vector_rows * vector_parts - vectors.shape[0]), (0, 0)))
    vector_shard = (
        padded_vectors.reshape(vector_parts, vector_rows, -1).transpose(1, 0, 2).reshape(vector_rows, -1)
    )
    shard_up_one = jnp.concatenate([first_up, vector_shard], axis=0)[None]
    shard_attend = jnp.concatenate([attend_in, packed(attend_out)[None]])
    shard_point = jnp.concatenate([pointwise_in, packed(pointwise_out)[None]])

    own_facts = jnp.stack([clip_valid, frame_counts])
    other_facts = place.turn(own_facts, "core", 1)
    up_one = gather_t(place, shard_up_one)
    rows_low = to_clip(place, frames)
    up_one, first_down, frames_, shard_attend = fence(up_one, first_down, frames, shard_attend)
    up_one = gather_a(place, up_one)
    down_one = gather_t(place, first_down)
    up_one, down_one, rows_low, shard_attend = fence(up_one, down_one, rows_low, shard_attend)
    up_one = gather_b(place, up_one)
    down_one = gather_a(place, down_one)
    attend_mix = gather_t(place, shard_attend)
    up_one, down_one, attend_mix, shard_point, rows_low = fence(
        up_one, down_one, attend_mix, shard_point, rows_low
    )
    up_one = gather_core(place, up_one)
    down_one = gather_b(place, down_one)
    attend_mix = gather_a(place, attend_mix)
    point_mix = gather_t(place, shard_point)
    up_one, vector_slabs = assemble(
        place, up_one, [("rows", 0, 1, up_rows), ("slabs", up_rows, vector_rows)]
    )
    up_one = up_one[0]
    vector_wide = vector_slabs.reshape(place.dp_count, vector_rows, vector_parts, -1)
    vector_wide = vector_wide.transpose(2, 1, 0, 3).reshape(vector_rows * vector_parts, width)
    vector_wide = vector_wide[: vectors.shape[0]].astype(jnp.float32)

    rows_in = ordered_clip(place, rows_low).astype(jnp.float32)
    row_count = rows_in.shape[0]
    z_here = place.index["z"]
    facts = jnp.where(z_here // micro == place.index["core"], own_facts, other_facts)
    facts = lax.dynamic_index_in_dim(facts, lax.rem(z_here, micro), 1, keepdims=False)
    valid_flag = (facts[0] > 0).astype(jnp.float32)
    first_row = place.index["seq"] * row_count
    live = ((first_row + jnp.arange(row_count)) < facts[1]).astype(jnp.float32)[:, None]
    meta = jnp.stack([place.index["seq"] * (row_count // LANES), facts[1]]).astype(jnp.int32)
    pick_rows = (rel_rows[:, None] == jnp.arange(OFFSETS)[None, :]).astype(jnp.bfloat16)
    table = wide_table(matmul(pick_rows, distance).astype(jnp.bfloat16))

    one_hidden, one_kept = feed_up(
        rows_in,
        up_one,
        vector_wide[2 : 2 + ratio_rows].reshape(FF),
        vector_wide[0],
        vector_wide[1],
    )
    (down_one, attend_mix, point_mix, second_up, one_hidden, one_kept, up_one, table) = fence(
        down_one, attend_mix, point_mix, second_up, one_hidden, one_kept, up_one, table
    )
    down_one = gather_core(place, down_one)
    attend_mix = gather_b(place, attend_mix)
    point_mix = gather_a(place, point_mix)
    up_two = gather_t(place, second_up[None])
    (down_one,) = assemble(place, down_one, [("columns",)])
    after_one = rows_in + 0.5 * (matmul(one_hidden, down_one) + vector_wide[2 + ratio_rows])
    attend_normed, attend_normal, attend_inverse = norm_rows(
        after_one, vector_wide[attend_base], vector_wide[attend_base + 1]
    )
    attend_normed = attend_normed.astype(jnp.bfloat16)
    (attend_mix, point_mix, up_two, second_down, after_one, attend_normed, attend_normal, attend_inverse) = fence(
        attend_mix, point_mix, up_two, second_down, after_one, attend_normed, attend_normal, attend_inverse
    )
    attend_mix = gather_core(place, attend_mix)
    point_mix = gather_b(place, point_mix)
    up_two = gather_a(place, up_two)
    down_two = gather_t(place, second_down)
    attend_mix, attend_back_weight = assemble(place, attend_mix, [("rows", 0, 3, up_rows), ("packed", 3)])
    queries = (matmul(attend_normed, attend_mix[0]) + vector_wide[attend_base + 2]).astype(jnp.bfloat16)
    queries = (queries.astype(jnp.float32) * scale).astype(jnp.bfloat16)
    own_keys = matmul(attend_normed, attend_mix[1]).astype(jnp.bfloat16)
    own_values = (matmul(attend_normed, attend_mix[2]) + vector_wide[attend_base + 3]).astype(jnp.bfloat16)
    key_rows, value_rows = all_rows(place, own_keys), all_rows(place, own_values)
    context, levels = attend(meta, queries, key_rows, value_rows, table)
    (point_mix, up_two, down_two, cotangent, context, levels, after_one) = fence(
        point_mix, up_two, down_two, cotangent, context, levels, after_one
    )
    point_mix = gather_core(place, point_mix)
    up_two = gather_b(place, up_two)
    down_two = gather_a(place, down_two)
    cot_low = to_clip(place, cotangent)
    point_mix, point_back = assemble(place, point_mix, [("rows", 0, 2, up_rows), ("packed", 2)])
    after_two = after_one + matmul(context, attend_back_weight) + vector_wide[attend_base + 4]
    conv_normed, conv_normal, conv_inverse = norm_rows(
        after_two, vector_wide[conv_base], vector_wide[conv_base + 1]
    )
    conv_normed = conv_normed.astype(jnp.bfloat16)
    linear = matmul(conv_normed, point_mix[0])
    logistic = jax.nn.sigmoid(matmul(conv_normed, point_mix[1]))
    gated = linear * logistic * live
    taps = vector_wide[taps_base : taps_base + KERNEL]
    reach = KERNEL - 1
    before = neighbour_rows(place, gated[-reach:], 1)
    padded = jnp.concatenate([before, gated], axis=0)
    depth_out = jnp.zeros_like(gated)
    for offset in range(KERNEL):
        depth_out = depth_out + taps[offset] * padded[offset : offset + row_count]
    deep_gain = vector_wide[conv_base + 2]
    deep_norm, deep_normal, deep_inverse = norm_rows(depth_out, deep_gain, vector_wide[conv_base + 3])
    activated = apply_swish(deep_norm).astype(jnp.bfloat16)
    after_three = after_two + matmul(activated, point_back)
    (up_two, down_two, cot_low, after_three, padded, deep_norm, deep_normal, activated) = fence(
        up_two, down_two, cot_low, after_three, padded, deep_norm, deep_normal, activated
    )
    up_two = gather_core(place, up_two)
    down_two = gather_b(place, down_two)
    (up_two,) = assemble(place, up_two, [("rows", 0, 1, up_rows)])
    up_two = up_two[0]
    two_hidden, two_kept = feed_up(
        after_three,
        up_two,
        vector_wide[second_base + 2 : second_base + 2 + ratio_rows].reshape(FF),
        vector_wide[second_base],
        vector_wide[second_base + 1],
    )
    (down_two, two_hidden, two_kept, up_two) = fence(down_two, two_hidden, two_kept, up_two)
    down_two = gather_core(place, down_two)
    (down_two,) = assemble(place, down_two, [("columns",)])
    two_out = matmul(two_hidden, down_two) + vector_wide[second_base + 2 + ratio_rows]
    after_four = after_three + 0.5 * two_out
    final_rows, final_normal, final_inverse = norm_rows(
        after_four, vector_wide[final_base], vector_wide[final_base + 1]
    )
    row_out = jnp.where(valid_flag > 0, final_rows, rows_in).astype(jnp.bfloat16)
    rows_cot = ordered_clip(place, cot_low).astype(jnp.float32)
    grad_four, final_gain_grad, final_shift_grad = norm_back(
        rows_cot * valid_flag, final_normal, final_inverse, vector_wide[final_base]
    )
    grad_low, grad_upper, two_up_bias, two_down_bias = feed_back_down(
        0.5 * grad_four, two_kept, down_two
    )
    sum_down_two = reduce_core(place, term_by_columns(place, two_hidden, grad_low))
    (sum_down_two, grad_four, grad_upper, row_out) = fence(sum_down_two, grad_four, grad_upper, row_out)
    sum_down_two = reduce_b(place, sum_down_two)
    frames_out = from_clip(place, row_out, micro)
    sum_up_two = reduce_core(place, term_by_rows(place, two_kept[2], [grad_upper]))
    grad_normed = dot_f32(grad_upper, up_two, NT)
    grad_two_in, two_gain, two_shift = norm_back(
        grad_normed, two_kept[0], two_kept[1], vector_wide[second_base]
    )
    grad_three = grad_four + grad_two_in
    conv_low = grad_three.astype(jnp.bfloat16)
    grad_deep = dot_f32(conv_low, point_back, NT) * swish_slope(deep_norm)
    grad_depth, deep_gain_grad, deep_shift_grad = norm_back(
        grad_deep, deep_normal, deep_inverse, deep_gain
    )
    after = neighbour_rows(place, grad_depth[:reach], -1)
    (sum_down_two, frames_out, sum_up_two, grad_three, conv_low, grad_depth, after) = fence(
        sum_down_two, frames_out, sum_up_two, grad_three, conv_low, grad_depth, after
    )
    sum_down_two = reduce_a(place, sum_down_two)
    sum_up_two = reduce_b(place, sum_up_two)
    extended = jnp.concatenate([grad_depth, after], axis=0)
    grad_gated = jnp.zeros_like(grad_depth)
    tap_grads = []
    for offset in range(KERNEL):
        tap_grads.append(jnp.sum(padded[offset : offset + row_count] * grad_depth, axis=0))
        grad_gated = grad_gated + taps[offset] * extended[reach - offset : reach - offset + row_count]
    tap_grads = jnp.stack(tap_grads)
    grad_gated = grad_gated * live
    grad_linear = (grad_gated * logistic).astype(jnp.bfloat16)
    grad_gate = (grad_gated * linear * logistic * (1.0 - logistic)).astype(jnp.bfloat16)
    (sum_down_two, sum_up_two, grad_linear, grad_gate, tap_grads) = fence(
        sum_down_two, sum_up_two, grad_linear, grad_gate, tap_grads
    )
    sum_down_two = reduce_t(place, sum_down_two)
    sum_up_two = reduce_a(place, sum_up_two)
    sum_point = reduce_core(
        place, term_by_rows(place, conv_normed, [grad_linear, grad_gate], (activated, conv_low))
    )
    grad_conv_normed = dot_f32(grad_linear, point_mix[0], NT) + dot_f32(grad_gate, point_mix[1], NT)
    grad_conv_in, conv_gain_grad, conv_shift_grad = norm_back(
        grad_conv_normed, conv_normal, conv_inverse, vector_wide[conv_base]
    )
    grad_two = grad_three + grad_conv_in
    attend_low = grad_two.astype(jnp.bfloat16)
    grad_context = dot_f32(attend_low, attend_back_weight, NT).astype(jnp.bfloat16)
    (sum_down_two, sum_up_two, sum_point, grad_two, attend_low, grad_context) = fence(
        sum_down_two, sum_up_two, sum_point, grad_two, attend_low, grad_context
    )
    grad_second_down = reduce_end(sum_down_two)
    sum_up_two = reduce_t(place, sum_up_two)
    sum_point = reduce_b(place, sum_point)
    grad_queries, part_keys, part_values, grad_table = attend_back(
        meta, queries, key_rows, value_rows, table, grad_context, context, levels
    )
    (sum_up_two, sum_point, grad_queries, part_keys, part_values, grad_table) = fence(
        sum_up_two, sum_point, grad_queries, part_keys, part_values, grad_table
    )
    grad_second_up = reduce_end(sum_up_two)[0]
    sum_point = reduce_a(place, sum_point)
    grad_keys = own_sum(place, part_keys).astype(jnp.bfloat16)
    grad_values = own_sum(place, part_values).astype(jnp.bfloat16)
    sum_distance = jnp.dot(
        pick_rows.astype(jnp.float32).T, table_grad(grad_table), precision=lax.Precision.HIGHEST
    )
    sum_distance = sum_distance + place.turn(sum_distance, "core", 1)
    sum_attend = reduce_core(
        place,
        term_by_rows(place, attend_normed, [grad_queries, grad_keys, grad_values], (context, attend_low)),
    )
    grad_attend_normed = (
        dot_f32(grad_queries, attend_mix[0], NT)
        + dot_f32(grad_keys, attend_mix[1], NT)
        + dot_f32(grad_values, attend_mix[2], NT)
    )
    grad_attend_in, attend_gain_grad, attend_shift_grad = norm_back(
        grad_attend_normed, attend_normal, attend_inverse, vector_wide[attend_base]
    )
    grad_one = grad_two + grad_attend_in
    (sum_point, sum_attend, sum_distance, grad_one) = fence(sum_point, sum_attend, sum_distance, grad_one)
    sum_point = reduce_t(place, sum_point)
    sum_attend = reduce_b(place, sum_attend)
    sum_distance = sum(
        (place.turn(sum_distance, "b", step) for step in place.steps("b")), sum_distance
    )
    grad_low, grad_upper, one_up_bias, one_down_bias = feed_back_down(0.5 * grad_one, one_kept, down_one)
    sum_down_one = reduce_core(place, term_by_columns(place, one_hidden, grad_low))
    (sum_point, sum_attend, sum_distance, sum_down_one, grad_upper) = fence(
        sum_point, sum_attend, sum_distance, sum_down_one, grad_upper
    )
    grad_point = reduce_end(sum_point)
    sum_attend = reduce_a(place, sum_attend)
    sum_down_one = reduce_b(place, sum_down_one)
    sum_distance = sum(
        (place.turn(sum_distance, "a", step) for step in place.steps("a")), sum_distance
    )
    sum_up_one = reduce_core(place, term_by_rows(place, one_kept[2], [grad_upper]))
    grad_normed = dot_f32(grad_upper, up_one, NT)
    grad_one_in, one_gain, one_shift = norm_back(grad_normed, one_kept[0], one_kept[1], vector_wide[0])
    grad_rows = grad_one + grad_one_in + (1.0 - valid_flag) * rows_cot

    def column_sum(rows):
        return jnp.sum(rows.astype(jnp.float32), axis=0)

    vector_part = jnp.concatenate(
        [
            jnp.stack([one_gain, one_shift]),
            one_up_bias.reshape(ratio_rows, width),
            jnp.stack(
                [
                    one_down_bias,
                    attend_gain_grad,
                    attend_shift_grad,
                    column_sum(grad_queries),
                    column_sum(grad_values),
                    column_sum(attend_low),
                    conv_gain_grad,
                    conv_shift_grad,
                    deep_gain_grad,
                    deep_shift_grad,
                    two_gain,
                    two_shift,
                ]
            ),
            two_up_bias.reshape(ratio_rows, width),
            jnp.stack([two_down_bias, final_gain_grad, final_shift_grad]),
            tap_grads,
        ],
        axis=0,
    )
    grad_rows = grad_rows.astype(jnp.bfloat16)
    sum_vectors = reduce_core(place, term_of_vectors(place, vector_part))
    (sum_attend, sum_down_one, sum_distance, sum_up_one, sum_vectors, grad_rows) = fence(
        sum_attend, sum_down_one, sum_distance, sum_up_one, sum_vectors, grad_rows
    )
    sum_up_one = reduce_b(place, sum_up_one)
    sum_down_one = reduce_a(place, sum_down_one)
    sum_attend = reduce_t(place, sum_attend)
    sum_vectors = reduce_b(place, sum_vectors)
    sum_distance = sum(
        (place.turn(sum_distance, "t", step) for step in place.steps("t")), sum_distance
    )
    frames_grad = from_clip(place, grad_rows, micro)
    (sum_up_one, sum_down_one, sum_attend, sum_vectors, sum_distance) = fence(
        sum_up_one, sum_down_one, sum_attend, sum_vectors, sum_distance
    )
    grad_attend = reduce_end(sum_attend)
    sum_up_one = reduce_a(place, sum_up_one)
    sum_down_one = reduce_t(place, sum_down_one)
    sum_vectors = reduce_a(place, sum_vectors)
    (sum_up_one, sum_down_one, sum_vectors, frames_grad) = fence(
        sum_up_one, sum_down_one, sum_vectors, frames_grad
    )
    grad_first_down = reduce_end(sum_down_one)
    sum_up_one = reduce_t(place, sum_up_one)
    sum_vectors = reduce_t(place, sum_vectors)
    grad_first_up = reduce_end(sum_up_one)[0]
    grad_vectors = reduce_end(sum_vectors)[0]
    return (
        own_clips(place, frames_out),
        own_clips(place, frames_grad),
        grad_first_up,
        grad_first_down,
        grad_attend[:3],
        unpacked(grad_attend[3]),
        grad_point[:2],
        unpacked(grad_point[2]),
        grad_second_up,
        grad_second_down,
        grad_vectors,
        sum_distance,
    )


def solution(mesh):
    dp_count, tensor_count = mesh.shape["dp"], mesh.shape["tensor"]

    def program(*arrays):
        group = 2 * (arrays[0].shape[0] // dp_count)
        parted = Mesh(
            mesh.devices.reshape(dp_count // 4, 2, 2, tensor_count // group, group),
            ("y", "x", "core", "far", "z"),
        )
        dp, tensor = ("y", "x", "core"), TENSOR
        return jax.shard_map(
            body,
            mesh=parted,
            in_specs=(
                P(dp, tensor, None),
                P(dp, tensor, None),
                P(dp),
                P(dp),
                P(),
                P(dp, tensor),
                P(tensor, dp),
                P(None, dp, tensor),
                P(tensor, dp),
                P(None, dp, tensor),
                P(tensor, dp),
                P(dp, tensor),
                P(tensor, dp),
                P(None, dp),
                P(),
            ),
            out_specs=(
                P(dp, tensor, None),
                P(dp, tensor, None),
                P(dp, tensor),
                P(tensor, dp),
                P(None, dp, tensor),
                P(tensor, dp),
                P(None, dp, tensor),
                P(tensor, dp),
                P(dp, tensor),
                P(tensor, dp),
                P(None, dp + tensor),
                P(),
            ),
            check_vma=False,
        )(*arrays)

    return program
```

```python
import jax
import jax.numpy as jnp
from jax import lax
from jax.experimental import pallas as pl
from jax.experimental.pallas import tpu as pltpu
from jax.sharding import Mesh
from jax.sharding import PartitionSpec as P

HEADS = 16
HEAD_DIM = 64
FF = 4096
KERNEL = 31
LEFT = 64
OFFSETS = 73
EPSILON = 1e-05

LANES = 128
SOFT_ROWS = 32
SLOPE_ROWS = 16
RIGHT = OFFSETS - 1 - LEFT
NT = (((1,), (1,)), ((), ()))
NN = (((1,), (0,)), ((), ()))
TN = (((0,), (0,)), ((), ()))


def dot_f32(left_side, right_side, dims):
    return lax.dot_general(left_side, right_side, dims, preferred_element_type=jnp.float32)


def band_distance():
    shape = (LANES, 3 * LANES)
    return (
        lax.broadcasted_iota(jnp.int32, shape, 1)
        - LANES
        - lax.broadcasted_iota(jnp.int32, shape, 0)
    )


LAST_ROWS = 8


def add_band(score_ref, half, source, distance, block, number):
    rows = slice(number * LANES, (number + 1) * LANES)
    own = source[rows]
    left_col = own[:, 2 * LANES - LEFT : 2 * LANES - LEFT + 1]
    right_col = own[:, RIGHT : RIGHT + 1]
    rolled = pltpu.roll(own - right_col, LANES, 1, stride=1, stride_axis=0)
    window = pl.multiple_of(block * LANES, LANES)
    near = rolled[:LEFT, :LANES] + (right_col - left_col)[:LEFT]
    near = jnp.where(distance[:LEFT, :LANES] > -LEFT, near, 0.0)
    score_ref[half, number * LANES : number * LANES + LEFT, pl.ds(window, LANES)] += near
    score_ref[half, rows, pl.ds(window + LANES, LANES)] += rolled[:, LANES:]
    last = LANES - LAST_ROWS
    after = jnp.where(distance[last:, 2 * LANES :] < RIGHT, rolled[last:, :LANES], 0.0)
    score_ref[half, number * LANES + last : (number + 1) * LANES, pl.ds(window + 2 * LANES, LANES)] += after


def in_half(shape, half):
    lanes = lax.broadcasted_iota(jnp.int32, shape, 1)
    return (lanes < HEAD_DIM) if half == 0 else (lanes >= HEAD_DIM)


def spare_lane(shape):
    return lax.rem(lax.broadcasted_iota(jnp.int32, shape, 1), HEAD_DIM)


def key_marks(meta_ref, key_count, blocks):
    shape = (key_count, LANES)
    spare, keys = spare_lane(shape), lax.broadcasted_iota(jnp.int32, shape, 0)
    before = keys < (meta_ref[0] + spare // 2) * LANES
    side = jnp.where(lax.rem(spare, 2) == 0, before.astype(jnp.float32), 1.0 - before.astype(jnp.float32))
    dead = jnp.where(keys < meta_ref[1], 0.0, -1e30)
    ones = (spare < 2 * blocks + 4).astype(jnp.float32)
    marks = jnp.where(spare < 2 * blocks, side, jnp.where(spare == 2 * blocks, dead, ones))
    return marks.astype(jnp.bfloat16)


def in_parts(column):
    parts = []
    for _ in range(3):
        part = column.astype(jnp.bfloat16).astype(jnp.float32)
        parts.append(part)
        column = column - part
    return parts


def with_marks(rows_half, half, columns_of):
    square = (LANES, LANES)
    spare, mine = spare_lane(square), in_half(square, half)
    parts = []
    for number in range(rows_half.shape[0] // LANES):
        own = rows_half[number * LANES : (number + 1) * LANES].astype(jnp.float32)
        marks = jnp.zeros(square, jnp.float32)
        for place, column in columns_of(number):
            marks = jnp.where(spare == place, column, marks)
        parts.append(jnp.where(mine, own, marks).astype(jnp.bfloat16))
    return jnp.concatenate(parts, axis=0)


def marked_queries(q_half, half, source, extra, blocks):
    def columns_of(number):
        rows = slice(number * LANES, (number + 1) * LANES)
        own = source[rows]
        columns = [
            (2 * number, own[:, 2 * LANES - LEFT : 2 * LANES - LEFT + 1]),
            (2 * number + 1, own[:, RIGHT : RIGHT + 1]),
            (2 * blocks, 1.0),
        ]
        return columns + [(2 * blocks + 1 + place, part[rows]) for place, part in enumerate(extra)]

    return with_marks(q_half, half, columns_of)


def attend_kernel(meta_ref, q_ref, k_ref, v_ref, e_ref, c_ref, lse_ref, score_ref, share_ref, marks_ref):
    row_count, key_count = q_ref.shape[0], k_ref.shape[0]
    blocks = row_count // LANES
    pair = pl.program_id(0)
    lanes = lax.broadcasted_iota(jnp.int32, (row_count, LANES), 1)
    distance = band_distance()

    @pl.when(pair == 0)
    def _():
        marks_ref[...] = key_marks(meta_ref, key_count, blocks)

    sources = []
    for half in range(2):
        mine = in_half((row_count, LANES), half)
        q_half = jnp.where(mine, q_ref[...], 0)
        source = dot_f32(q_half, e_ref[...], NT).astype(jnp.bfloat16).astype(jnp.float32)
        sources.append(source)
        queries = marked_queries(q_half, half, source, [], blocks)
        keys = jnp.where(in_half((key_count, LANES), half), k_ref[...], marks_ref[...])
        score_ref[half, :, LANES : LANES + key_count] = dot_f32(queries, keys, NT)
    result = None
    for half in range(2):
        inverses = []
        for number in range(blocks):
            rows = slice(number * LANES, (number + 1) * LANES)
            add_band(score_ref, half, sources[half], distance, meta_ref[0] + number, number)
            for first in range(number * LANES, (number + 1) * LANES, SOFT_ROWS):
                few = slice(first, first + SOFT_ROWS)
                scores = score_ref[half, few, LANES : LANES + key_count]
                peak = jnp.max(scores, axis=1, keepdims=True)
                grown = jnp.exp(scores - peak)
                total = jnp.sum(grown, axis=1, keepdims=True)
                share_ref[half, few] = grown.astype(jnp.bfloat16)
                inverses.append(1.0 / total)
                lse_ref[few] = jnp.where(
                    lanes[few] == 2 * pair + half, peak + jnp.log(total), lse_ref[few]
                )
        context = dot_f32(share_ref[half], v_ref[...], NN) * jnp.concatenate(inverses, axis=0)
        result = context if half == 0 else jnp.where(in_half(context.shape, 1), context, result)
    c_ref[...] = result.astype(jnp.bfloat16)


def attend_back_kernel(
    meta_ref, q_ref, k_ref, v_ref, e_ref, dc_ref, c_ref, lse_ref,
    dq_ref, dk_ref, dv_ref, de_ref,
    score_ref, grad_ref, share_ref, slope_ref, source_ref, wide_ref, marks_ref,
):
    row_count, key_count = q_ref.shape[0], k_ref.shape[0]
    key_blocks, blocks = key_count // LANES, row_count // LANES
    pair = pl.program_id(0)
    lanes = lax.broadcasted_iota(jnp.int32, (row_count, LANES), 1)
    distance = band_distance()
    square = (LANES, LANES)
    flip = (
        lax.broadcasted_iota(jnp.int32, square, 0) + lax.broadcasted_iota(jnp.int32, square, 1)
        == LANES - 1
    ).astype(jnp.float32).astype(jnp.bfloat16)
    spots = lax.broadcasted_iota(jnp.int32, square, 1)

    @pl.when(pair == 0)
    def _():
        shape = (key_count, LANES)
        place = lax.broadcasted_iota(jnp.int32, shape, 1)
        edge = (meta_ref[0] + place // 2) * LANES
        key = lax.broadcasted_iota(jnp.int32, shape, 0)
        before = (key < edge).astype(jnp.float32)
        after = (key >= edge + LANES).astype(jnp.float32)
        wide_ref[:, LANES:] = jnp.where(lax.rem(place, 2) == 0, before, after).astype(jnp.bfloat16)
        for half in range(2):
            slope_ref[half, :, :LANES] = jnp.zeros((row_count, LANES), jnp.bfloat16)
            slope_ref[half, :, LANES + key_count :] = jnp.zeros((row_count, LANES), jnp.bfloat16)
        de_ref[...] = jnp.zeros(de_ref.shape, jnp.float32)
        marks_ref[0] = key_marks(meta_ref, key_count, blocks)
        marks_ref[1] = (spare_lane(shape) < 3).astype(jnp.float32).astype(jnp.bfloat16)

    wide_ref[:, :LANES] = k_ref[...]
    inner_all = dc_ref[...].astype(jnp.float32) * c_ref[...].astype(jnp.float32)
    sources, q_halves, dc_halves = [], [], []
    for half in range(2):
        mine, mine_keys = in_half((row_count, LANES), half), in_half((key_count, LANES), half)
        q_half = jnp.where(mine, q_ref[...], 0)
        dc_half = jnp.where(mine, dc_ref[...], 0)
        source = dot_f32(q_half, e_ref[...], NT).astype(jnp.bfloat16).astype(jnp.float32)
        inner = jnp.sum(jnp.where(mine, inner_all, 0.0), axis=1, keepdims=True)
        level = jnp.sum(
            jnp.where(lanes == 2 * pair + half, lse_ref[...], 0.0), axis=1, keepdims=True
        )
        queries = marked_queries(q_half, half, source, in_parts(-level), blocks)
        keys = jnp.where(mine_keys, k_ref[...], marks_ref[0])
        score_ref[half, :, LANES : LANES + key_count] = dot_f32(queries, keys, NT)
        inner_parts = in_parts(-inner)
        grads = with_marks(
            dc_half,
            half,
            lambda number, parts=inner_parts: [
                (place, part[number * LANES : (number + 1) * LANES])
                for place, part in enumerate(parts)
            ],
        )
        values = jnp.where(mine_keys, v_ref[...], marks_ref[1])
        grad_ref[half] = dot_f32(grads, values, NT)
        sources.append(source)
        q_halves.append(q_half)
        dc_halves.append(dc_half)
    grad_q = grad_k = grad_v = None
    for half in range(2):
        for number in range(blocks):
            rows = slice(number * LANES, (number + 1) * LANES)
            add_band(score_ref, half, sources[half], distance, meta_ref[0] + number, number)
            for first in range(number * LANES, (number + 1) * LANES, SLOPE_ROWS):
                few = slice(first, first + SLOPE_ROWS)
                shares = jnp.exp(score_ref[half, few, LANES : LANES + key_count])
                share_ref[half, few] = shares.astype(jnp.bfloat16)
                slope_ref[half, few, LANES : LANES + key_count] = (
                    shares * grad_ref[half, few]
                ).astype(jnp.bfloat16)
    for half in range(2):
        mine = in_half((row_count, LANES), half)
        slopes = slope_ref[half, :, LANES : LANES + key_count]
        wide = dot_f32(slopes, wide_ref[...], NN)
        before = wide[:, LANES:]
        for number in range(blocks):
            rows = slice(number * LANES, (number + 1) * LANES)
            window = pl.multiple_of((meta_ref[0] + number) * LANES, LANES)
            first, last = number * LANES, (number + 1) * LANES - LAST_ROWS
            near = slope_ref[half, first : first + LEFT, pl.ds(window, LANES)].astype(jnp.float32)
            near = jnp.where(distance[:LEFT, :LANES] > -LEFT, near, 0.0)
            final = slope_ref[half, last - 8 : last + 8, pl.ds(window + 2 * LANES, LANES)]
            final = final.astype(jnp.float32)[8:]
            final = jnp.where(distance[LANES - LAST_ROWS :, 2 * LANES :] < RIGHT, final, 0.0)
            middle = slope_ref[half, rows, pl.ds(window + LANES, LANES)]
            gap = jnp.zeros((LANES - LEFT - LAST_ROWS, LANES), jnp.float32)
            edges = jnp.concatenate([near, gap, final], axis=0)
            inner_sum = jnp.sum(edges, axis=1, keepdims=True)
            first_rows = lax.broadcasted_iota(jnp.int32, (LANES, 1), 0) < LEFT
            far_left = before[rows, 2 * number : 2 * number + 1] - jnp.where(first_rows, inner_sum, 0.0)
            far_right = before[rows, 2 * number + 1 : 2 * number + 2] - jnp.where(
                first_rows, 0.0, inner_sum
            )
            band = jnp.concatenate([edges.astype(jnp.bfloat16), middle], axis=1)
            turned = dot_f32(flip, band, NN)
            turned = pltpu.roll(turned, 1, 1, stride=1, stride_axis=0)
            turned = dot_f32(flip, turned.astype(jnp.bfloat16), NN)
            turned = jnp.concatenate(
                [
                    turned[:, :LANES] + jnp.where(spots == RIGHT, far_right, 0.0),
                    turned[:, LANES:] + jnp.where(spots == 0, far_left, 0.0),
                ],
                axis=1,
            )
            source_ref[half, rows] = turned.astype(jnp.bfloat16)
        q_part = wide[:, :LANES] + dot_f32(source_ref[half], e_ref[...], NN)
        k_part = dot_f32(q_halves[half], slopes, TN)
        v_part = dot_f32(dc_halves[half], share_ref[half], TN)
        de_ref[...] += dot_f32(q_halves[half], source_ref[half], TN)
        grad_q = q_part if half == 0 else jnp.where(mine, q_part, grad_q)
        grad_k = k_part if half == 0 else grad_k + k_part
        grad_v = v_part if half == 0 else grad_v + v_part
    dq_ref[...] = (grad_q * HEAD_DIM ** (-0.5)).astype(jnp.bfloat16)
    dk_ref[...] = grad_k.T.astype(jnp.bfloat16)
    dv_ref[...] = grad_v.T.astype(jnp.bfloat16)


def pair_spec(row_count):
    return pl.BlockSpec((row_count, LANES), lambda pair, meta: (0, pair))


def fixed_spec(row_count, column_count):
    return pl.BlockSpec((row_count, column_count), lambda pair, meta: (0, 0))


def attend(meta, queries, key_rows, value_rows, table):
    row_count, width = queries.shape
    key_count = key_rows.shape[0]
    return pl.pallas_call(
        attend_kernel,
        grid_spec=pltpu.PrefetchScalarGridSpec(
            num_scalar_prefetch=1,
            grid=(width // LANES,),
            in_specs=[
                pair_spec(row_count),
                pair_spec(key_count),
                pair_spec(key_count),
                fixed_spec(2 * LANES, LANES),
            ],
            out_specs=[pair_spec(row_count), fixed_spec(row_count, LANES)],
            scratch_shapes=[
                pltpu.VMEM((2, row_count, key_count + 2 * LANES), jnp.float32),
                pltpu.VMEM((2, row_count, key_count), jnp.bfloat16),
                pltpu.VMEM((key_count, LANES), jnp.bfloat16),
            ],
        ),
        out_shape=[
            jax.ShapeDtypeStruct((row_count, width), jnp.bfloat16),
            jax.ShapeDtypeStruct((row_count, LANES), jnp.float32),
        ],
        compiler_params=pltpu.CompilerParams(vmem_limit_bytes=48 * 2**20),
        name="attend",
    )(meta, queries, key_rows, value_rows, table)


def attend_back(meta, queries, key_rows, value_rows, table, grad_context, context, levels):
    row_count, width = queries.shape
    key_count = key_rows.shape[0]
    return pl.pallas_call(
        attend_back_kernel,
        grid_spec=pltpu.PrefetchScalarGridSpec(
            num_scalar_prefetch=1,
            grid=(width // LANES,),
            in_specs=[
                pair_spec(row_count),
                pair_spec(key_count),
                pair_spec(key_count),
                fixed_spec(2 * LANES, LANES),
                pair_spec(row_count),
                pair_spec(row_count),
                fixed_spec(row_count, LANES),
            ],
            out_specs=[
                pair_spec(row_count),
                pair_spec(key_count),
                pair_spec(key_count),
                fixed_spec(LANES, 2 * LANES),
            ],
            scratch_shapes=[
                pltpu.VMEM((2, row_count, key_count + 2 * LANES), jnp.float32),
                pltpu.VMEM((2, row_count, key_count), jnp.float32),
                pltpu.VMEM((2, row_count, key_count), jnp.bfloat16),
                pltpu.VMEM((2, row_count, key_count + 2 * LANES), jnp.bfloat16),
                pltpu.VMEM((2, row_count, 2 * LANES), jnp.bfloat16),
                pltpu.VMEM((key_count, 2 * LANES), jnp.bfloat16),
                pltpu.VMEM((2, key_count, LANES), jnp.bfloat16),
            ],
        ),
        out_shape=[
            jax.ShapeDtypeStruct((row_count, width), jnp.bfloat16),
            jax.ShapeDtypeStruct((key_count, width), jnp.bfloat16),
            jax.ShapeDtypeStruct((key_count, width), jnp.bfloat16),
            jax.ShapeDtypeStruct((LANES, 2 * LANES), jnp.float32),
        ],
        compiler_params=pltpu.CompilerParams(vmem_limit_bytes=48 * 2**20),
        name="attend_back",
    )(meta, queries, key_rows, value_rows, table, grad_context, context, levels)


def wide_table(table_low):
    places = jnp.arange(2 * LANES)
    offsets = jnp.clip(jnp.where(places < LANES, places, places - 2 * LANES) + LEFT, 0, OFFSETS - 1)
    rows = table_low[offsets]
    return jnp.concatenate([rows, rows], axis=1)


def table_grad(wide_grad):
    folded = (wide_grad[:HEAD_DIM] + wide_grad[HEAD_DIM:]).T
    first = jnp.sum(folded[LANES : 2 * LANES - LEFT + 1], axis=0, keepdims=True)
    last = jnp.sum(folded[RIGHT:LANES], axis=0, keepdims=True)
    return jnp.concatenate([first, folded[2 * LANES - LEFT + 1 :], folded[:RIGHT], last], axis=0)


def sigmoid(values):
    return 0.5 * jnp.tanh(0.5 * values) + 0.5


def swish_slope(values, logistic):
    return logistic + values * logistic * (1.0 - logistic)


def matmul(left_side, right_side):
    return dot_f32(left_side, right_side, NN)


def norm_rows(values, gain_row, shift_row):
    centred = values - jnp.mean(values, axis=-1, keepdims=True)
    variance = jnp.mean(centred * centred, axis=-1, keepdims=True)
    inverse = lax.rsqrt(variance + EPSILON)
    normal = centred * inverse
    return (normal * gain_row + shift_row, normal, inverse)


def norm_back(grad_out, normal, inverse, gain_row):
    grad_normal = grad_out * gain_row
    grad_in = inverse * (
        grad_normal
        - jnp.mean(grad_normal, axis=-1, keepdims=True)
        - normal * jnp.mean(grad_normal * normal, axis=-1, keepdims=True)
    )
    return (grad_in, jnp.sum(grad_out * normal, axis=0), jnp.sum(grad_out, axis=0))


CHUNK = 64
HALO = 32


def tap_slices(window, offsets):
    length = window.shape[0]
    slices = {}
    for rest in range(8):
        wanted = [offset for offset in offsets if offset % 8 == rest]
        if wanted:
            turned = pltpu.roll(window, length - rest, 0) if rest else window
            for offset in wanted:
                slices[offset] = turned[offset - rest : offset - rest + CHUNK]
    return slices


def convolve_kernel(before_ref, gated_ref, taps_ref, gain_ref, shift_ref, deep_ref, low_ref, padded_ref):
    row_count, width = gated_ref.shape
    lead = HALO - (KERNEL - 1)
    padded_ref[:HALO] = before_ref[...]
    padded_ref[HALO:] = gated_ref[...]

    @pl.loop(0, width // LANES)
    def _(column):
        lanes = pl.ds(pl.multiple_of(column * LANES, LANES), LANES)
        taps = [taps_ref[tap : tap + 1, lanes] for tap in range(KERNEL)]

        @pl.loop(0, row_count // CHUNK)
        def _(chunk):
            first = pl.multiple_of(chunk * CHUNK, CHUNK)
            window = padded_ref[pl.ds(first, CHUNK + HALO), lanes]
            slices = tap_slices(window, [tap + lead for tap in range(KERNEL)])
            total = taps[0] * slices[lead]
            for tap in range(1, KERNEL):
                total = total + taps[tap] * slices[tap + lead]
            deep_ref[pl.ds(first, CHUNK), lanes] = total

    @pl.loop(0, row_count // CHUNK)
    def _(chunk):
        rows = pl.ds(pl.multiple_of(chunk * CHUNK, CHUNK), CHUNK)
        deep_norm, _, _ = norm_rows(deep_ref[rows, :], gain_ref[...], shift_ref[...])
        low_ref[rows, :] = (deep_norm * sigmoid(deep_norm)).astype(jnp.bfloat16)


def convolve(before, gated, taps, gain_row, shift_row):
    shape = gated.shape
    return pl.pallas_call(
        convolve_kernel,
        in_specs=[pl.BlockSpec(memory_space=pltpu.VMEM)] * 5,
        out_specs=[pl.BlockSpec(memory_space=pltpu.VMEM)] * 2,
        out_shape=[
            jax.ShapeDtypeStruct(shape, jnp.float32),
            jax.ShapeDtypeStruct(shape, jnp.bfloat16),
        ],
        scratch_shapes=[pltpu.VMEM((shape[0] + HALO, shape[1]), jnp.float32)],
        compiler_params=pltpu.CompilerParams(vmem_limit_bytes=32 * 2**20),
        name="convolve",
    )(before, gated, taps, gain_row[None], shift_row[None])


def convolve_back_kernel(
    meta_ref, grad_ref, after_ref, before_ref, gated_ref, taps_ref, linear_ref, logistic_ref,
    pair_ref, tap_grad_ref, padded_ref, extended_ref,
):
    row_count, width = gated_ref.shape
    lead = HALO - (KERNEL - 1)
    padded_ref[:HALO] = before_ref[...]
    padded_ref[HALO:] = gated_ref[...]
    extended_ref[:row_count] = grad_ref[...]
    extended_ref[row_count:] = after_ref[...]
    live_rows = meta_ref[1] - meta_ref[0] * LANES

    @pl.loop(0, width // LANES)
    def _(column):
        start = pl.multiple_of(column * LANES, LANES)
        lanes = pl.ds(start, LANES)
        taps = [taps_ref[tap : tap + 1, lanes] for tap in range(KERNEL)]

        @pl.loop(0, row_count // CHUNK)
        def _(chunk):
            first = pl.multiple_of(chunk * CHUNK, CHUNK)
            rows = pl.ds(first, CHUNK)
            window = extended_ref[pl.ds(first, CHUNK + HALO), lanes]
            slices = tap_slices(window, [KERNEL - 1 - tap for tap in range(KERNEL)])
            total = taps[0] * slices[KERNEL - 1]
            for tap in range(1, KERNEL):
                total = total + taps[tap] * slices[KERNEL - 1 - tap]
            places = first + lax.broadcasted_iota(jnp.int32, (CHUNK, LANES), 0)
            logistic = logistic_ref[rows, lanes]
            grad_linear = jnp.where(places < live_rows, total, 0.0) * logistic
            pair_ref[rows, lanes] = grad_linear.astype(jnp.bfloat16)
            grad_gate = grad_linear * linear_ref[rows, lanes] * (1.0 - logistic)
            gate_lanes = pl.ds(pl.multiple_of(width + start, LANES), LANES)
            pair_ref[rows, gate_lanes] = grad_gate.astype(jnp.bfloat16)

        def tap_step(chunk, totals):
            first = pl.multiple_of(chunk * CHUNK, CHUNK)
            window = padded_ref[pl.ds(first, CHUNK + HALO), lanes]
            slices = tap_slices(window, [tap + lead for tap in range(KERNEL)])
            grad = extended_ref[pl.ds(first, CHUNK), lanes]
            added_up = []
            for tap in range(KERNEL):
                product = slices[tap + lead] * grad
                part = product[:8]
                for piece in range(1, CHUNK // 8):
                    part = part + product[8 * piece : 8 * piece + 8]
                added_up.append(totals[tap] + part)
            return tuple(added_up)

        zero = jnp.zeros((8, LANES), jnp.float32)
        totals = lax.fori_loop(0, row_count // CHUNK, tap_step, (zero,) * KERNEL)
        for tap in range(KERNEL):
            tap_grad_ref[tap : tap + 1, lanes] = jnp.sum(totals[tap], axis=0, keepdims=True)


def convolve_back(meta, grad_depth, after, before, gated, taps, linear, logistic):
    row_count, width = gated.shape
    vmem = pl.BlockSpec(memory_space=pltpu.VMEM)
    return pl.pallas_call(
        convolve_back_kernel,
        grid_spec=pltpu.PrefetchScalarGridSpec(
            num_scalar_prefetch=1,
            grid=(),
            in_specs=[vmem] * 7,
            out_specs=[vmem] * 2,
            scratch_shapes=[pltpu.VMEM((row_count + HALO, width), jnp.float32)] * 2,
        ),
        out_shape=[
            jax.ShapeDtypeStruct((row_count, 2 * width), jnp.bfloat16),
            jax.ShapeDtypeStruct(taps.shape, jnp.float32),
        ],
        compiler_params=pltpu.CompilerParams(vmem_limit_bytes=40 * 2**20),
        name="convolve_back",
    )(meta, grad_depth, after, before, gated, taps, linear, logistic)


def fence(*values):
    return lax.optimization_barrier(values)


TENSOR = ("far", "z")


class Place:
    def __init__(self):
        axes = ("y", "x", "core", "far", "z")
        self.count = {axis: lax.axis_size(axis) for axis in axes}
        self.index = {axis: lax.axis_index(axis) for axis in axes}
        count, index = self.count, self.index
        count["t"] = count["far"] * count["z"]
        index["t"] = index["far"] * count["z"] + index["z"]
        count["seq"] = count["far"] * 2
        index["seq"] = index["far"] * 2 + index["core"]
        count["a"], count["b"] = count["x"], count["y"]
        self.mixed = count["x"] == count["y"]
        self.names = {"t": TENSOR, "seq": ("core", "far")}
        self.dp_count = count["y"] * count["x"] * 2

    def seq_pair(self, start, end):
        far = self.count["far"]
        return ((start % 2) * far + start // 2, (end % 2) * far + end // 2)

    def turn(self, block, axis, step):
        size = self.count[axis]
        pairs = [(start, (start + step) % size) for start in range(size)]
        if axis == "seq":
            pairs = [self.seq_pair(*pair) for pair in pairs]
        if axis in ("a", "b"):
            y_count, x_count = self.count["y"], self.count["x"]
            pairs = []
            for y in range(y_count):
                for x in range(x_count):
                    for core in range(2):
                        along_x = (axis == "a") != (self.mixed and core == 1)
                        new_y = y if along_x else (y + step) % y_count
                        new_x = (x + step) % x_count if along_x else x
                        pairs.append(
                            ((y * x_count + x) * 2 + core, (new_y * x_count + new_x) * 2 + core)
                        )
            return lax.ppermute(block, ("y", "x", "core"), pairs)
        return lax.ppermute(block, self.names.get(axis, axis), pairs)

    def after(self, axis, step):
        return lax.rem(self.index[axis] + step, self.count[axis])

    def blocks_for(self, core):
        y_count, x_count = self.count["y"], self.count["x"]
        numbers = []
        for b_step in [*self.steps("b"), 0]:
            for a_step in [*self.steps("a"), 0]:
                y = lax.rem(self.index["y"] + b_step, y_count)
                x = lax.rem(self.index["x"] + a_step, x_count)
                if self.mixed:
                    y = jnp.where(core == 1, lax.rem(self.index["y"] + a_step, y_count), y)
                    x = jnp.where(core == 1, lax.rem(self.index["x"] + b_step, x_count), x)
                numbers.append((y * x_count + x) * 2 + core)
        return numbers

    def steps(self, axis):
        return range(1, self.count[axis])


def packed(shard):
    rows, columns = shard.shape
    blocks = shard.reshape(rows // columns, columns, columns)
    return blocks.transpose(1, 0, 2).reshape(columns, rows)


def gather_t(place, shard):
    return lax.all_gather(shard, TENSOR, axis=0)


def gather_a(place, stack):
    return jnp.concatenate([stack] + [place.turn(stack, "a", step) for step in place.steps("a")])


def gather_b(place, stack):
    return [stack] + [place.turn(stack, "b", step) for step in place.steps("b")]


def gather_core(place, stacks):
    return stacks + [place.turn(stack, "core", 1) for stack in stacks]


def assemble(place, stacks, targets):
    counts, dp_count, t_count = place.count, place.dp_count, place.count["t"]
    dtype = stacks[0].dtype
    shard_shape = stacks[0].shape[1:]
    rows, columns = shard_shape[-2:]
    shapes, copy_counts = [], 0
    for target in targets:
        if target[0] == "rows":
            shapes.append((target[2], target[3] * dp_count, columns * t_count))
            copy_counts += dp_count * t_count
        elif target[0] == "columns":
            aligned = columns % LANES == 0
            shape = (rows * t_count, columns * dp_count)
            shapes.append(shape if aligned else (dp_count, rows * t_count, columns))
            copy_counts += dp_count * t_count
        elif target[0] == "packed":
            aligned = rows % LANES == 0
            shape = (columns * t_count, rows * dp_count)
            shapes.append(shape if aligned else (dp_count, t_count, rows, columns))
            copy_counts += dp_count * t_count * (columns // rows if aligned else 1)
        else:
            shapes.append((dp_count, target[2], columns))
            copy_counts += dp_count

    def kernel(meta_ref, *refs):
        stack_refs = refs[: len(stacks)]
        out_refs = refs[len(stacks) : len(stacks) + len(targets)]
        sem = refs[-1]
        copies = []

        def send(source, target):
            copy = pltpu.make_async_copy(source, target, sem.at[len(copies)])
            copy.start()
            copies.append(copy)

        b_count = counts["b"]
        for number, stack_ref in enumerate(stack_refs):
            other, b_step = number // b_count, number % b_count
            core = lax.rem(meta_ref[2] + other, 2)
            for a_step in range(counts["a"]):
                y_spot = lax.rem(meta_ref[0] - b_step + counts["y"], counts["y"])
                x_spot = lax.rem(meta_ref[1] - a_step + counts["x"], counts["x"])
                if place.mixed:
                    y_other = lax.rem(meta_ref[0] - a_step + counts["y"], counts["y"])
                    x_other = lax.rem(meta_ref[1] - b_step + counts["x"], counts["x"])
                    y_spot = jnp.where(core == 1, y_other, y_spot)
                    x_spot = jnp.where(core == 1, x_other, x_spot)
                dp_spot = (y_spot * counts["x"] + x_spot) * 2 + core
                for t_step in range(t_count):
                    t_spot = t_step
                    shard_ref = stack_ref.at[a_step * t_count + t_step]
                    for target, out_ref in zip(targets, out_refs):
                        t_columns = pl.ds(pl.multiple_of(t_spot * columns, columns), columns)
                        if target[0] == "rows":
                            first, depth, count = target[1:]
                            source = shard_ref.at[first : first + depth, 0:count, :]
                            here = pl.ds(pl.multiple_of(dp_spot * count, count), count)
                            send(source, out_ref.at[:, here, t_columns])
                        elif target[0] == "columns":
                            here = pl.ds(pl.multiple_of(t_spot * rows, rows), rows)
                            if columns % LANES == 0:
                                there = pl.ds(pl.multiple_of(dp_spot * columns, columns), columns)
                                send(shard_ref, out_ref.at[here, there])
                            else:
                                send(shard_ref, out_ref.at[dp_spot, here, :])
                        elif target[0] == "packed":
                            if rows % LANES == 0:
                                there = pl.ds(pl.multiple_of(dp_spot * rows, rows), rows)
                                for part in range(columns // rows):
                                    here = pl.ds(
                                        pl.multiple_of(t_spot * columns + part * rows, rows), rows
                                    )
                                    send(
                                        shard_ref.at[target[1], :, part * rows : (part + 1) * rows],
                                        out_ref.at[here, there],
                                    )
                            else:
                                send(shard_ref.at[target[1]], out_ref.at[dp_spot, t_spot])
                        elif t_step == 0:
                            first_row, count = target[1:]
                            send(shard_ref.at[0, first_row : first_row + count, :], out_ref.at[dp_spot])
        for copy in copies:
            copy.wait()

    meta = jnp.stack([place.index[axis] for axis in ("y", "x", "core", "t")]).astype(jnp.int32)
    results = pl.pallas_call(
        kernel,
        grid_spec=pltpu.PrefetchScalarGridSpec(
            num_scalar_prefetch=1,
            grid=(),
            in_specs=[pl.BlockSpec(memory_space=pl.ANY)] * len(stacks),
            out_specs=[pl.BlockSpec(memory_space=pltpu.VMEM)] * len(targets),
            scratch_shapes=[pltpu.SemaphoreType.DMA((copy_counts,))],
        ),
        out_shape=[jax.ShapeDtypeStruct(shape, dtype) for shape in shapes],
        compiler_params=pltpu.CompilerParams(vmem_limit_bytes=20 * 2**20),
        name="assemble",
    )(meta, *stacks)
    finished = []
    for target, whole in zip(targets, results):
        if target[0] == "columns" and columns % LANES:
            whole = whole.transpose(1, 0, 2).reshape(rows * t_count, columns * dp_count)
        if target[0] == "packed" and rows % LANES:
            whole = whole.reshape(dp_count, t_count, rows, columns // rows, rows)
            whole = whole.transpose(1, 3, 2, 0, 4).reshape(columns * t_count, rows * dp_count)
        finished.append(whole)
    return finished


def sent_order(place, width):
    core = place.index["core"]
    numbers = jnp.stack(place.blocks_for(1 - core) + place.blocks_for(core))
    block = width // place.dp_count
    sources = (numbers[:, None] * block + jnp.arange(block)[None, :]).reshape(1, width)
    return (jnp.arange(width)[:, None] == sources).astype(jnp.bfloat16)


def reduce_core(place, pairs):
    group = []
    for inputs, grads in pairs:
        half = inputs.shape[1] // 2
        product = dot_f32(inputs[:, :half], grads, TN).astype(jnp.bfloat16)
        group.append((inputs, grads, place.turn(product, "core", 1)))
    return group


def reduce_b(place, group):
    result = []
    for inputs, grads, other in group:
        half = inputs.shape[1] // 2
        step_rows = half // place.count["b"]
        arrived = []
        for number, step in enumerate([*place.steps("b"), 0]):
            columns = slice(half + number * step_rows, half + (number + 1) * step_rows)
            rows = slice(number * step_rows, (number + 1) * step_rows)
            term = dot_f32(inputs[:, columns], grads, TN) + other[rows].astype(jnp.float32)
            term = term.astype(jnp.bfloat16)
            arrived.append(term if step == 0 else place.turn(term, "b", step))
        result.append(arrived)
    return result


def added(arrays):
    total = arrays[0].astype(jnp.float32)
    for array in arrays[1:]:
        total = total + array.astype(jnp.float32)
    return total


def reduce_a(place, group):
    result = []
    for arrived in group:
        step_rows = arrived[0].shape[0] // place.count["a"]
        kept = []
        for number, step in enumerate([*place.steps("a"), 0]):
            rows = slice(number * step_rows, (number + 1) * step_rows)
            mine = [one[rows] for one in arrived]
            if step == 0:
                kept += mine
            else:
                kept.append(place.turn(added(mine).astype(mine[0].dtype), "a", step))
        result.append(kept)
    return result


def by_tensor(total, count):
    width = total.shape[1] // count
    return [total[:, number * width : (number + 1) * width] for number in range(count)]


def reduce_t(place, group):
    count = place.count["t"]
    blocks = [[] for _ in range(count)]
    for depth, kept in group:
        total = added(kept).astype(jnp.bfloat16)
        for part in by_tensor(total, depth):
            for number, block in enumerate(by_tensor(part, count)):
                blocks[number].append(block)
    stack = jnp.stack([jnp.stack(block) for block in blocks])
    return lax.psum_scatter(stack, TENSOR, scatter_dimension=0)


def reduce_t_vectors(place, kept, vectors):
    count = place.count["t"]
    total = added(kept).astype(jnp.bfloat16)
    vector_count, columns = vectors.shape[0], total.shape[1] // count
    extra_rows = -(-vectors.size // (count * columns) // 16) * 16 if vectors.size else 0
    extra_rows = max(extra_rows, 16)
    width = vectors.shape[1] // count
    blocks = []
    for block, part in zip(by_tensor(total, count), by_tensor(vectors, count)):
        flat = part.astype(jnp.bfloat16).reshape(1, -1)
        flat = jnp.pad(flat, ((0, 0), (0, extra_rows * columns - flat.shape[1])))
        blocks.append(jnp.concatenate([block, flat.reshape(extra_rows, columns)]))
    result = lax.psum_scatter(jnp.stack(blocks), TENSOR, scatter_dimension=0)
    flat = result[-extra_rows:].reshape(-1)[: vector_count * width]
    return (result[:-extra_rows], flat.reshape(vector_count, width).astype(jnp.float32))


def reduce_vectors_core(place, columns):
    half = columns.shape[1] // 2
    total = columns[:, half:] + place.turn(columns[:, :half], "core", 1)
    return total


def reduce_vectors(place, total, axis):
    width = total.shape[1] // place.count[axis]
    arrived = total[:, -width:]
    for number, step in enumerate(place.steps(axis)):
        arrived = arrived + place.turn(total[:, number * width : (number + 1) * width], axis, step)
    return arrived


def clip_pairs(micro, z_count, step):
    return [
        (core * z_count + z, (z // micro) * z_count + micro * core + (step + z) % micro)
        for core in range(2)
        for z in range(z_count)
    ]


def to_clip(place, blocks):
    micro, z_count = blocks.shape[0], place.count["z"]
    z_here = place.index["z"]
    arrived = []
    for step in range(micro):
        block = lax.dynamic_index_in_dim(blocks, lax.rem(z_here + step, micro), 0, keepdims=False)
        arrived.append(lax.ppermute(block, ("core", "z"), clip_pairs(micro, z_count, step)))
    return arrived


def ordered_clip(place, arrived):
    micro, z_here = len(arrived), place.index["z"]
    stack = jnp.stack(arrived)
    ordered = [
        lax.dynamic_index_in_dim(stack, lax.rem(z_here - spot + micro, micro), 0, keepdims=False)
        for spot in range(micro)
    ]
    return jnp.concatenate(ordered, axis=0)


def from_clip(place, rows_in, micro):
    z_count, z_here = place.count["z"], place.index["z"]
    blocks = rows_in.reshape(micro, -1, rows_in.shape[-1])
    arrived = []
    for step in range(micro):
        spot = lax.rem(z_here - step + micro, micro)
        block = lax.dynamic_index_in_dim(blocks, spot, 0, keepdims=False)
        pairs = [(end, start) for start, end in clip_pairs(micro, z_count, step)]
        arrived.append(lax.ppermute(block, ("core", "z"), pairs))
    return arrived


def own_clips(place, arrived):
    micro, z_here = len(arrived), place.index["z"]
    stack = jnp.stack(arrived)
    return jnp.stack(
        [
            lax.dynamic_index_in_dim(
                stack, lax.rem(number - lax.rem(z_here, micro) + micro, micro), 0, keepdims=False
            )
            for number in range(micro)
        ]
    )


def all_rows(place, own):
    count = place.count["seq"]
    whole = jnp.zeros((count,) + own.shape, own.dtype)
    for step in range(count):
        block = own if step == 0 else place.turn(own, "seq", step)
        spot = lax.rem(place.index["seq"] - step + count, count)
        whole = lax.dynamic_update_index_in_dim(whole, block, spot, 0)
    return whole.reshape((count * own.shape[0],) + own.shape[1:])


def own_sum(place, partial):
    count = place.count["seq"]
    blocks = partial.reshape(count, -1, partial.shape[-1])
    total = lax.dynamic_index_in_dim(blocks, place.index["seq"], 0, keepdims=False).astype(jnp.float32)
    for step in range(1, count):
        message = lax.dynamic_index_in_dim(blocks, place.after("seq", step), 0, keepdims=False)
        total = total + place.turn(message, "seq", step).astype(jnp.float32)
    return total


def neighbour_rows(place, rows_in, step):
    count = place.count["seq"]
    pairs = [
        place.seq_pair(start, start + step) for start in range(count) if 0 <= start + step < count
    ]
    return lax.ppermute(rows_in, place.names["seq"], pairs)


def feed_up(inputs, up_weight, up_bias, gain_row, shift_row):
    normed, normal, inverse = norm_rows(inputs, gain_row, shift_row)
    normed = normed.astype(jnp.bfloat16)
    upper_rows = matmul(normed, up_weight) + up_bias
    logistic = sigmoid(upper_rows)
    hidden = (upper_rows * logistic).astype(jnp.bfloat16)
    slope = swish_slope(upper_rows, logistic).astype(jnp.bfloat16)
    return (hidden, (normal, inverse, normed, slope))


def feed_back_down(grad_result, stored, down_weight):
    grad_low = grad_result.astype(jnp.bfloat16)
    grad_hidden = dot_f32(grad_low, down_weight, NT)
    grad_upper = (grad_hidden * stored[3].astype(jnp.float32)).astype(jnp.bfloat16)
    up_bias_grad = jnp.sum(grad_upper.astype(jnp.float32), axis=0)
    down_bias_grad = jnp.sum(grad_low.astype(jnp.float32), axis=0)
    return (grad_low, grad_upper, up_bias_grad, down_bias_grad)


def body(
    frames,
    cotangent,
    clip_valid,
    frame_counts,
    rel_rows,
    first_up,
    first_down,
    attend_in,
    attend_out,
    pointwise_in,
    pointwise_out,
    second_up,
    second_down,
    vectors,
    distance,
):
    place = Place()
    micro, _, width = frames.shape
    ratio_rows = FF // width
    attend_base = 3 + ratio_rows
    conv_base = attend_base + 5
    second_base = conv_base + 4
    final_base = second_base + 3 + ratio_rows
    taps_base = final_base + 2
    scale = HEAD_DIM ** (-0.5)
    order = sent_order(place, width)

    def sent(rows_low):
        return matmul(rows_low, order).astype(jnp.bfloat16)

    up_rows, up_columns = first_up.shape
    vector_rows = 16
    vector_parts = up_columns // vectors.shape[1]
    padded_vectors = jnp.pad(vectors, ((0, vector_rows * vector_parts - vectors.shape[0]), (0, 0)))
    vector_shard = (
        padded_vectors.reshape(vector_parts, vector_rows, -1).transpose(1, 0, 2).reshape(vector_rows, -1)
    )
    shard_up_one = jnp.concatenate([first_up, vector_shard], axis=0)[None]
    shard_mix = jnp.concatenate(
        [attend_in, packed(attend_out)[None], pointwise_in, packed(pointwise_out)[None]]
    )

    own_facts = jnp.stack([clip_valid, frame_counts])
    up_one = gather_t(place, shard_up_one)
    up_one, first_down, own_facts = fence(up_one, first_down, own_facts)
    up_one = gather_a(place, up_one)
    down_one = gather_t(place, first_down)
    other_facts = place.turn(own_facts, "core", 1)
    up_one, frames, shard_mix = fence(up_one, frames, shard_mix)
    up_one = gather_b(place, up_one)
    rows_low = to_clip(place, frames)
    down_one = gather_a(place, down_one)
    both_mix = gather_t(place, shard_mix)
    up_one, down_one, second_up = fence(up_one, down_one, second_up)
    up_one = gather_core(place, up_one)
    down_one = gather_b(place, down_one)
    attend_mix = gather_a(place, both_mix[:, : attend_in.shape[0] + 1])
    point_mix = both_mix[:, attend_in.shape[0] + 1 :]
    up_two = gather_t(place, second_up[None])
    up_one, vector_slabs = assemble(
        place, up_one, [("rows", 0, 1, up_rows), ("slabs", up_rows, vector_rows)]
    )
    up_one = up_one[0]
    vector_wide = vector_slabs.reshape(place.dp_count, vector_rows, vector_parts, -1)
    vector_wide = vector_wide.transpose(2, 1, 0, 3).reshape(vector_rows * vector_parts, width)
    vector_wide = vector_wide[: vectors.shape[0]].astype(jnp.float32)

    rows_in = ordered_clip(place, rows_low).astype(jnp.float32)
    row_count = rows_in.shape[0]
    z_here = place.index["z"]
    facts = jnp.where(z_here // micro == place.index["core"], own_facts, other_facts)
    facts = lax.dynamic_index_in_dim(facts, lax.rem(z_here, micro), 1, keepdims=False)
    valid_flag = (facts[0] > 0).astype(jnp.float32)
    first_row = place.index["seq"] * row_count
    live = ((first_row + jnp.arange(row_count)) < facts[1]).astype(jnp.float32)[:, None]
    meta = jnp.stack([place.index["seq"] * (row_count // LANES), facts[1]]).astype(jnp.int32)
    pick_rows = (rel_rows[:, None] == jnp.arange(OFFSETS)[None, :]).astype(jnp.bfloat16)
    table = wide_table(matmul(pick_rows, distance).astype(jnp.bfloat16))

    one_hidden, one_kept = feed_up(
        rows_in,
        up_one,
        vector_wide[2 : 2 + ratio_rows].reshape(FF),
        vector_wide[0],
        vector_wide[1],
    )
    (down_one, attend_mix, point_mix, second_down, one_hidden, one_kept, up_one, table) = fence(
        down_one, attend_mix, point_mix, second_down, one_hidden, one_kept, up_one, table
    )
    down_one = gather_core(place, down_one)
    attend_mix = gather_b(place, attend_mix)
    point_mix = gather_a(place, point_mix)
    down_two = gather_t(place, second_down)
    (down_one,) = assemble(place, down_one, [("columns",)])
    after_one = rows_in + 0.5 * (matmul(one_hidden, down_one) + vector_wide[2 + ratio_rows])
    attend_normed, attend_normal, attend_inverse = norm_rows(
        after_one, vector_wide[attend_base], vector_wide[attend_base + 1]
    )
    attend_normed = attend_normed.astype(jnp.bfloat16)
    (attend_mix, point_mix, up_two, after_one, attend_normed, attend_normal, attend_inverse) = fence(
        attend_mix, point_mix, up_two, after_one, attend_normed, attend_normal, attend_inverse
    )
    attend_mix = gather_core(place, attend_mix)
    point_mix = gather_b(place, point_mix)
    up_two = gather_a(place, up_two)
    attend_mix, attend_back_weight = assemble(place, attend_mix, [("rows", 0, 3, up_rows), ("packed", 3)])
    queries = (matmul(attend_normed, attend_mix[0]) + vector_wide[attend_base + 2]).astype(jnp.bfloat16)
    queries = (queries.astype(jnp.float32) * scale).astype(jnp.bfloat16)
    own_keys = matmul(attend_normed, attend_mix[1]).astype(jnp.bfloat16)
    own_values = (matmul(attend_normed, attend_mix[2]) + vector_wide[attend_base + 3]).astype(jnp.bfloat16)
    key_rows, value_rows = all_rows(place, own_keys), all_rows(place, own_values)
    (point_mix, up_two, down_two, cotangent, queries, key_rows, value_rows) = fence(
        point_mix, up_two, down_two, cotangent, queries, key_rows, value_rows
    )
    point_mix = gather_core(place, point_mix)
    up_two = gather_b(place, up_two)
    down_two = gather_a(place, down_two)
    cot_low = to_clip(place, cotangent)
    context, levels = attend(meta, queries, key_rows, value_rows, table)
    (point_mix, up_two, down_two, context, levels, after_one) = fence(
        point_mix, up_two, down_two, context, levels, after_one
    )
    down_two = gather_b(place, down_two)
    up_two = gather_core(place, up_two)
    point_mix, point_back = assemble(place, point_mix, [("rows", 0, 2, up_rows), ("packed", 2)])
    after_two = after_one + matmul(context, attend_back_weight) + vector_wide[attend_base + 4]
    conv_normed, conv_normal, conv_inverse = norm_rows(
        after_two, vector_wide[conv_base], vector_wide[conv_base + 1]
    )
    conv_normed = conv_normed.astype(jnp.bfloat16)
    linear = matmul(conv_normed, point_mix[0])
    logistic = sigmoid(matmul(conv_normed, point_mix[1]))
    gated = linear * logistic * live
    taps = vector_wide[taps_base : taps_base + KERNEL]
    before = neighbour_rows(place, gated[-HALO:], 1)
    deep_gain, deep_shift = vector_wide[conv_base + 2], vector_wide[conv_base + 3]
    depth_out, activated = convolve(before, gated, taps, deep_gain, deep_shift)
    after_three = after_two + matmul(activated, point_back)
    (up_two, down_two, cot_low, after_three, depth_out, activated) = fence(
        up_two, down_two, cot_low, after_three, depth_out, activated
    )
    down_two = gather_core(place, down_two)
    (up_two,) = assemble(place, up_two, [("rows", 0, 1, up_rows)])
    up_two = up_two[0]
    two_hidden, two_kept = feed_up(
        after_three,
        up_two,
        vector_wide[second_base + 2 : second_base + 2 + ratio_rows].reshape(FF),
        vector_wide[second_base],
        vector_wide[second_base + 1],
    )
    (down_two, two_hidden, two_kept, up_two) = fence(down_two, two_hidden, two_kept, up_two)
    (down_two,) = assemble(place, down_two, [("columns",)])
    two_out = matmul(two_hidden, down_two) + vector_wide[second_base + 2 + ratio_rows]
    after_four = after_three + 0.5 * two_out
    final_rows, final_normal, final_inverse = norm_rows(
        after_four, vector_wide[final_base], vector_wide[final_base + 1]
    )
    row_out = jnp.where(valid_flag > 0, final_rows, rows_in).astype(jnp.bfloat16)
    rows_cot = ordered_clip(place, cot_low).astype(jnp.float32)
    grad_four, final_gain_grad, final_shift_grad = norm_back(
        rows_cot * valid_flag, final_normal, final_inverse, vector_wide[final_base]
    )
    grad_low, grad_upper, two_up_bias, two_down_bias = feed_back_down(
        0.5 * grad_four, two_kept, down_two
    )
    sum_down_two = reduce_core(place, [(sent(grad_low), two_hidden)])
    (sum_down_two, grad_four, grad_upper, row_out) = fence(sum_down_two, grad_four, grad_upper, row_out)
    sum_down_two = reduce_b(place, sum_down_two)
    frames_out = from_clip(place, row_out, micro)
    sum_up_two = reduce_core(place, [(sent(two_kept[2]), grad_upper)])
    grad_normed = dot_f32(grad_upper, up_two, NT)
    grad_two_in, two_gain, two_shift = norm_back(
        grad_normed, two_kept[0], two_kept[1], vector_wide[second_base]
    )
    grad_three = grad_four + grad_two_in
    conv_low = grad_three.astype(jnp.bfloat16)
    deep_norm, deep_normal, deep_inverse = norm_rows(depth_out, deep_gain, deep_shift)
    grad_deep = dot_f32(conv_low, point_back, NT) * swish_slope(deep_norm, sigmoid(deep_norm))
    grad_depth, deep_gain_grad, deep_shift_grad = norm_back(
        grad_deep, deep_normal, deep_inverse, deep_gain
    )
    after = neighbour_rows(place, grad_depth[:HALO], -1)
    (sum_down_two, sum_up_two, grad_three, conv_low, grad_depth, after, frames_out) = fence(
        sum_down_two, sum_up_two, grad_three, conv_low, grad_depth, after, frames_out
    )
    sum_down_two = reduce_a(place, sum_down_two)
    sum_up_two = reduce_b(place, sum_up_two)
    grad_pair, tap_grads = convolve_back(
        meta, grad_depth, after, before, gated, taps, linear, logistic
    )
    (sum_down_two, sum_up_two, grad_pair) = fence(sum_down_two, sum_up_two, grad_pair)
    sum_down_two = reduce_t(place, [(1, sum_down_two[0])])
    sum_up_two = reduce_a(place, sum_up_two)
    sum_point = reduce_core(
        place,
        [
            (sent(conv_normed), grad_pair),
            (sent(conv_low), activated),
        ],
    )
    grad_conv_normed = dot_f32(grad_pair[:, :width], point_mix[0], NT)
    grad_conv_normed = grad_conv_normed + dot_f32(grad_pair[:, width:], point_mix[1], NT)
    grad_conv_in, conv_gain_grad, conv_shift_grad = norm_back(
        grad_conv_normed, conv_normal, conv_inverse, vector_wide[conv_base]
    )
    grad_two = grad_three + grad_conv_in
    attend_low = grad_two.astype(jnp.bfloat16)
    grad_context = dot_f32(attend_low, attend_back_weight, NT).astype(jnp.bfloat16)
    (sum_up_two, sum_point, grad_two, attend_low, grad_context) = fence(
        sum_up_two, sum_point, grad_two, attend_low, grad_context
    )
    sum_up_two = reduce_t(place, [(1, sum_up_two[0])])
    sum_point = reduce_b(place, sum_point)
    grad_queries, part_keys, part_values, grad_table = attend_back(
        meta, queries, key_rows, value_rows, table, grad_context, context, levels
    )
    (sum_point, grad_queries, part_keys, part_values, grad_table) = fence(
        sum_point, grad_queries, part_keys, part_values, grad_table
    )
    sum_point = reduce_a(place, sum_point)
    grad_keys = own_sum(place, part_keys).astype(jnp.bfloat16)
    grad_values = own_sum(place, part_values).astype(jnp.bfloat16)
    sum_distance = jnp.dot(
        pick_rows.astype(jnp.float32).T, table_grad(grad_table), precision=lax.Precision.HIGHEST
    )
    sum_distance = sum(
        (place.turn(sum_distance, "t", step) for step in place.steps("t")), sum_distance
    )
    sum_attend = reduce_core(
        place,
        [
            (
                sent(attend_normed),
                jnp.concatenate([grad_queries, grad_keys, grad_values], axis=1),
            ),
            (sent(attend_low), context),
        ],
    )
    grad_attend_normed = (
        dot_f32(grad_queries, attend_mix[0], NT)
        + dot_f32(grad_keys, attend_mix[1], NT)
        + dot_f32(grad_values, attend_mix[2], NT)
    )
    grad_attend_in, attend_gain_grad, attend_shift_grad = norm_back(
        grad_attend_normed, attend_normal, attend_inverse, vector_wide[attend_base]
    )
    grad_one = grad_two + grad_attend_in
    (sum_point, sum_attend, sum_distance, grad_one) = fence(sum_point, sum_attend, sum_distance, grad_one)
    sum_point = reduce_t(place, [(2, sum_point[0]), (1, sum_point[1])])
    sum_attend = reduce_b(place, sum_attend)
    sum_distance = sum_distance + place.turn(sum_distance, "core", 1)
    grad_low, grad_upper, one_up_bias, one_down_bias = feed_back_down(0.5 * grad_one, one_kept, down_one)
    sum_down_one = reduce_core(place, [(sent(grad_low), one_hidden)])
    sum_up_one = reduce_core(place, [(sent(one_kept[2]), grad_upper)])
    (sum_attend, sum_down_one, sum_up_one, grad_upper) = fence(
        sum_attend, sum_down_one, sum_up_one, grad_upper
    )
    sum_down_one = reduce_b(place, sum_down_one)
    sum_attend = reduce_a(place, sum_attend)
    sum_up_one = reduce_b(place, sum_up_one)
    sum_distance = sum(
        (place.turn(sum_distance, "b", step) for step in place.steps("b")), sum_distance
    )
    grad_normed = dot_f32(grad_upper, up_one, NT)
    grad_one_in, one_gain, one_shift = norm_back(grad_normed, one_kept[0], one_kept[1], vector_wide[0])
    grad_rows = grad_one + grad_one_in + (1.0 - valid_flag) * rows_cot

    def column_sum(rows):
        return jnp.sum(rows.astype(jnp.float32), axis=0)

    vector_part = jnp.concatenate(
        [
            jnp.stack([one_gain, one_shift]),
            one_up_bias.reshape(ratio_rows, width),
            jnp.stack(
                [
                    one_down_bias,
                    attend_gain_grad,
                    attend_shift_grad,
                    column_sum(grad_queries),
                    column_sum(grad_values),
                    column_sum(attend_low),
                    conv_gain_grad,
                    conv_shift_grad,
                    deep_gain_grad,
                    deep_shift_grad,
                    two_gain,
                    two_shift,
                ]
            ),
            two_up_bias.reshape(ratio_rows, width),
            jnp.stack([two_down_bias, final_gain_grad, final_shift_grad]),
            tap_grads[:KERNEL],
        ],
        axis=0,
    )
    grad_rows = grad_rows.astype(jnp.bfloat16)
    vector_part = jnp.dot(vector_part, order.astype(jnp.float32), precision=lax.Precision.HIGHEST)
    (sum_attend, sum_down_one, sum_up_one, vector_part, grad_rows) = fence(
        sum_attend, sum_down_one, sum_up_one, vector_part, grad_rows
    )
    sum_up_one = reduce_a(place, sum_up_one)
    sum_down_one = reduce_a(place, sum_down_one)
    sum_vectors = reduce_vectors_core(place, vector_part)
    sum_attend = reduce_t(place, [(3, sum_attend[0]), (1, sum_attend[1])])
    sum_distance = sum(
        (place.turn(sum_distance, "a", step) for step in place.steps("a")), sum_distance
    )
    frames_grad = from_clip(place, grad_rows, micro)
    (sum_up_one, sum_down_one, sum_vectors) = fence(sum_up_one, sum_down_one, sum_vectors)
    sum_up_one = reduce_t(place, [(1, sum_up_one[0])])
    sum_vectors = reduce_vectors(place, sum_vectors, "b")
    sum_vectors = reduce_vectors(place, sum_vectors, "a")
    sum_down_one, grad_vectors = reduce_t_vectors(place, sum_down_one[0], sum_vectors)
    wide = jnp.float32
    return (
        own_clips(place, frames_out),
        own_clips(place, frames_grad),
        sum_up_one[0].astype(wide),
        sum_down_one.T.astype(wide),
        sum_attend[:3].astype(wide),
        sum_attend[3].T.astype(wide),
        sum_point[:2].astype(wide),
        sum_point[2].T.astype(wide),
        sum_up_two[0].astype(wide),
        sum_down_two[0].T.astype(wide),
        grad_vectors,
        sum_distance,
    )


def solution(mesh):
    dp_count, tensor_count = mesh.shape["dp"], mesh.shape["tensor"]

    def program(*arrays):
        group = 2 * (arrays[0].shape[0] // dp_count)
        parted = Mesh(
            mesh.devices.reshape(dp_count // 4, 2, 2, tensor_count // group, group),
            ("y", "x", "core", "far", "z"),
        )
        dp, tensor = ("y", "x", "core"), TENSOR
        return jax.shard_map(
            body,
            mesh=parted,
            in_specs=(
                P(dp, tensor, None),
                P(dp, tensor, None),
                P(dp),
                P(dp),
                P(),
                P(dp, tensor),
                P(tensor, dp),
                P(None, dp, tensor),
                P(tensor, dp),
                P(None, dp, tensor),
                P(tensor, dp),
                P(dp, tensor),
                P(tensor, dp),
                P(None, dp),
                P(),
            ),
            out_specs=(
                P(dp, tensor, None),
                P(dp, tensor, None),
                P(dp, tensor),
                P(tensor, dp),
                P(None, dp, tensor),
                P(tensor, dp),
                P(None, dp, tensor),
                P(tensor, dp),
                P(dp, tensor),
                P(tensor, dp),
                P(None, dp + tensor),
                P(),
            ),
            check_vma=False,
        )(*arrays)

    return program
```

```python
import functools

import jax
import jax.numpy as jnp
from jax import lax
from jax.experimental import pallas as pl
from jax.experimental.pallas import tpu as pltpu
from jax.sharding import Mesh
from jax.sharding import PartitionSpec as P

HEADS = 16
HEAD_DIM = 64
FF = 4096
KERNEL = 31
LEFT = 64
OFFSETS = 73
EPSILON = 1e-05

LANES = 128
SOFT_ROWS = 32
SLOPE_ROWS = 16
RIGHT = OFFSETS - 1 - LEFT
NT = (((1,), (1,)), ((), ()))
NN = (((1,), (0,)), ((), ()))
TN = (((0,), (0,)), ((), ()))


def dot_f32(left_side, right_side, dims):
    return lax.dot_general(left_side, right_side, dims, preferred_element_type=jnp.float32)


def band_distance():
    shape = (LANES, 3 * LANES)
    return (
        lax.broadcasted_iota(jnp.int32, shape, 1)
        - LANES
        - lax.broadcasted_iota(jnp.int32, shape, 0)
    )


LAST_ROWS = 8


def add_band(score_ref, half, source, distance, block, number):
    rows = slice(number * LANES, (number + 1) * LANES)
    own = source[rows]
    left_col = own[:, 2 * LANES - LEFT : 2 * LANES - LEFT + 1]
    right_col = own[:, RIGHT : RIGHT + 1]
    rolled = pltpu.roll(own - right_col, LANES, 1, stride=1, stride_axis=0)
    window = pl.multiple_of(block * LANES, LANES)
    near = rolled[:LEFT, :LANES] + (right_col - left_col)[:LEFT]
    near = jnp.where(distance[:LEFT, :LANES] > -LEFT, near, 0.0)
    score_ref[half, number * LANES : number * LANES + LEFT, pl.ds(window, LANES)] += near
    score_ref[half, rows, pl.ds(window + LANES, LANES)] += rolled[:, LANES:]
    last = LANES - LAST_ROWS
    after = jnp.where(distance[last:, 2 * LANES :] < RIGHT, rolled[last:, :LANES], 0.0)
    score_ref[half, number * LANES + last : (number + 1) * LANES, pl.ds(window + 2 * LANES, LANES)] += after


def in_half(shape, half):
    lanes = lax.broadcasted_iota(jnp.int32, shape, 1)
    return (lanes < HEAD_DIM) if half == 0 else (lanes >= HEAD_DIM)


def spare_lane(shape):
    return lax.rem(lax.broadcasted_iota(jnp.int32, shape, 1), HEAD_DIM)


def key_marks(meta_ref, key_count, blocks):
    shape = (key_count, LANES)
    spare, keys = spare_lane(shape), lax.broadcasted_iota(jnp.int32, shape, 0)
    before = keys < (meta_ref[0] + spare // 2) * LANES
    side = jnp.where(lax.rem(spare, 2) == 0, before.astype(jnp.float32), 1.0 - before.astype(jnp.float32))
    dead = jnp.where(keys < meta_ref[1], 0.0, -1e30)
    ones = (spare < 2 * blocks + 4).astype(jnp.float32)
    marks = jnp.where(spare < 2 * blocks, side, jnp.where(spare == 2 * blocks, dead, ones))
    return marks.astype(jnp.bfloat16)


def in_parts(column):
    parts = []
    for _ in range(3):
        part = column.astype(jnp.bfloat16).astype(jnp.float32)
        parts.append(part)
        column = column - part
    return parts


def with_marks(rows_half, half, columns_of):
    square = (LANES, LANES)
    spare, mine = spare_lane(square), in_half(square, half)
    parts = []
    for number in range(rows_half.shape[0] // LANES):
        own = rows_half[number * LANES : (number + 1) * LANES].astype(jnp.float32)
        marks = jnp.zeros(square, jnp.float32)
        for place, column in columns_of(number):
            marks = jnp.where(spare == place, column, marks)
        parts.append(jnp.where(mine, own, marks).astype(jnp.bfloat16))
    return jnp.concatenate(parts, axis=0)


def marked_queries(q_half, half, source, extra, blocks):
    def columns_of(number):
        rows = slice(number * LANES, (number + 1) * LANES)
        own = source[rows]
        columns = [
            (2 * number, own[:, 2 * LANES - LEFT : 2 * LANES - LEFT + 1]),
            (2 * number + 1, own[:, RIGHT : RIGHT + 1]),
            (2 * blocks, 1.0),
        ]
        return columns + [(2 * blocks + 1 + place, part[rows]) for place, part in enumerate(extra)]

    return with_marks(q_half, half, columns_of)


def key_spot(meta_ref, step, count, row_count):
    spot = lax.rem(meta_ref[2] - step + count, count)
    return pl.ds(pl.multiple_of(spot * row_count, row_count), row_count)


def attend_kernel(count, meta_ref, q_ref, e_ref, *refs):
    key_refs, value_refs = refs[:count], refs[count : 2 * count]
    c_ref, lse_ref, score_ref, share_ref, marks_ref, k_ref, v_ref = refs[2 * count :]
    row_count, key_count = q_ref.shape[0], k_ref.shape[0]
    for step in range(count):
        k_ref[key_spot(meta_ref, step, count, row_count)] = key_refs[step][...]
        v_ref[key_spot(meta_ref, step, count, row_count)] = value_refs[step][...]
    blocks = row_count // LANES
    pair = pl.program_id(0)
    lanes = lax.broadcasted_iota(jnp.int32, (row_count, LANES), 1)
    distance = band_distance()

    @pl.when(pair == 0)
    def _():
        marks_ref[...] = key_marks(meta_ref, key_count, blocks)

    sources = []
    for half in range(2):
        mine = in_half((row_count, LANES), half)
        q_half = jnp.where(mine, q_ref[...], 0)
        source = dot_f32(q_half, e_ref[...], NT).astype(jnp.bfloat16).astype(jnp.float32)
        sources.append(source)
        queries = marked_queries(q_half, half, source, [], blocks)
        keys = jnp.where(in_half((key_count, LANES), half), k_ref[...], marks_ref[...])
        score_ref[half, :, LANES : LANES + key_count] = dot_f32(queries, keys, NT)
    result = None
    for half in range(2):
        inverses = []
        for number in range(blocks):
            rows = slice(number * LANES, (number + 1) * LANES)
            add_band(score_ref, half, sources[half], distance, meta_ref[0] + number, number)
            for first in range(number * LANES, (number + 1) * LANES, SOFT_ROWS):
                few = slice(first, first + SOFT_ROWS)
                scores = score_ref[half, few, LANES : LANES + key_count]
                peak = jnp.max(scores, axis=1, keepdims=True)
                grown = jnp.exp(scores - peak)
                total = jnp.sum(grown, axis=1, keepdims=True)
                share_ref[half, few] = grown.astype(jnp.bfloat16)
                inverses.append(1.0 / total)
                lse_ref[few] = jnp.where(
                    lanes[few] == 2 * pair + half, peak + jnp.log(total), lse_ref[few]
                )
        context = dot_f32(share_ref[half], v_ref[...], NN) * jnp.concatenate(inverses, axis=0)
        result = context if half == 0 else jnp.where(in_half(context.shape, 1), context, result)
    c_ref[...] = result.astype(jnp.bfloat16)


def attend_back_kernel(count, meta_ref, q_ref, e_ref, dc_ref, c_ref, lse_ref, *refs):
    key_refs, value_refs = refs[:count], refs[count : 2 * count]
    dq_ref, de_ref = refs[2 * count : 2 * count + 2]
    dk_refs, dv_refs = refs[2 * count + 2 : 3 * count + 2], refs[3 * count + 2 : 4 * count + 2]
    score_ref, grad_ref, share_ref, slope_ref, source_ref, wide_ref, marks_ref, k_ref, v_ref, turn_ref = refs[
        4 * count + 2 :
    ]
    row_count, key_count = q_ref.shape[0], k_ref.shape[0]
    for step in range(count):
        k_ref[key_spot(meta_ref, step, count, row_count)] = key_refs[step][...]
        v_ref[key_spot(meta_ref, step, count, row_count)] = value_refs[step][...]
    key_blocks, blocks = key_count // LANES, row_count // LANES
    pair = pl.program_id(0)
    lanes = lax.broadcasted_iota(jnp.int32, (row_count, LANES), 1)
    distance = band_distance()
    square = (LANES, LANES)
    flip = (
        lax.broadcasted_iota(jnp.int32, square, 0) + lax.broadcasted_iota(jnp.int32, square, 1)
        == LANES - 1
    ).astype(jnp.float32).astype(jnp.bfloat16)
    spots = lax.broadcasted_iota(jnp.int32, square, 1)

    @pl.when(pair == 0)
    def _():
        shape = (key_count, LANES)
        place = lax.broadcasted_iota(jnp.int32, shape, 1)
        edge = (meta_ref[0] + place // 2) * LANES
        key = lax.broadcasted_iota(jnp.int32, shape, 0)
        before = (key < edge).astype(jnp.float32)
        after = (key >= edge + LANES).astype(jnp.float32)
        wide_ref[:, LANES:] = jnp.where(lax.rem(place, 2) == 0, before, after).astype(jnp.bfloat16)
        for half in range(2):
            slope_ref[half, :, :LANES] = jnp.zeros((row_count, LANES), jnp.bfloat16)
            slope_ref[half, :, LANES + key_count :] = jnp.zeros((row_count, LANES), jnp.bfloat16)
        de_ref[...] = jnp.zeros(de_ref.shape, jnp.float32)
        marks_ref[0] = key_marks(meta_ref, key_count, blocks)
        marks_ref[1] = (spare_lane(shape) < 3).astype(jnp.float32).astype(jnp.bfloat16)

    wide_ref[:, :LANES] = k_ref[...]
    inner_all = dc_ref[...].astype(jnp.float32) * c_ref[...].astype(jnp.float32)
    sources, q_halves, dc_halves = [], [], []
    for half in range(2):
        mine, mine_keys = in_half((row_count, LANES), half), in_half((key_count, LANES), half)
        q_half = jnp.where(mine, q_ref[...], 0)
        dc_half = jnp.where(mine, dc_ref[...], 0)
        source = dot_f32(q_half, e_ref[...], NT).astype(jnp.bfloat16).astype(jnp.float32)
        inner = jnp.sum(jnp.where(mine, inner_all, 0.0), axis=1, keepdims=True)
        level = jnp.sum(
            jnp.where(lanes == 2 * pair + half, lse_ref[...], 0.0), axis=1, keepdims=True
        )
        queries = marked_queries(q_half, half, source, in_parts(-level), blocks)
        keys = jnp.where(mine_keys, k_ref[...], marks_ref[0])
        score_ref[half, :, LANES : LANES + key_count] = dot_f32(queries, keys, NT)
        inner_parts = in_parts(-inner)
        grads = with_marks(
            dc_half,
            half,
            lambda number, parts=inner_parts: [
                (place, part[number * LANES : (number + 1) * LANES])
                for place, part in enumerate(parts)
            ],
        )
        values = jnp.where(mine_keys, v_ref[...], marks_ref[1])
        grad_ref[half] = dot_f32(grads, values, NT)
        sources.append(source)
        q_halves.append(q_half)
        dc_halves.append(dc_half)
    grad_q = grad_k = grad_v = None
    for half in range(2):
        for number in range(blocks):
            rows = slice(number * LANES, (number + 1) * LANES)
            add_band(score_ref, half, sources[half], distance, meta_ref[0] + number, number)
            for first in range(number * LANES, (number + 1) * LANES, SLOPE_ROWS):
                few = slice(first, first + SLOPE_ROWS)
                shares = jnp.exp(score_ref[half, few, LANES : LANES + key_count])
                share_ref[half, few] = shares.astype(jnp.bfloat16)
                slope_ref[half, few, LANES : LANES + key_count] = (
                    shares * grad_ref[half, few]
                ).astype(jnp.bfloat16)
    for half in range(2):
        mine = in_half((row_count, LANES), half)
        slopes = slope_ref[half, :, LANES : LANES + key_count]
        wide = dot_f32(slopes, wide_ref[...], NN)
        before = wide[:, LANES:]
        for number in range(blocks):
            rows = slice(number * LANES, (number + 1) * LANES)
            window = pl.multiple_of((meta_ref[0] + number) * LANES, LANES)
            first, last = number * LANES, (number + 1) * LANES - LAST_ROWS
            near = slope_ref[half, first : first + LEFT, pl.ds(window, LANES)].astype(jnp.float32)
            near = jnp.where(distance[:LEFT, :LANES] > -LEFT, near, 0.0)
            final = slope_ref[half, last - 8 : last + 8, pl.ds(window + 2 * LANES, LANES)]
            final = final.astype(jnp.float32)[8:]
            final = jnp.where(distance[LANES - LAST_ROWS :, 2 * LANES :] < RIGHT, final, 0.0)
            middle = slope_ref[half, rows, pl.ds(window + LANES, LANES)]
            gap = jnp.zeros((LANES - LEFT - LAST_ROWS, LANES), jnp.float32)
            edges = jnp.concatenate([near, gap, final], axis=0)
            inner_sum = jnp.sum(edges, axis=1, keepdims=True)
            first_rows = lax.broadcasted_iota(jnp.int32, (LANES, 1), 0) < LEFT
            far_left = before[rows, 2 * number : 2 * number + 1] - jnp.where(first_rows, inner_sum, 0.0)
            far_right = before[rows, 2 * number + 1 : 2 * number + 2] - jnp.where(
                first_rows, 0.0, inner_sum
            )
            band = jnp.concatenate([edges.astype(jnp.bfloat16), middle], axis=1)
            turned = dot_f32(flip, band, NN)
            turned = pltpu.roll(turned, 1, 1, stride=1, stride_axis=0)
            turned = dot_f32(flip, turned.astype(jnp.bfloat16), NN)
            turned = jnp.concatenate(
                [
                    turned[:, :LANES] + jnp.where(spots == RIGHT, far_right, 0.0),
                    turned[:, LANES:] + jnp.where(spots == 0, far_left, 0.0),
                ],
                axis=1,
            )
            source_ref[half, rows] = turned.astype(jnp.bfloat16)
        q_part = wide[:, :LANES] + dot_f32(source_ref[half], e_ref[...], NN)
        k_part = dot_f32(q_halves[half], slopes, TN)
        v_part = dot_f32(dc_halves[half], share_ref[half], TN)
        de_ref[...] += dot_f32(q_halves[half], source_ref[half], TN)
        grad_q = q_part if half == 0 else jnp.where(mine, q_part, grad_q)
        grad_k = k_part if half == 0 else grad_k + k_part
        grad_v = v_part if half == 0 else grad_v + v_part
    dq_ref[...] = (grad_q * HEAD_DIM ** (-0.5)).astype(jnp.bfloat16)
    for grad, grad_refs in ((grad_k, dk_refs), (grad_v, dv_refs)):
        turn_ref[...] = grad.T
        for step in range(count):
            rows = key_spot(meta_ref, -step, count, row_count)
            grad_refs[step][...] = turn_ref[rows].astype(jnp.bfloat16)


def pair_spec(row_count):
    return pl.BlockSpec((row_count, LANES), lambda pair, meta: (0, pair))


def fixed_spec(row_count, column_count):
    return pl.BlockSpec((row_count, column_count), lambda pair, meta: (0, 0))


def attend(meta, queries, key_rows, value_rows, table):
    row_count, width = queries.shape
    count = len(key_rows)
    key_count = row_count * count
    return pl.pallas_call(
        functools.partial(attend_kernel, count),
        grid_spec=pltpu.PrefetchScalarGridSpec(
            num_scalar_prefetch=1,
            grid=(width // LANES,),
            in_specs=[pair_spec(row_count), fixed_spec(2 * LANES, LANES)]
            + [pair_spec(row_count)] * (2 * count),
            out_specs=[pair_spec(row_count), fixed_spec(row_count, LANES)],
            scratch_shapes=[
                pltpu.VMEM((2, row_count, key_count + 2 * LANES), jnp.float32),
                pltpu.VMEM((2, row_count, key_count), jnp.bfloat16),
                pltpu.VMEM((key_count, LANES), jnp.bfloat16),
                pltpu.VMEM((key_count, LANES), jnp.bfloat16),
                pltpu.VMEM((key_count, LANES), jnp.bfloat16),
            ],
        ),
        out_shape=[
            jax.ShapeDtypeStruct((row_count, width), jnp.bfloat16),
            jax.ShapeDtypeStruct((row_count, LANES), jnp.float32),
        ],
        compiler_params=pltpu.CompilerParams(vmem_limit_bytes=48 * 2**20),
        name="attend",
    )(meta, queries, table, *key_rows, *value_rows)


def attend_back(meta, queries, key_rows, value_rows, table, grad_context, context, levels):
    row_count, width = queries.shape
    count = len(key_rows)
    key_count = row_count * count
    rows_out = jax.ShapeDtypeStruct((row_count, width), jnp.bfloat16)
    results = pl.pallas_call(
        functools.partial(attend_back_kernel, count),
        grid_spec=pltpu.PrefetchScalarGridSpec(
            num_scalar_prefetch=1,
            grid=(width // LANES,),
            in_specs=[
                pair_spec(row_count),
                fixed_spec(2 * LANES, LANES),
                pair_spec(row_count),
                pair_spec(row_count),
                fixed_spec(row_count, LANES),
            ]
            + [pair_spec(row_count)] * (2 * count),
            out_specs=[pair_spec(row_count), fixed_spec(LANES, 2 * LANES)]
            + [pair_spec(row_count)] * (2 * count),
            scratch_shapes=[
                pltpu.VMEM((2, row_count, key_count + 2 * LANES), jnp.float32),
                pltpu.VMEM((2, row_count, key_count), jnp.float32),
                pltpu.VMEM((2, row_count, key_count), jnp.bfloat16),
                pltpu.VMEM((2, row_count, key_count + 2 * LANES), jnp.bfloat16),
                pltpu.VMEM((2, row_count, 2 * LANES), jnp.bfloat16),
                pltpu.VMEM((key_count, 2 * LANES), jnp.bfloat16),
                pltpu.VMEM((2, key_count, LANES), jnp.bfloat16),
                pltpu.VMEM((key_count, LANES), jnp.bfloat16),
                pltpu.VMEM((key_count, LANES), jnp.bfloat16),
                pltpu.VMEM((key_count, LANES), jnp.float32),
            ],
        ),
        out_shape=[rows_out, jax.ShapeDtypeStruct((LANES, 2 * LANES), jnp.float32)]
        + [rows_out] * (2 * count),
        compiler_params=pltpu.CompilerParams(vmem_limit_bytes=48 * 2**20),
        name="attend_back",
    )(meta, queries, table, grad_context, context, levels, *key_rows, *value_rows)
    return results[0], results[2 : 2 + count], results[2 + count :], results[1]


def wide_table(table_low):
    places = jnp.arange(2 * LANES)
    offsets = jnp.clip(jnp.where(places < LANES, places, places - 2 * LANES) + LEFT, 0, OFFSETS - 1)
    rows = table_low[offsets]
    return jnp.concatenate([rows, rows], axis=1)


def table_grad(wide_grad):
    folded = (wide_grad[:HEAD_DIM] + wide_grad[HEAD_DIM:]).T
    first = jnp.sum(folded[LANES : 2 * LANES - LEFT + 1], axis=0, keepdims=True)
    last = jnp.sum(folded[RIGHT:LANES], axis=0, keepdims=True)
    return jnp.concatenate([first, folded[2 * LANES - LEFT + 1 :], folded[:RIGHT], last], axis=0)


def sigmoid(values):
    return 0.5 * jnp.tanh(0.5 * values) + 0.5


def swish_slope(values, logistic):
    return logistic + values * logistic * (1.0 - logistic)


def matmul(left_side, right_side):
    return dot_f32(left_side, right_side, NN)


def norm_rows(values, gain_row, shift_row):
    centred = values - jnp.mean(values, axis=-1, keepdims=True)
    variance = jnp.mean(centred * centred, axis=-1, keepdims=True)
    inverse = lax.rsqrt(variance + EPSILON)
    normal = centred * inverse
    return (normal * gain_row + shift_row, normal, inverse)


def norm_back(grad_out, normal, inverse, gain_row):
    grad_normal = grad_out * gain_row
    grad_in = inverse * (
        grad_normal
        - jnp.mean(grad_normal, axis=-1, keepdims=True)
        - normal * jnp.mean(grad_normal * normal, axis=-1, keepdims=True)
    )
    return (grad_in, jnp.sum(grad_out * normal, axis=0), jnp.sum(grad_out, axis=0))


CHUNK = 64
HALO = 32


def tap_slices(window, offsets):
    length = window.shape[0]
    slices = {}
    for rest in range(8):
        wanted = [offset for offset in offsets if offset % 8 == rest]
        if wanted:
            turned = pltpu.roll(window, length - rest, 0) if rest else window
            for offset in wanted:
                slices[offset] = turned[offset - rest : offset - rest + CHUNK]
    return slices


def convolve_kernel(before_ref, gated_ref, taps_ref, gain_ref, shift_ref, deep_ref, low_ref, padded_ref):
    row_count, width = gated_ref.shape
    lead = HALO - (KERNEL - 1)
    padded_ref[:HALO] = before_ref[...]
    padded_ref[HALO:] = gated_ref[...]

    @pl.loop(0, width // LANES)
    def _(column):
        lanes = pl.ds(pl.multiple_of(column * LANES, LANES), LANES)
        taps = [taps_ref[tap : tap + 1, lanes] for tap in range(KERNEL)]

        @pl.loop(0, row_count // CHUNK)
        def _(chunk):
            first = pl.multiple_of(chunk * CHUNK, CHUNK)
            window = padded_ref[pl.ds(first, CHUNK + HALO), lanes]
            slices = tap_slices(window, [tap + lead for tap in range(KERNEL)])
            total = taps[0] * slices[lead]
            for tap in range(1, KERNEL):
                total = total + taps[tap] * slices[tap + lead]
            deep_ref[pl.ds(first, CHUNK), lanes] = total

    @pl.loop(0, row_count // CHUNK)
    def _(chunk):
        rows = pl.ds(pl.multiple_of(chunk * CHUNK, CHUNK), CHUNK)
        deep_norm, _, _ = norm_rows(deep_ref[rows, :], gain_ref[...], shift_ref[...])
        low_ref[rows, :] = (deep_norm * sigmoid(deep_norm)).astype(jnp.bfloat16)


def convolve(before, gated, taps, gain_row, shift_row):
    shape = gated.shape
    return pl.pallas_call(
        convolve_kernel,
        in_specs=[pl.BlockSpec(memory_space=pltpu.VMEM)] * 5,
        out_specs=[pl.BlockSpec(memory_space=pltpu.VMEM)] * 2,
        out_shape=[
            jax.ShapeDtypeStruct(shape, jnp.float32),
            jax.ShapeDtypeStruct(shape, jnp.bfloat16),
        ],
        scratch_shapes=[pltpu.VMEM((shape[0] + HALO, shape[1]), jnp.float32)],
        compiler_params=pltpu.CompilerParams(vmem_limit_bytes=32 * 2**20),
        name="convolve",
    )(before, gated, taps, gain_row[None], shift_row[None])


def convolve_back_kernel(
    meta_ref, grad_ref, after_ref, before_ref, gated_ref, taps_ref, linear_ref, logistic_ref,
    pair_ref, tap_grad_ref, padded_ref, extended_ref,
):
    row_count, width = gated_ref.shape
    lead = HALO - (KERNEL - 1)
    padded_ref[:HALO] = before_ref[...]
    padded_ref[HALO:] = gated_ref[...]
    extended_ref[:row_count] = grad_ref[...]
    extended_ref[row_count:] = after_ref[...]
    live_rows = meta_ref[1] - meta_ref[0] * LANES

    @pl.loop(0, width // LANES)
    def _(column):
        start = pl.multiple_of(column * LANES, LANES)
        lanes = pl.ds(start, LANES)
        taps = [taps_ref[tap : tap + 1, lanes] for tap in range(KERNEL)]

        @pl.loop(0, row_count // CHUNK)
        def _(chunk):
            first = pl.multiple_of(chunk * CHUNK, CHUNK)
            rows = pl.ds(first, CHUNK)
            window = extended_ref[pl.ds(first, CHUNK + HALO), lanes]
            slices = tap_slices(window, [KERNEL - 1 - tap for tap in range(KERNEL)])
            total = taps[0] * slices[KERNEL - 1]
            for tap in range(1, KERNEL):
                total = total + taps[tap] * slices[KERNEL - 1 - tap]
            places = first + lax.broadcasted_iota(jnp.int32, (CHUNK, LANES), 0)
            logistic = logistic_ref[rows, lanes]
            grad_linear = jnp.where(places < live_rows, total, 0.0) * logistic
            pair_ref[rows, lanes] = grad_linear.astype(jnp.bfloat16)
            grad_gate = grad_linear * linear_ref[rows, lanes] * (1.0 - logistic)
            gate_lanes = pl.ds(pl.multiple_of(width + start, LANES), LANES)
            pair_ref[rows, gate_lanes] = grad_gate.astype(jnp.bfloat16)

        def tap_step(chunk, totals):
            first = pl.multiple_of(chunk * CHUNK, CHUNK)
            window = padded_ref[pl.ds(first, CHUNK + HALO), lanes]
            slices = tap_slices(window, [tap + lead for tap in range(KERNEL)])
            grad = extended_ref[pl.ds(first, CHUNK), lanes]
            added_up = []
            for tap in range(KERNEL):
                product = slices[tap + lead] * grad
                part = product[:8]
                for piece in range(1, CHUNK // 8):
                    part = part + product[8 * piece : 8 * piece + 8]
                added_up.append(totals[tap] + part)
            return tuple(added_up)

        zero = jnp.zeros((8, LANES), jnp.float32)
        totals = lax.fori_loop(0, row_count // CHUNK, tap_step, (zero,) * KERNEL)
        for tap in range(KERNEL):
            tap_grad_ref[tap : tap + 1, lanes] = jnp.sum(totals[tap], axis=0, keepdims=True)


def convolve_back(meta, grad_depth, after, before, gated, taps, linear, logistic):
    row_count, width = gated.shape
    vmem = pl.BlockSpec(memory_space=pltpu.VMEM)
    return pl.pallas_call(
        convolve_back_kernel,
        grid_spec=pltpu.PrefetchScalarGridSpec(
            num_scalar_prefetch=1,
            grid=(),
            in_specs=[vmem] * 7,
            out_specs=[vmem] * 2,
            scratch_shapes=[pltpu.VMEM((row_count + HALO, width), jnp.float32)] * 2,
        ),
        out_shape=[
            jax.ShapeDtypeStruct((row_count, 2 * width), jnp.bfloat16),
            jax.ShapeDtypeStruct(taps.shape, jnp.float32),
        ],
        compiler_params=pltpu.CompilerParams(vmem_limit_bytes=40 * 2**20),
        name="convolve_back",
    )(meta, grad_depth, after, before, gated, taps, linear, logistic)


def fence(*values):
    return lax.optimization_barrier(values)


TENSOR = ("far", "z")


class Place:
    def __init__(self):
        axes = ("y", "x", "core", "far", "z")
        self.count = {axis: lax.axis_size(axis) for axis in axes}
        self.index = {axis: lax.axis_index(axis) for axis in axes}
        count, index = self.count, self.index
        count["t"] = count["far"] * count["z"]
        index["t"] = index["far"] * count["z"] + index["z"]
        count["seq"] = count["far"] * 2
        index["seq"] = index["far"] * 2 + index["core"]
        count["a"], count["b"] = count["x"], count["y"]
        self.mixed = count["x"] == count["y"]
        self.names = {"t": TENSOR, "seq": ("core", "far")}
        self.dp_count = count["y"] * count["x"] * 2

    def seq_pair(self, start, end):
        far = self.count["far"]
        return ((start % 2) * far + start // 2, (end % 2) * far + end // 2)

    def turn(self, block, axis, step):
        size = self.count[axis]
        pairs = [(start, (start + step) % size) for start in range(size)]
        if axis == "seq":
            pairs = [self.seq_pair(*pair) for pair in pairs]
        if axis in ("a", "b"):
            y_count, x_count = self.count["y"], self.count["x"]
            pairs = []
            for y in range(y_count):
                for x in range(x_count):
                    for core in range(2):
                        along_x = (axis == "a") != (self.mixed and core == 1)
                        new_y = y if along_x else (y + step) % y_count
                        new_x = (x + step) % x_count if along_x else x
                        pairs.append(
                            ((y * x_count + x) * 2 + core, (new_y * x_count + new_x) * 2 + core)
                        )
            return lax.ppermute(block, ("y", "x", "core"), pairs)
        return lax.ppermute(block, self.names.get(axis, axis), pairs)

    def after(self, axis, step):
        return lax.rem(self.index[axis] + step, self.count[axis])

    def blocks_for(self, core):
        y_count, x_count = self.count["y"], self.count["x"]
        numbers = []
        for b_step in [*self.steps("b"), 0]:
            for a_step in [*self.steps("a"), 0]:
                y = lax.rem(self.index["y"] + b_step, y_count)
                x = lax.rem(self.index["x"] + a_step, x_count)
                if self.mixed:
                    y = jnp.where(core == 1, lax.rem(self.index["y"] + a_step, y_count), y)
                    x = jnp.where(core == 1, lax.rem(self.index["x"] + b_step, x_count), x)
                numbers.append((y * x_count + x) * 2 + core)
        return numbers

    def steps(self, axis):
        return range(1, self.count[axis])


def packed(shard):
    rows, columns = shard.shape
    blocks = shard.reshape(rows // columns, columns, columns)
    return blocks.transpose(1, 0, 2).reshape(columns, rows)


def gather_t(place, shard):
    return lax.all_gather(shard, TENSOR, axis=0)


def gather_a(place, stack):
    return jnp.concatenate([stack] + [place.turn(stack, "a", step) for step in place.steps("a")])


def gather_b(place, stack):
    return [stack] + [place.turn(stack, "b", step) for step in place.steps("b")]


def gather_core(place, stacks):
    return stacks + [place.turn(stack, "core", 1) for stack in stacks]


def assemble(place, stacks, targets):
    counts, dp_count, t_count = place.count, place.dp_count, place.count["t"]
    dtype = stacks[0].dtype
    shard_shape = stacks[0].shape[1:]
    rows, columns = shard_shape[-2:]
    shapes, copy_counts = [], 0
    for target in targets:
        if target[0] == "rows":
            shapes.append((target[2], target[3] * dp_count, columns * t_count))
            copy_counts += dp_count * t_count
        elif target[0] == "columns":
            aligned = columns % LANES == 0
            shape = (rows * t_count, columns * dp_count)
            shapes.append(shape if aligned else (dp_count, rows * t_count, columns))
            copy_counts += dp_count * t_count
        elif target[0] == "packed":
            aligned = rows % LANES == 0
            shape = (columns * t_count, rows * dp_count)
            shapes.append(shape if aligned else (dp_count, t_count, rows, columns))
            copy_counts += dp_count * t_count * (columns // rows if aligned else 1)
        else:
            shapes.append((dp_count, target[2], columns))
            copy_counts += dp_count

    def kernel(meta_ref, *refs):
        stack_refs = refs[: len(stacks)]
        out_refs = refs[len(stacks) : len(stacks) + len(targets)]
        sem = refs[-1]
        copies = []

        def send(source, target):
            copy = pltpu.make_async_copy(source, target, sem.at[len(copies)])
            copy.start()
            copies.append(copy)

        b_count = counts["b"]
        for number, stack_ref in enumerate(stack_refs):
            other, b_step = number // b_count, number % b_count
            core = lax.rem(meta_ref[2] + other, 2)
            for a_step in range(counts["a"]):
                y_spot = lax.rem(meta_ref[0] - b_step + counts["y"], counts["y"])
                x_spot = lax.rem(meta_ref[1] - a_step + counts["x"], counts["x"])
                if place.mixed:
                    y_other = lax.rem(meta_ref[0] - a_step + counts["y"], counts["y"])
                    x_other = lax.rem(meta_ref[1] - b_step + counts["x"], counts["x"])
                    y_spot = jnp.where(core == 1, y_other, y_spot)
                    x_spot = jnp.where(core == 1, x_other, x_spot)
                dp_spot = (y_spot * counts["x"] + x_spot) * 2 + core
                for t_step in range(t_count):
                    t_spot = t_step
                    shard_ref = stack_ref.at[a_step * t_count + t_step]
                    for target, out_ref in zip(targets, out_refs):
                        t_columns = pl.ds(pl.multiple_of(t_spot * columns, columns), columns)
                        if target[0] == "rows":
                            first, depth, count = target[1:]
                            source = shard_ref.at[first : first + depth, 0:count, :]
                            here = pl.ds(pl.multiple_of(dp_spot * count, count), count)
                            send(source, out_ref.at[:, here, t_columns])
                        elif target[0] == "columns":
                            here = pl.ds(pl.multiple_of(t_spot * rows, rows), rows)
                            if columns % LANES == 0:
                                there = pl.ds(pl.multiple_of(dp_spot * columns, columns), columns)
                                send(shard_ref, out_ref.at[here, there])
                            else:
                                send(shard_ref, out_ref.at[dp_spot, here, :])
                        elif target[0] == "packed":
                            if rows % LANES == 0:
                                there = pl.ds(pl.multiple_of(dp_spot * rows, rows), rows)
                                for part in range(columns // rows):
                                    here = pl.ds(
                                        pl.multiple_of(t_spot * columns + part * rows, rows), rows
                                    )
                                    send(
                                        shard_ref.at[target[1], :, part * rows : (part + 1) * rows],
                                        out_ref.at[here, there],
                                    )
                            else:
                                send(shard_ref.at[target[1]], out_ref.at[dp_spot, t_spot])
                        elif t_step == 0:
                            first_row, count = target[1:]
                            send(shard_ref.at[0, first_row : first_row + count, :], out_ref.at[dp_spot])
        for copy in copies:
            copy.wait()

    meta = jnp.stack([place.index[axis] for axis in ("y", "x", "core", "t")]).astype(jnp.int32)
    results = pl.pallas_call(
        kernel,
        grid_spec=pltpu.PrefetchScalarGridSpec(
            num_scalar_prefetch=1,
            grid=(),
            in_specs=[pl.BlockSpec(memory_space=pl.ANY)] * len(stacks),
            out_specs=[pl.BlockSpec(memory_space=pltpu.VMEM)] * len(targets),
            scratch_shapes=[pltpu.SemaphoreType.DMA((copy_counts,))],
        ),
        out_shape=[jax.ShapeDtypeStruct(shape, dtype) for shape in shapes],
        compiler_params=pltpu.CompilerParams(vmem_limit_bytes=20 * 2**20),
        name="assemble",
    )(meta, *stacks)
    finished = []
    for target, whole in zip(targets, results):
        if target[0] == "columns" and columns % LANES:
            whole = whole.transpose(1, 0, 2).reshape(rows * t_count, columns * dp_count)
        if target[0] == "packed" and rows % LANES:
            whole = whole.reshape(dp_count, t_count, rows, columns // rows, rows)
            whole = whole.transpose(1, 3, 2, 0, 4).reshape(columns * t_count, rows * dp_count)
        finished.append(whole)
    return finished


def sent_order(place, width):
    core = place.index["core"]
    numbers = jnp.stack(place.blocks_for(1 - core) + place.blocks_for(core))
    block = width // place.dp_count
    sources = (numbers[:, None] * block + jnp.arange(block)[None, :]).reshape(1, width)
    return (jnp.arange(width)[:, None] == sources).astype(jnp.bfloat16)


def other_terms(place, pairs):
    result = []
    for inputs, grads in pairs:
        product = dot_f32(inputs[:, : inputs.shape[1] // 2], grads, TN).astype(jnp.bfloat16)
        result.append((inputs, grads, place.turn(product, "core", 1)))
    return result


def chip_terms(place, group):
    result = []
    for inputs, grads, other in group:
        half = inputs.shape[1] // 2
        step_rows = half // place.count["b"]
        terms = []
        for number in range(place.count["b"]):
            columns = slice(half + number * step_rows, half + (number + 1) * step_rows)
            rows = slice(number * step_rows, (number + 1) * step_rows)
            term = dot_f32(inputs[:, columns], grads, TN) + other[rows].astype(jnp.float32)
            terms.append(term.astype(jnp.bfloat16))
        result.append(terms)
    return result


def send_b(place, group):
    return [
        [place.turn(term, "b", step) for term, step in zip(terms, place.steps("b"))] + [terms[-1]]
        for terms in group
    ]


def added(arrays):
    total = arrays[0].astype(jnp.float32)
    for array in arrays[1:]:
        total = total + array.astype(jnp.float32)
    return total


def messages_a(place, group):
    result = []
    for arrived in group:
        step_rows = arrived[0].shape[0] // place.count["a"]
        messages = []
        for number in range(place.count["a"] - 1):
            rows = slice(number * step_rows, (number + 1) * step_rows)
            messages.append(added([one[rows] for one in arrived]).astype(jnp.bfloat16))
        result.append((messages, arrived))
    return result


def send_a(place, group):
    return [
        kept + [place.turn(message, "a", step) for message, step in zip(messages, place.steps("a"))]
        for messages, kept in group
    ]


def last_rows(kept):
    rows = kept[-1].shape[0]
    return added([one[-rows:] for one in kept])


def by_tensor(total, count):
    width = total.shape[1] // count
    return [total[:, number * width : (number + 1) * width] for number in range(count)]


def tensor_blocks(place, group):
    count = place.count["t"]
    blocks = [[] for _ in range(count)]
    for depth, kept in group:
        total = last_rows(kept).astype(jnp.bfloat16)
        for part in by_tensor(total, depth):
            for number, block in enumerate(by_tensor(part, count)):
                blocks[number].append(block)
    return jnp.stack([jnp.stack(block) for block in blocks])


def reduce_t(stack):
    return lax.psum_scatter(stack, TENSOR, scatter_dimension=0)


def reduce_t_vectors(place, kept, vectors):
    count = place.count["t"]
    total = last_rows(kept).astype(jnp.bfloat16)
    vector_count, columns = vectors.shape[0], total.shape[1] // count
    extra_rows = -(-vectors.size // (count * columns) // 16) * 16 if vectors.size else 0
    extra_rows = max(extra_rows, 16)
    width = vectors.shape[1] // count
    blocks = []
    for block, part in zip(by_tensor(total, count), by_tensor(vectors, count)):
        flat = part.astype(jnp.bfloat16).reshape(1, -1)
        flat = jnp.pad(flat, ((0, 0), (0, extra_rows * columns - flat.shape[1])))
        blocks.append(jnp.concatenate([block, flat.reshape(extra_rows, columns)]))
    result = lax.psum_scatter(jnp.stack(blocks), TENSOR, scatter_dimension=0)
    flat = result[-extra_rows:].reshape(-1)[: vector_count * width]
    return (result[:-extra_rows], flat.reshape(vector_count, width).astype(jnp.float32))


def reduce_vectors_core(place, columns):
    half = columns.shape[1] // 2
    total = columns[:, half:] + place.turn(columns[:, :half], "core", 1)
    return total


def reduce_vectors(place, total, axis):
    width = total.shape[1] // place.count[axis]
    arrived = total[:, -width:]
    for number, step in enumerate(place.steps(axis)):
        arrived = arrived + place.turn(total[:, number * width : (number + 1) * width], axis, step)
    return arrived


def clip_pairs(micro, z_count, step):
    return [
        (core * z_count + z, (z // micro) * z_count + micro * core + (step + z) % micro)
        for core in range(2)
        for z in range(z_count)
    ]


def clip_blocks(place, blocks):
    micro, z_here = blocks.shape[0], place.index["z"]
    return [
        lax.dynamic_index_in_dim(blocks, lax.rem(z_here + step, micro), 0, keepdims=False)
        for step in range(micro)
    ]


def to_clip(place, blocks):
    micro, z_count = len(blocks), place.count["z"]
    return [
        lax.ppermute(block, ("core", "z"), clip_pairs(micro, z_count, step))
        for step, block in enumerate(blocks)
    ]


def ordered_clip(place, arrived):
    micro, z_here = len(arrived), place.index["z"]
    stack = jnp.stack(arrived)
    ordered = [
        lax.dynamic_index_in_dim(stack, lax.rem(z_here - spot + micro, micro), 0, keepdims=False)
        for spot in range(micro)
    ]
    return jnp.concatenate(ordered, axis=0)


def own_blocks(place, rows_in, micro):
    z_here = place.index["z"]
    blocks = rows_in.reshape(micro, -1, rows_in.shape[-1])
    return [
        lax.dynamic_index_in_dim(blocks, lax.rem(z_here - step + micro, micro), 0, keepdims=False)
        for step in range(micro)
    ]


def from_clip(place, blocks):
    micro, z_count = len(blocks), place.count["z"]
    arrived = []
    for step, block in enumerate(blocks):
        pairs = [(end, start) for start, end in clip_pairs(micro, z_count, step)]
        arrived.append(lax.ppermute(block, ("core", "z"), pairs))
    return arrived


def own_clips(place, arrived):
    micro, z_here = len(arrived), place.index["z"]
    stack = jnp.stack(arrived)
    return jnp.stack(
        [
            lax.dynamic_index_in_dim(
                stack, lax.rem(number - lax.rem(z_here, micro) + micro, micro), 0, keepdims=False
            )
            for number in range(micro)
        ]
    )


def all_rows(place, own):
    return [own] + [place.turn(own, "seq", step) for step in place.steps("seq")]


def own_sum(place, parts):
    total = parts[0].astype(jnp.float32)
    for part, step in zip(parts[1:], place.steps("seq")):
        total = total + place.turn(part, "seq", step).astype(jnp.float32)
    return total


def neighbour_rows(place, rows_in, step):
    count = place.count["seq"]
    pairs = [
        place.seq_pair(start, start + step) for start in range(count) if 0 <= start + step < count
    ]
    return lax.ppermute(rows_in, place.names["seq"], pairs)


def feed_up(inputs, up_weight, up_bias, gain_row, shift_row):
    normed, normal, inverse = norm_rows(inputs, gain_row, shift_row)
    normed = normed.astype(jnp.bfloat16)
    upper_rows = matmul(normed, up_weight) + up_bias
    logistic = sigmoid(upper_rows)
    hidden = (upper_rows * logistic).astype(jnp.bfloat16)
    slope = swish_slope(upper_rows, logistic).astype(jnp.bfloat16)
    return (hidden, (normal, inverse, normed, slope))


def feed_back_down(grad_result, stored, down_weight):
    grad_low = grad_result.astype(jnp.bfloat16)
    grad_hidden = dot_f32(grad_low, down_weight, NT)
    grad_upper = (grad_hidden * stored[3].astype(jnp.float32)).astype(jnp.bfloat16)
    up_bias_grad = jnp.sum(grad_upper.astype(jnp.float32), axis=0)
    down_bias_grad = jnp.sum(grad_low.astype(jnp.float32), axis=0)
    return (grad_low, grad_upper, up_bias_grad, down_bias_grad)


def body(
    frames,
    cotangent,
    clip_valid,
    frame_counts,
    rel_rows,
    first_up,
    first_down,
    attend_in,
    attend_out,
    pointwise_in,
    pointwise_out,
    second_up,
    second_down,
    vectors,
    distance,
):
    place = Place()
    micro, _, width = frames.shape
    ratio_rows = FF // width
    attend_base = 3 + ratio_rows
    conv_base = attend_base + 5
    second_base = conv_base + 4
    final_base = second_base + 3 + ratio_rows
    taps_base = final_base + 2
    scale = HEAD_DIM ** (-0.5)
    order = sent_order(place, width)

    def sent(rows_low):
        return matmul(rows_low, order).astype(jnp.bfloat16)

    up_rows, up_columns = first_up.shape
    vector_rows = 16
    vector_parts = up_columns // vectors.shape[1]
    padded_vectors = jnp.pad(vectors, ((0, vector_rows * vector_parts - vectors.shape[0]), (0, 0)))
    vector_shard = (
        padded_vectors.reshape(vector_parts, vector_rows, -1).transpose(1, 0, 2).reshape(vector_rows, -1)
    )
    shard_up_one = jnp.concatenate([first_up, vector_shard], axis=0)[None]
    shard_mix = jnp.concatenate(
        [attend_in, packed(attend_out)[None], pointwise_in, packed(pointwise_out)[None]]
    )

    own_facts = jnp.stack([clip_valid, frame_counts])
    up_one = gather_t(place, shard_up_one)
    up_one, first_down, own_facts = fence(up_one, first_down, own_facts)
    up_one = gather_a(place, up_one)
    down_one = gather_t(place, first_down)
    other_facts = place.turn(own_facts, "core", 1)
    up_one, frames, shard_mix = fence(up_one, frames, shard_mix)
    up_one = gather_b(place, up_one)
    rows_low = to_clip(place, clip_blocks(place, frames))
    down_one = gather_a(place, down_one)
    both_mix = gather_t(place, shard_mix)
    up_one, down_one, second_up = fence(up_one, down_one, second_up)
    up_one = gather_core(place, up_one)
    down_one = gather_b(place, down_one)
    attend_mix = gather_a(place, both_mix[:, : attend_in.shape[0] + 1])
    point_mix = both_mix[:, attend_in.shape[0] + 1 :]
    up_two = gather_t(place, second_up[None])
    up_one, vector_slabs = assemble(
        place, up_one, [("rows", 0, 1, up_rows), ("slabs", up_rows, vector_rows)]
    )
    up_one = up_one[0]
    vector_wide = vector_slabs.reshape(place.dp_count, vector_rows, vector_parts, -1)
    vector_wide = vector_wide.transpose(2, 1, 0, 3).reshape(vector_rows * vector_parts, width)
    vector_wide = vector_wide[: vectors.shape[0]].astype(jnp.float32)

    rows_in = ordered_clip(place, rows_low).astype(jnp.float32)
    row_count = rows_in.shape[0]
    z_here = place.index["z"]
    facts = jnp.where(z_here // micro == place.index["core"], own_facts, other_facts)
    facts = lax.dynamic_index_in_dim(facts, lax.rem(z_here, micro), 1, keepdims=False)
    valid_flag = (facts[0] > 0).astype(jnp.float32)
    first_row = place.index["seq"] * row_count
    live = ((first_row + jnp.arange(row_count)) < facts[1]).astype(jnp.float32)[:, None]
    meta = jnp.stack([place.index["seq"] * (row_count // LANES), facts[1], place.index["seq"]])
    meta = meta.astype(jnp.int32)
    pick_rows = (rel_rows[:, None] == jnp.arange(OFFSETS)[None, :]).astype(jnp.bfloat16)
    table = wide_table(matmul(pick_rows, distance).astype(jnp.bfloat16))

    one_hidden, one_kept = feed_up(
        rows_in,
        up_one,
        vector_wide[2 : 2 + ratio_rows].reshape(FF),
        vector_wide[0],
        vector_wide[1],
    )
    (down_one, attend_mix, point_mix, second_down, one_hidden, one_kept, table) = fence(
        down_one, attend_mix, point_mix, second_down, one_hidden, one_kept, table
    )
    down_one = gather_core(place, down_one)
    attend_mix = gather_b(place, attend_mix)
    point_mix = gather_a(place, point_mix)
    down_two = gather_t(place, second_down)
    (down_one,) = assemble(place, down_one, [("columns",)])
    after_one = rows_in + 0.5 * (matmul(one_hidden, down_one) + vector_wide[2 + ratio_rows])
    attend_normed, attend_normal, attend_inverse = norm_rows(
        after_one, vector_wide[attend_base], vector_wide[attend_base + 1]
    )
    attend_normed = attend_normed.astype(jnp.bfloat16)
    (attend_mix, point_mix, up_two, after_one, attend_normed, attend_normal, attend_inverse) = fence(
        attend_mix, point_mix, up_two, after_one, attend_normed, attend_normal, attend_inverse
    )
    attend_mix = gather_core(place, attend_mix)
    point_mix = gather_b(place, point_mix)
    up_two = gather_a(place, up_two)
    attend_mix, attend_back_weight = assemble(place, attend_mix, [("rows", 0, 3, up_rows), ("packed", 3)])
    queries = (matmul(attend_normed, attend_mix[0]) + vector_wide[attend_base + 2]).astype(jnp.bfloat16)
    queries = (queries.astype(jnp.float32) * scale).astype(jnp.bfloat16)
    own_keys = matmul(attend_normed, attend_mix[1]).astype(jnp.bfloat16)
    own_values = (matmul(attend_normed, attend_mix[2]) + vector_wide[attend_base + 3]).astype(jnp.bfloat16)
    key_rows, value_rows = all_rows(place, own_keys), all_rows(place, own_values)
    (point_mix, up_two, down_two, cotangent, queries, key_rows, value_rows) = fence(
        point_mix, up_two, down_two, cotangent, queries, key_rows, value_rows
    )
    point_mix = gather_core(place, point_mix)
    up_two = gather_b(place, up_two)
    down_two = gather_a(place, down_two)
    cot_low = to_clip(place, clip_blocks(place, cotangent))
    context, levels = attend(meta, queries, key_rows, value_rows, table)
    (point_mix, up_two, down_two, context, levels, after_one) = fence(
        point_mix, up_two, down_two, context, levels, after_one
    )
    down_two = gather_b(place, down_two)
    up_two = gather_core(place, up_two)
    point_mix, point_back = assemble(place, point_mix, [("rows", 0, 2, up_rows), ("packed", 2)])
    after_two = after_one + matmul(context, attend_back_weight) + vector_wide[attend_base + 4]
    conv_normed, conv_normal, conv_inverse = norm_rows(
        after_two, vector_wide[conv_base], vector_wide[conv_base + 1]
    )
    conv_normed = conv_normed.astype(jnp.bfloat16)
    linear = matmul(conv_normed, point_mix[0])
    logistic = sigmoid(matmul(conv_normed, point_mix[1]))
    gated = linear * logistic * live
    taps = vector_wide[taps_base : taps_base + KERNEL]
    before = neighbour_rows(place, gated[-HALO:], 1)
    deep_gain, deep_shift = vector_wide[conv_base + 2], vector_wide[conv_base + 3]
    depth_out, activated = convolve(before, gated, taps, deep_gain, deep_shift)
    after_three = after_two + matmul(activated, point_back)
    (up_two, down_two, cot_low, after_three, depth_out, activated) = fence(
        up_two, down_two, cot_low, after_three, depth_out, activated
    )
    down_two = gather_core(place, down_two)
    (up_two,) = assemble(place, up_two, [("rows", 0, 1, up_rows)])
    up_two = up_two[0]
    two_hidden, two_kept = feed_up(
        after_three,
        up_two,
        vector_wide[second_base + 2 : second_base + 2 + ratio_rows].reshape(FF),
        vector_wide[second_base],
        vector_wide[second_base + 1],
    )
    (down_two, two_hidden, two_kept, up_two) = fence(down_two, two_hidden, two_kept, up_two)
    (down_two,) = assemble(place, down_two, [("columns",)])
    two_out = matmul(two_hidden, down_two) + vector_wide[second_base + 2 + ratio_rows]
    after_four = after_three + 0.5 * two_out
    final_rows, final_normal, final_inverse = norm_rows(
        after_four, vector_wide[final_base], vector_wide[final_base + 1]
    )
    row_out = jnp.where(valid_flag > 0, final_rows, rows_in).astype(jnp.bfloat16)
    rows_cot = ordered_clip(place, cot_low).astype(jnp.float32)
    grad_four, final_gain_grad, final_shift_grad = norm_back(
        rows_cot * valid_flag, final_normal, final_inverse, vector_wide[final_base]
    )
    grad_low, grad_upper, two_up_bias, two_down_bias = feed_back_down(
        0.5 * grad_four, two_kept, down_two
    )
    sum_down_two = other_terms(place, [(sent(grad_low), two_hidden)])
    (sum_down_two, grad_four, grad_upper, row_out) = fence(sum_down_two, grad_four, grad_upper, row_out)
    sum_down_two = send_b(place, chip_terms(place, sum_down_two))
    frames_out = from_clip(place, own_blocks(place, row_out, micro))
    sum_up_two = other_terms(place, [(sent(two_kept[2]), grad_upper)])
    grad_normed = dot_f32(grad_upper, up_two, NT)
    grad_two_in, two_gain, two_shift = norm_back(
        grad_normed, two_kept[0], two_kept[1], vector_wide[second_base]
    )
    grad_three = grad_four + grad_two_in
    conv_low = grad_three.astype(jnp.bfloat16)
    deep_norm, deep_normal, deep_inverse = norm_rows(depth_out, deep_gain, deep_shift)
    grad_deep = dot_f32(conv_low, point_back, NT) * swish_slope(deep_norm, sigmoid(deep_norm))
    grad_depth, deep_gain_grad, deep_shift_grad = norm_back(
        grad_deep, deep_normal, deep_inverse, deep_gain
    )
    after = neighbour_rows(place, grad_depth[:HALO], -1)
    (sum_down_two, sum_up_two, grad_three, conv_low, grad_depth, after, frames_out) = fence(
        sum_down_two, sum_up_two, grad_three, conv_low, grad_depth, after, frames_out
    )
    sum_down_two = send_a(place, messages_a(place, sum_down_two))
    sum_up_two = send_b(place, chip_terms(place, sum_up_two))
    grad_pair, tap_grads = convolve_back(
        meta, grad_depth, after, before, gated, taps, linear, logistic
    )
    (sum_down_two, sum_up_two, grad_pair) = fence(sum_down_two, sum_up_two, grad_pair)
    sum_down_two = reduce_t(tensor_blocks(place, [(1, sum_down_two[0])]))
    sum_up_two = send_a(place, messages_a(place, sum_up_two))
    sum_point = other_terms(
        place,
        [
            (sent(conv_normed), grad_pair),
            (sent(conv_low), activated),
        ],
    )
    grad_conv_normed = dot_f32(grad_pair[:, :width], point_mix[0], NT)
    grad_conv_normed = grad_conv_normed + dot_f32(grad_pair[:, width:], point_mix[1], NT)
    grad_conv_in, conv_gain_grad, conv_shift_grad = norm_back(
        grad_conv_normed, conv_normal, conv_inverse, vector_wide[conv_base]
    )
    grad_two = grad_three + grad_conv_in
    attend_low = grad_two.astype(jnp.bfloat16)
    grad_context = dot_f32(attend_low, attend_back_weight, NT).astype(jnp.bfloat16)
    (sum_up_two, sum_point, grad_two, attend_low, grad_context) = fence(
        sum_up_two, sum_point, grad_two, attend_low, grad_context
    )
    sum_up_two = reduce_t(tensor_blocks(place, [(1, sum_up_two[0])]))
    sum_point = send_b(place, chip_terms(place, sum_point))
    grad_queries, part_keys, part_values, grad_table = attend_back(
        meta, queries, key_rows, value_rows, table, grad_context, context, levels
    )
    (sum_point, grad_queries, part_keys, part_values, grad_table, sum_down_two) = fence(
        sum_point, grad_queries, part_keys, part_values, grad_table, sum_down_two
    )
    sum_point = send_a(place, messages_a(place, sum_point))
    grad_keys = own_sum(place, part_keys).astype(jnp.bfloat16)
    grad_values = own_sum(place, part_values).astype(jnp.bfloat16)
    sum_distance = jnp.dot(
        pick_rows.astype(jnp.float32).T, table_grad(grad_table), precision=lax.Precision.HIGHEST
    )
    sent_attend, sent_out = sent(attend_normed), sent(attend_low)
    (sum_point, sum_distance, grad_keys, grad_values, sum_up_two, sent_attend, sent_out) = fence(
        sum_point, sum_distance, grad_keys, grad_values, sum_up_two, sent_attend, sent_out
    )
    sum_attend = other_terms(
        place,
        [
            (sent_attend, jnp.concatenate([grad_queries, grad_keys, grad_values], axis=1)),
            (sent_out, context),
        ],
    )
    sum_distance = sum(
        [place.turn(sum_distance, "t", step) for step in place.steps("t")], sum_distance
    )
    sum_attend = chip_terms(place, sum_attend)
    sum_point = tensor_blocks(place, [(2, sum_point[0]), (1, sum_point[1])])
    grad_attend_normed = (
        dot_f32(grad_queries, attend_mix[0], NT)
        + dot_f32(grad_keys, attend_mix[1], NT)
        + dot_f32(grad_values, attend_mix[2], NT)
    )
    grad_attend_in, attend_gain_grad, attend_shift_grad = norm_back(
        grad_attend_normed, attend_normal, attend_inverse, vector_wide[attend_base]
    )
    grad_one = grad_two + grad_attend_in
    (sum_point, sum_attend, sum_distance, grad_one) = fence(sum_point, sum_attend, sum_distance, grad_one)
    sum_attend = send_b(place, sum_attend)
    sum_point = reduce_t(sum_point)
    grad_low, grad_upper, one_up_bias, one_down_bias = feed_back_down(0.5 * grad_one, one_kept, down_one)
    sent_low, sent_one = sent(grad_low), sent(one_kept[2])
    (sum_attend, grad_upper, sum_distance, sent_low, sent_one, one_up_bias) = fence(
        sum_attend, grad_upper, sum_distance, sent_low, sent_one, one_up_bias
    )
    sum_attend = send_a(place, messages_a(place, sum_attend))
    sum_down_one = other_terms(place, [(sent_low, one_hidden)])
    sum_up_one = other_terms(place, [(sent_one, grad_upper)])
    sum_down_one = chip_terms(place, sum_down_one)
    sum_distance = sum_distance + place.turn(sum_distance, "core", 1)
    sum_attend = tensor_blocks(place, [(3, sum_attend[0]), (1, sum_attend[1])])
    (sum_attend, sum_down_one, sum_up_one, grad_upper, sum_distance, sum_point) = fence(
        sum_attend, sum_down_one, sum_up_one, grad_upper, sum_distance, sum_point
    )
    sum_down_one = send_b(place, sum_down_one)
    sum_attend = reduce_t(sum_attend)
    sum_up_one = chip_terms(place, sum_up_one)
    sum_distance = sum(
        [place.turn(sum_distance, "b", step) for step in place.steps("b")], sum_distance
    )
    grad_normed = dot_f32(grad_upper, up_one, NT)
    grad_one_in, one_gain, one_shift = norm_back(grad_normed, one_kept[0], one_kept[1], vector_wide[0])
    grad_rows = grad_one + grad_one_in + (1.0 - valid_flag) * rows_cot

    grad_blocks = own_blocks(place, grad_rows.astype(jnp.bfloat16), micro)
    (sum_attend, sum_down_one, sum_up_one, grad_blocks, one_gain, one_shift, sum_distance) = fence(
        sum_attend, sum_down_one, sum_up_one, grad_blocks, one_gain, one_shift, sum_distance
    )
    sum_down_one = send_a(place, messages_a(place, sum_down_one))
    sum_up_one = send_b(place, sum_up_one)
    frames_grad = from_clip(place, grad_blocks)
    sum_distance = sum(
        [place.turn(sum_distance, "a", step) for step in place.steps("a")], sum_distance
    )

    def column_sum(rows):
        return jnp.sum(rows.astype(jnp.float32), axis=0)

    vector_part = jnp.concatenate(
        [
            jnp.stack([one_gain, one_shift]),
            one_up_bias.reshape(ratio_rows, width),
            jnp.stack(
                [
                    one_down_bias,
                    attend_gain_grad,
                    attend_shift_grad,
                    column_sum(grad_queries),
                    column_sum(grad_values),
                    column_sum(attend_low),
                    conv_gain_grad,
                    conv_shift_grad,
                    deep_gain_grad,
                    deep_shift_grad,
                    two_gain,
                    two_shift,
                ]
            ),
            two_up_bias.reshape(ratio_rows, width),
            jnp.stack([two_down_bias, final_gain_grad, final_shift_grad]),
            tap_grads[:KERNEL],
        ],
        axis=0,
    )
    vector_part = jnp.dot(vector_part, order.astype(jnp.float32), precision=lax.Precision.HIGHEST)
    sum_vectors = reduce_vectors_core(place, vector_part)
    (sum_up_one, sum_down_one, sum_vectors, frames_grad) = fence(
        sum_up_one, sum_down_one, sum_vectors, frames_grad
    )
    sum_up_one = send_a(place, messages_a(place, sum_up_one))
    sum_down_one = reduce_t(tensor_blocks(place, [(1, sum_down_one[0])]))
    sum_vectors = reduce_vectors(place, sum_vectors, "b")
    sum_vectors = reduce_vectors(place, sum_vectors, "a")
    (sum_up_one, sum_vectors) = fence(sum_up_one, sum_vectors)
    sum_up_one, grad_vectors = reduce_t_vectors(place, sum_up_one[0], sum_vectors)
    wide = jnp.float32
    return (
        own_clips(place, frames_out),
        own_clips(place, frames_grad),
        sum_up_one.astype(wide),
        sum_down_one[0].T.astype(wide),
        sum_attend[:3].astype(wide),
        sum_attend[3].T.astype(wide),
        sum_point[:2].astype(wide),
        sum_point[2].T.astype(wide),
        sum_up_two[0].astype(wide),
        sum_down_two[0].T.astype(wide),
        grad_vectors,
        sum_distance,
    )


def solution(mesh):
    dp_count, tensor_count = mesh.shape["dp"], mesh.shape["tensor"]

    def program(*arrays):
        group = 2 * (arrays[0].shape[0] // dp_count)
        parted = Mesh(
            mesh.devices.reshape(dp_count // 4, 2, 2, tensor_count // group, group),
            ("y", "x", "core", "far", "z"),
        )
        dp, tensor = ("y", "x", "core"), TENSOR
        return jax.shard_map(
            body,
            mesh=parted,
            in_specs=(
                P(dp, tensor, None),
                P(dp, tensor, None),
                P(dp),
                P(dp),
                P(),
                P(dp, tensor),
                P(tensor, dp),
                P(None, dp, tensor),
                P(tensor, dp),
                P(None, dp, tensor),
                P(tensor, dp),
                P(dp, tensor),
                P(tensor, dp),
                P(None, dp),
                P(),
            ),
            out_specs=(
                P(dp, tensor, None),
                P(dp, tensor, None),
                P(dp, tensor),
                P(tensor, dp),
                P(None, dp, tensor),
                P(tensor, dp),
                P(None, dp, tensor),
                P(tensor, dp),
                P(dp, tensor),
                P(tensor, dp),
                P(None, dp + tensor),
                P(),
            ),
            check_vma=False,
        )(*arrays)

    return program
```

```python
import functools

import jax
import jax.numpy as jnp
from jax import lax
from jax.experimental import pallas as pl
from jax.experimental.pallas import tpu as pltpu
from jax.sharding import Mesh
from jax.sharding import PartitionSpec as P

HEADS = 16
HEAD_DIM = 64
FF = 4096
KERNEL = 31
LEFT = 64
OFFSETS = 73
EPSILON = 1e-05

LANES = 128
SOFT_ROWS = 32
SLOPE_ROWS = 16
RIGHT = OFFSETS - 1 - LEFT
NT = (((1,), (1,)), ((), ()))
NN = (((1,), (0,)), ((), ()))
TN = (((0,), (0,)), ((), ()))


def dot_f32(left_side, right_side, dims):
    return lax.dot_general(left_side, right_side, dims, preferred_element_type=jnp.float32)


def band_distance():
    shape = (LANES, 3 * LANES)
    return (
        lax.broadcasted_iota(jnp.int32, shape, 1)
        - LANES
        - lax.broadcasted_iota(jnp.int32, shape, 0)
    )


LAST_ROWS = 8


def add_band(score_ref, half, source, distance, block, number):
    rows = slice(number * LANES, (number + 1) * LANES)
    own = source[rows]
    left_col = own[:, 2 * LANES - LEFT : 2 * LANES - LEFT + 1]
    right_col = own[:, RIGHT : RIGHT + 1]
    rolled = pltpu.roll(own - right_col, LANES, 1, stride=1, stride_axis=0)
    window = pl.multiple_of(block * LANES, LANES)
    near = rolled[:LEFT, :LANES] + (right_col - left_col)[:LEFT]
    near = jnp.where(distance[:LEFT, :LANES] > -LEFT, near, 0.0)
    score_ref[half, number * LANES : number * LANES + LEFT, pl.ds(window, LANES)] += near
    score_ref[half, rows, pl.ds(window + LANES, LANES)] += rolled[:, LANES:]
    last = LANES - LAST_ROWS
    after = jnp.where(distance[last:, 2 * LANES :] < RIGHT, rolled[last:, :LANES], 0.0)
    score_ref[half, number * LANES + last : (number + 1) * LANES, pl.ds(window + 2 * LANES, LANES)] += after


def in_half(shape, half):
    lanes = lax.broadcasted_iota(jnp.int32, shape, 1)
    return (lanes < HEAD_DIM) if half == 0 else (lanes >= HEAD_DIM)


def spare_lane(shape):
    return lax.rem(lax.broadcasted_iota(jnp.int32, shape, 1), HEAD_DIM)


def key_marks(meta_ref, key_count, blocks):
    shape = (key_count, LANES)
    spare, keys = spare_lane(shape), lax.broadcasted_iota(jnp.int32, shape, 0)
    before = keys < (meta_ref[0] + spare // 2) * LANES
    side = jnp.where(lax.rem(spare, 2) == 0, before.astype(jnp.float32), 1.0 - before.astype(jnp.float32))
    dead = jnp.where(keys < meta_ref[1], 0.0, -1e30)
    ones = (spare < 2 * blocks + 4).astype(jnp.float32)
    marks = jnp.where(spare < 2 * blocks, side, jnp.where(spare == 2 * blocks, dead, ones))
    return marks.astype(jnp.bfloat16)


def in_parts(column):
    parts = []
    for _ in range(3):
        part = column.astype(jnp.bfloat16).astype(jnp.float32)
        parts.append(part)
        column = column - part
    return parts


def with_marks(rows_half, half, columns_of):
    square = (LANES, LANES)
    spare, mine = spare_lane(square), in_half(square, half)
    parts = []
    for number in range(rows_half.shape[0] // LANES):
        own = rows_half[number * LANES : (number + 1) * LANES].astype(jnp.float32)
        marks = jnp.zeros(square, jnp.float32)
        for place, column in columns_of(number):
            marks = jnp.where(spare == place, column, marks)
        parts.append(jnp.where(mine, own, marks).astype(jnp.bfloat16))
    return jnp.concatenate(parts, axis=0)


def marked_queries(q_half, half, source, extra, blocks):
    def columns_of(number):
        rows = slice(number * LANES, (number + 1) * LANES)
        own = source[rows]
        columns = [
            (2 * number, own[:, 2 * LANES - LEFT : 2 * LANES - LEFT + 1]),
            (2 * number + 1, own[:, RIGHT : RIGHT + 1]),
            (2 * blocks, 1.0),
        ]
        return columns + [(2 * blocks + 1 + place, part[rows]) for place, part in enumerate(extra)]

    return with_marks(q_half, half, columns_of)


def key_spot(meta_ref, step, count, row_count):
    spot = lax.rem(meta_ref[2] - step + count, count)
    return pl.ds(pl.multiple_of(spot * row_count, row_count), row_count)


def attend_kernel(count, meta_ref, q_ref, e_ref, *refs):
    key_refs, value_refs = refs[:count], refs[count : 2 * count]
    c_ref, lse_ref, score_ref, share_ref, marks_ref, k_ref, v_ref = refs[2 * count :]
    row_count, key_count = q_ref.shape[0], k_ref.shape[0]
    for step in range(count):
        k_ref[key_spot(meta_ref, step, count, row_count)] = key_refs[step][...]
        v_ref[key_spot(meta_ref, step, count, row_count)] = value_refs[step][...]
    blocks = row_count // LANES
    pair = pl.program_id(0)
    lanes = lax.broadcasted_iota(jnp.int32, (row_count, LANES), 1)
    distance = band_distance()

    @pl.when(pair == 0)
    def _():
        marks_ref[...] = key_marks(meta_ref, key_count, blocks)

    sources = []
    for half in range(2):
        mine = in_half((row_count, LANES), half)
        q_half = jnp.where(mine, q_ref[...], 0)
        source = dot_f32(q_half, e_ref[...], NT).astype(jnp.bfloat16).astype(jnp.float32)
        sources.append(source)
        queries = marked_queries(q_half, half, source, [], blocks)
        keys = jnp.where(in_half((key_count, LANES), half), k_ref[...], marks_ref[...])
        score_ref[half, :, LANES : LANES + key_count] = dot_f32(queries, keys, NT)
    result = None
    for half in range(2):
        inverses = []
        for number in range(blocks):
            rows = slice(number * LANES, (number + 1) * LANES)
            add_band(score_ref, half, sources[half], distance, meta_ref[0] + number, number)
            for first in range(number * LANES, (number + 1) * LANES, SOFT_ROWS):
                few = slice(first, first + SOFT_ROWS)
                scores = score_ref[half, few, LANES : LANES + key_count]
                peak = jnp.max(scores, axis=1, keepdims=True)
                grown = jnp.exp(scores - peak)
                total = jnp.sum(grown, axis=1, keepdims=True)
                share_ref[half, few] = grown.astype(jnp.bfloat16)
                inverses.append(1.0 / total)
                lse_ref[few] = jnp.where(
                    lanes[few] == 2 * pair + half, peak + jnp.log(total), lse_ref[few]
                )
        context = dot_f32(share_ref[half], v_ref[...], NN) * jnp.concatenate(inverses, axis=0)
        result = context if half == 0 else jnp.where(in_half(context.shape, 1), context, result)
    c_ref[...] = result.astype(jnp.bfloat16)


def attend_back_kernel(count, meta_ref, q_ref, e_ref, dc_ref, c_ref, lse_ref, *refs):
    key_refs, value_refs = refs[:count], refs[count : 2 * count]
    dq_ref, de_ref = refs[2 * count : 2 * count + 2]
    dk_refs, dv_refs = refs[2 * count + 2 : 3 * count + 2], refs[3 * count + 2 : 4 * count + 2]
    score_ref, grad_ref, share_ref, slope_ref, source_ref, wide_ref, marks_ref, k_ref, v_ref, turn_ref = refs[
        4 * count + 2 :
    ]
    row_count, key_count = q_ref.shape[0], k_ref.shape[0]
    for step in range(count):
        k_ref[key_spot(meta_ref, step, count, row_count)] = key_refs[step][...]
        v_ref[key_spot(meta_ref, step, count, row_count)] = value_refs[step][...]
    key_blocks, blocks = key_count // LANES, row_count // LANES
    pair = pl.program_id(0)
    lanes = lax.broadcasted_iota(jnp.int32, (row_count, LANES), 1)
    distance = band_distance()
    square = (LANES, LANES)
    flip = (
        lax.broadcasted_iota(jnp.int32, square, 0) + lax.broadcasted_iota(jnp.int32, square, 1)
        == LANES - 1
    ).astype(jnp.float32).astype(jnp.bfloat16)
    spots = lax.broadcasted_iota(jnp.int32, square, 1)

    @pl.when(pair == 0)
    def _():
        shape = (key_count, LANES)
        place = lax.broadcasted_iota(jnp.int32, shape, 1)
        edge = (meta_ref[0] + place // 2) * LANES
        key = lax.broadcasted_iota(jnp.int32, shape, 0)
        before = (key < edge).astype(jnp.float32)
        after = (key >= edge + LANES).astype(jnp.float32)
        wide_ref[:, LANES:] = jnp.where(lax.rem(place, 2) == 0, before, after).astype(jnp.bfloat16)
        for half in range(2):
            slope_ref[half, :, :LANES] = jnp.zeros((row_count, LANES), jnp.bfloat16)
            slope_ref[half, :, LANES + key_count :] = jnp.zeros((row_count, LANES), jnp.bfloat16)
        de_ref[...] = jnp.zeros(de_ref.shape, jnp.float32)
        marks_ref[0] = key_marks(meta_ref, key_count, blocks)
        marks_ref[1] = (spare_lane(shape) < 3).astype(jnp.float32).astype(jnp.bfloat16)

    wide_ref[:, :LANES] = k_ref[...]
    inner_all = dc_ref[...].astype(jnp.float32) * c_ref[...].astype(jnp.float32)
    sources, q_halves, dc_halves = [], [], []
    for half in range(2):
        mine, mine_keys = in_half((row_count, LANES), half), in_half((key_count, LANES), half)
        q_half = jnp.where(mine, q_ref[...], 0)
        dc_half = jnp.where(mine, dc_ref[...], 0)
        source = dot_f32(q_half, e_ref[...], NT).astype(jnp.bfloat16).astype(jnp.float32)
        inner = jnp.sum(jnp.where(mine, inner_all, 0.0), axis=1, keepdims=True)
        level = jnp.sum(
            jnp.where(lanes == 2 * pair + half, lse_ref[...], 0.0), axis=1, keepdims=True
        )
        queries = marked_queries(q_half, half, source, in_parts(-level), blocks)
        keys = jnp.where(mine_keys, k_ref[...], marks_ref[0])
        score_ref[half, :, LANES : LANES + key_count] = dot_f32(queries, keys, NT)
        inner_parts = in_parts(-inner)
        grads = with_marks(
            dc_half,
            half,
            lambda number, parts=inner_parts: [
                (place, part[number * LANES : (number + 1) * LANES])
                for place, part in enumerate(parts)
            ],
        )
        values = jnp.where(mine_keys, v_ref[...], marks_ref[1])
        grad_ref[half] = dot_f32(grads, values, NT)
        sources.append(source)
        q_halves.append(q_half)
        dc_halves.append(dc_half)
    grad_q = grad_k = grad_v = None
    for half in range(2):
        for number in range(blocks):
            rows = slice(number * LANES, (number + 1) * LANES)
            add_band(score_ref, half, sources[half], distance, meta_ref[0] + number, number)
            for first in range(number * LANES, (number + 1) * LANES, SLOPE_ROWS):
                few = slice(first, first + SLOPE_ROWS)
                shares = jnp.exp(score_ref[half, few, LANES : LANES + key_count])
                share_ref[half, few] = shares.astype(jnp.bfloat16)
                slope_ref[half, few, LANES : LANES + key_count] = (
                    shares * grad_ref[half, few]
                ).astype(jnp.bfloat16)
    for half in range(2):
        mine = in_half((row_count, LANES), half)
        slopes = slope_ref[half, :, LANES : LANES + key_count]
        wide = dot_f32(slopes, wide_ref[...], NN)
        before = wide[:, LANES:]
        for number in range(blocks):
            rows = slice(number * LANES, (number + 1) * LANES)
            window = pl.multiple_of((meta_ref[0] + number) * LANES, LANES)
            first, last = number * LANES, (number + 1) * LANES - LAST_ROWS
            near = slope_ref[half, first : first + LEFT, pl.ds(window, LANES)].astype(jnp.float32)
            near = jnp.where(distance[:LEFT, :LANES] > -LEFT, near, 0.0)
            final = slope_ref[half, last - 8 : last + 8, pl.ds(window + 2 * LANES, LANES)]
            final = final.astype(jnp.float32)[8:]
            final = jnp.where(distance[LANES - LAST_ROWS :, 2 * LANES :] < RIGHT, final, 0.0)
            middle = slope_ref[half, rows, pl.ds(window + LANES, LANES)]
            gap = jnp.zeros((LANES - LEFT - LAST_ROWS, LANES), jnp.float32)
            edges = jnp.concatenate([near, gap, final], axis=0)
            inner_sum = jnp.sum(edges, axis=1, keepdims=True)
            first_rows = lax.broadcasted_iota(jnp.int32, (LANES, 1), 0) < LEFT
            far_left = before[rows, 2 * number : 2 * number + 1] - jnp.where(first_rows, inner_sum, 0.0)
            far_right = before[rows, 2 * number + 1 : 2 * number + 2] - jnp.where(
                first_rows, 0.0, inner_sum
            )
            band = jnp.concatenate([edges.astype(jnp.bfloat16), middle], axis=1)
            turned = dot_f32(flip, band, NN)
            turned = pltpu.roll(turned, 1, 1, stride=1, stride_axis=0)
            turned = dot_f32(flip, turned.astype(jnp.bfloat16), NN)
            turned = jnp.concatenate(
                [
                    turned[:, :LANES] + jnp.where(spots == RIGHT, far_right, 0.0),
                    turned[:, LANES:] + jnp.where(spots == 0, far_left, 0.0),
                ],
                axis=1,
            )
            source_ref[half, rows] = turned.astype(jnp.bfloat16)
        q_part = wide[:, :LANES] + dot_f32(source_ref[half], e_ref[...], NN)
        k_part = dot_f32(q_halves[half], slopes, TN)
        v_part = dot_f32(dc_halves[half], share_ref[half], TN)
        de_ref[...] += dot_f32(q_halves[half], source_ref[half], TN)
        grad_q = q_part if half == 0 else jnp.where(mine, q_part, grad_q)
        grad_k = k_part if half == 0 else grad_k + k_part
        grad_v = v_part if half == 0 else grad_v + v_part
    dq_ref[...] = (grad_q * HEAD_DIM ** (-0.5)).astype(jnp.bfloat16)
    for grad, grad_refs in ((grad_k, dk_refs), (grad_v, dv_refs)):
        turn_ref[...] = grad.T
        for step in range(count):
            rows = key_spot(meta_ref, -step, count, row_count)
            grad_refs[step][...] = turn_ref[rows].astype(jnp.bfloat16)


def pair_spec(row_count):
    return pl.BlockSpec((row_count, LANES), lambda pair, meta: (0, pair))


def fixed_spec(row_count, column_count):
    return pl.BlockSpec((row_count, column_count), lambda pair, meta: (0, 0))


def attend(meta, queries, key_rows, value_rows, table):
    row_count, width = queries.shape
    count = len(key_rows)
    key_count = row_count * count
    return pl.pallas_call(
        functools.partial(attend_kernel, count),
        grid_spec=pltpu.PrefetchScalarGridSpec(
            num_scalar_prefetch=1,
            grid=(width // LANES,),
            in_specs=[pair_spec(row_count), fixed_spec(2 * LANES, LANES)]
            + [pair_spec(row_count)] * (2 * count),
            out_specs=[pair_spec(row_count), fixed_spec(row_count, LANES)],
            scratch_shapes=[
                pltpu.VMEM((2, row_count, key_count + 2 * LANES), jnp.float32),
                pltpu.VMEM((2, row_count, key_count), jnp.bfloat16),
                pltpu.VMEM((key_count, LANES), jnp.bfloat16),
                pltpu.VMEM((key_count, LANES), jnp.bfloat16),
                pltpu.VMEM((key_count, LANES), jnp.bfloat16),
            ],
        ),
        out_shape=[
            jax.ShapeDtypeStruct((row_count, width), jnp.bfloat16),
            jax.ShapeDtypeStruct((row_count, LANES), jnp.float32),
        ],
        compiler_params=pltpu.CompilerParams(vmem_limit_bytes=48 * 2**20),
        name="attend",
    )(meta, queries, table, *key_rows, *value_rows)


def attend_back(meta, queries, key_rows, value_rows, table, grad_context, context, levels):
    row_count, width = queries.shape
    count = len(key_rows)
    key_count = row_count * count
    rows_out = jax.ShapeDtypeStruct((row_count, width), jnp.bfloat16)
    results = pl.pallas_call(
        functools.partial(attend_back_kernel, count),
        grid_spec=pltpu.PrefetchScalarGridSpec(
            num_scalar_prefetch=1,
            grid=(width // LANES,),
            in_specs=[
                pair_spec(row_count),
                fixed_spec(2 * LANES, LANES),
                pair_spec(row_count),
                pair_spec(row_count),
                fixed_spec(row_count, LANES),
            ]
            + [pair_spec(row_count)] * (2 * count),
            out_specs=[pair_spec(row_count), fixed_spec(LANES, 2 * LANES)]
            + [pair_spec(row_count)] * (2 * count),
            scratch_shapes=[
                pltpu.VMEM((2, row_count, key_count + 2 * LANES), jnp.float32),
                pltpu.VMEM((2, row_count, key_count), jnp.float32),
                pltpu.VMEM((2, row_count, key_count), jnp.bfloat16),
                pltpu.VMEM((2, row_count, key_count + 2 * LANES), jnp.bfloat16),
                pltpu.VMEM((2, row_count, 2 * LANES), jnp.bfloat16),
                pltpu.VMEM((key_count, 2 * LANES), jnp.bfloat16),
                pltpu.VMEM((2, key_count, LANES), jnp.bfloat16),
                pltpu.VMEM((key_count, LANES), jnp.bfloat16),
                pltpu.VMEM((key_count, LANES), jnp.bfloat16),
                pltpu.VMEM((key_count, LANES), jnp.float32),
            ],
        ),
        out_shape=[rows_out, jax.ShapeDtypeStruct((LANES, 2 * LANES), jnp.float32)]
        + [rows_out] * (2 * count),
        compiler_params=pltpu.CompilerParams(vmem_limit_bytes=48 * 2**20),
        name="attend_back",
    )(meta, queries, table, grad_context, context, levels, *key_rows, *value_rows)
    return results[0], results[2 : 2 + count], results[2 + count :], results[1]


def wide_table(table_low):
    places = jnp.arange(2 * LANES)
    offsets = jnp.clip(jnp.where(places < LANES, places, places - 2 * LANES) + LEFT, 0, OFFSETS - 1)
    rows = table_low[offsets]
    return jnp.concatenate([rows, rows], axis=1)


def table_grad(wide_grad):
    folded = (wide_grad[:HEAD_DIM] + wide_grad[HEAD_DIM:]).T
    first = jnp.sum(folded[LANES : 2 * LANES - LEFT + 1], axis=0, keepdims=True)
    last = jnp.sum(folded[RIGHT:LANES], axis=0, keepdims=True)
    return jnp.concatenate([first, folded[2 * LANES - LEFT + 1 :], folded[:RIGHT], last], axis=0)


def sigmoid(values):
    return 0.5 * jnp.tanh(0.5 * values) + 0.5


def swish_slope(values, logistic):
    return logistic + values * logistic * (1.0 - logistic)


def matmul(left_side, right_side):
    return dot_f32(left_side, right_side, NN)


def norm_rows(values, gain_row, shift_row):
    centred = values - jnp.mean(values, axis=-1, keepdims=True)
    variance = jnp.mean(centred * centred, axis=-1, keepdims=True)
    inverse = lax.rsqrt(variance + EPSILON)
    normal = centred * inverse
    return (normal * gain_row + shift_row, normal, inverse)


def norm_back(grad_out, normal, inverse, gain_row):
    grad_normal = grad_out * gain_row
    grad_in = inverse * (
        grad_normal
        - jnp.mean(grad_normal, axis=-1, keepdims=True)
        - normal * jnp.mean(grad_normal * normal, axis=-1, keepdims=True)
    )
    return (grad_in, jnp.sum(grad_out * normal, axis=0), jnp.sum(grad_out, axis=0))


CHUNK = 64
HALO = 32


def tap_slices(window, offsets):
    length = window.shape[0]
    slices = {}
    for rest in range(8):
        wanted = [offset for offset in offsets if offset % 8 == rest]
        if wanted:
            turned = pltpu.roll(window, length - rest, 0) if rest else window
            for offset in wanted:
                slices[offset] = turned[offset - rest : offset - rest + CHUNK]
    return slices


def convolve_kernel(before_ref, gated_ref, taps_ref, gain_ref, shift_ref, deep_ref, low_ref, padded_ref):
    row_count, width = gated_ref.shape
    lead = HALO - (KERNEL - 1)
    padded_ref[:HALO] = before_ref[...]
    padded_ref[HALO:] = gated_ref[...]

    @pl.loop(0, width // LANES)
    def _(column):
        lanes = pl.ds(pl.multiple_of(column * LANES, LANES), LANES)
        taps = [taps_ref[tap : tap + 1, lanes] for tap in range(KERNEL)]

        @pl.loop(0, row_count // CHUNK)
        def _(chunk):
            first = pl.multiple_of(chunk * CHUNK, CHUNK)
            window = padded_ref[pl.ds(first, CHUNK + HALO), lanes]
            slices = tap_slices(window, [tap + lead for tap in range(KERNEL)])
            total = taps[0] * slices[lead]
            for tap in range(1, KERNEL):
                total = total + taps[tap] * slices[tap + lead]
            deep_ref[pl.ds(first, CHUNK), lanes] = total

    @pl.loop(0, row_count // CHUNK)
    def _(chunk):
        rows = pl.ds(pl.multiple_of(chunk * CHUNK, CHUNK), CHUNK)
        deep_norm, _, _ = norm_rows(deep_ref[rows, :], gain_ref[...], shift_ref[...])
        low_ref[rows, :] = (deep_norm * sigmoid(deep_norm)).astype(jnp.bfloat16)


def convolve(before, gated, taps, gain_row, shift_row):
    shape = gated.shape
    return pl.pallas_call(
        convolve_kernel,
        in_specs=[pl.BlockSpec(memory_space=pltpu.VMEM)] * 5,
        out_specs=[pl.BlockSpec(memory_space=pltpu.VMEM)] * 2,
        out_shape=[
            jax.ShapeDtypeStruct(shape, jnp.float32),
            jax.ShapeDtypeStruct(shape, jnp.bfloat16),
        ],
        scratch_shapes=[pltpu.VMEM((shape[0] + HALO, shape[1]), jnp.float32)],
        compiler_params=pltpu.CompilerParams(vmem_limit_bytes=32 * 2**20),
        name="convolve",
    )(before, gated, taps, gain_row[None], shift_row[None])


def convolve_back_kernel(
    meta_ref, grad_ref, after_ref, before_ref, gated_ref, taps_ref, linear_ref, logistic_ref,
    pair_ref, tap_grad_ref, padded_ref, extended_ref,
):
    row_count, width = gated_ref.shape
    lead = HALO - (KERNEL - 1)
    padded_ref[:HALO] = before_ref[...]
    padded_ref[HALO:] = gated_ref[...]
    extended_ref[:row_count] = grad_ref[...]
    extended_ref[row_count:] = after_ref[...]
    live_rows = meta_ref[1] - meta_ref[0] * LANES

    @pl.loop(0, width // LANES)
    def _(column):
        start = pl.multiple_of(column * LANES, LANES)
        lanes = pl.ds(start, LANES)
        taps = [taps_ref[tap : tap + 1, lanes] for tap in range(KERNEL)]

        @pl.loop(0, row_count // CHUNK)
        def _(chunk):
            first = pl.multiple_of(chunk * CHUNK, CHUNK)
            rows = pl.ds(first, CHUNK)
            window = extended_ref[pl.ds(first, CHUNK + HALO), lanes]
            slices = tap_slices(window, [KERNEL - 1 - tap for tap in range(KERNEL)])
            total = taps[0] * slices[KERNEL - 1]
            for tap in range(1, KERNEL):
                total = total + taps[tap] * slices[KERNEL - 1 - tap]
            places = first + lax.broadcasted_iota(jnp.int32, (CHUNK, LANES), 0)
            logistic = logistic_ref[rows, lanes]
            grad_linear = jnp.where(places < live_rows, total, 0.0) * logistic
            pair_ref[rows, lanes] = grad_linear.astype(jnp.bfloat16)
            grad_gate = grad_linear * linear_ref[rows, lanes] * (1.0 - logistic)
            gate_lanes = pl.ds(pl.multiple_of(width + start, LANES), LANES)
            pair_ref[rows, gate_lanes] = grad_gate.astype(jnp.bfloat16)

        def tap_step(chunk, totals):
            first = pl.multiple_of(chunk * CHUNK, CHUNK)
            window = padded_ref[pl.ds(first, CHUNK + HALO), lanes]
            slices = tap_slices(window, [tap + lead for tap in range(KERNEL)])
            grad = extended_ref[pl.ds(first, CHUNK), lanes]
            added_up = []
            for tap in range(KERNEL):
                product = slices[tap + lead] * grad
                part = product[:8]
                for piece in range(1, CHUNK // 8):
                    part = part + product[8 * piece : 8 * piece + 8]
                added_up.append(totals[tap] + part)
            return tuple(added_up)

        zero = jnp.zeros((8, LANES), jnp.float32)
        totals = lax.fori_loop(0, row_count // CHUNK, tap_step, (zero,) * KERNEL)
        for tap in range(KERNEL):
            tap_grad_ref[tap : tap + 1, lanes] = jnp.sum(totals[tap], axis=0, keepdims=True)


def convolve_back(meta, grad_depth, after, before, gated, taps, linear, logistic):
    row_count, width = gated.shape
    vmem = pl.BlockSpec(memory_space=pltpu.VMEM)
    return pl.pallas_call(
        convolve_back_kernel,
        grid_spec=pltpu.PrefetchScalarGridSpec(
            num_scalar_prefetch=1,
            grid=(),
            in_specs=[vmem] * 7,
            out_specs=[vmem] * 2,
            scratch_shapes=[pltpu.VMEM((row_count + HALO, width), jnp.float32)] * 2,
        ),
        out_shape=[
            jax.ShapeDtypeStruct((row_count, 2 * width), jnp.bfloat16),
            jax.ShapeDtypeStruct(taps.shape, jnp.float32),
        ],
        compiler_params=pltpu.CompilerParams(vmem_limit_bytes=40 * 2**20),
        name="convolve_back",
    )(meta, grad_depth, after, before, gated, taps, linear, logistic)


def fence(*values):
    return lax.optimization_barrier(values)


TENSOR = ("far", "z")


class Place:
    def __init__(self):
        axes = ("y", "x", "core", "far", "z")
        self.count = {axis: lax.axis_size(axis) for axis in axes}
        self.index = {axis: lax.axis_index(axis) for axis in axes}
        count, index = self.count, self.index
        count["t"] = count["far"] * count["z"]
        index["t"] = index["far"] * count["z"] + index["z"]
        count["seq"] = count["far"] * 2
        index["seq"] = index["far"] * 2 + index["core"]
        count["a"], count["b"] = count["x"], count["y"]
        self.mixed = count["x"] == count["y"]
        self.names = {"t": TENSOR, "seq": ("core", "far")}
        self.dp_count = count["y"] * count["x"] * 2

    def seq_pair(self, start, end):
        far = self.count["far"]
        return ((start % 2) * far + start // 2, (end % 2) * far + end // 2)

    def turn(self, block, axis, step):
        size = self.count[axis]
        pairs = [(start, (start + step) % size) for start in range(size)]
        if axis == "seq":
            pairs = [self.seq_pair(*pair) for pair in pairs]
        if axis in ("a", "b"):
            y_count, x_count = self.count["y"], self.count["x"]
            pairs = []
            for y in range(y_count):
                for x in range(x_count):
                    for core in range(2):
                        along_x = (axis == "a") != (self.mixed and core == 1)
                        new_y = y if along_x else (y + step) % y_count
                        new_x = (x + step) % x_count if along_x else x
                        pairs.append(
                            ((y * x_count + x) * 2 + core, (new_y * x_count + new_x) * 2 + core)
                        )
            return lax.ppermute(block, ("y", "x", "core"), pairs)
        return lax.ppermute(block, self.names.get(axis, axis), pairs)

    def after(self, axis, step):
        return lax.rem(self.index[axis] + step, self.count[axis])

    def blocks_for(self, core):
        y_count, x_count = self.count["y"], self.count["x"]
        numbers = []
        for b_step in [*self.steps("b"), 0]:
            for a_step in [*self.steps("a"), 0]:
                y = lax.rem(self.index["y"] + b_step, y_count)
                x = lax.rem(self.index["x"] + a_step, x_count)
                if self.mixed:
                    y = jnp.where(core == 1, lax.rem(self.index["y"] + a_step, y_count), y)
                    x = jnp.where(core == 1, lax.rem(self.index["x"] + b_step, x_count), x)
                numbers.append((y * x_count + x) * 2 + core)
        return numbers

    def steps(self, axis):
        return range(1, self.count[axis])


def packed(shard):
    rows, columns = shard.shape
    blocks = shard.reshape(rows // columns, columns, columns)
    return blocks.transpose(1, 0, 2).reshape(columns, rows)


def gather_t_turned(place, shard):
    return jnp.stack([shard] + [place.turn(shard, "t", step) for step in place.steps("t")])


def gather_t(place, shard):
    return lax.all_gather(shard, TENSOR, axis=0)


def gather_a(place, stack):
    return jnp.concatenate([stack] + [place.turn(stack, "a", step) for step in place.steps("a")])


def gather_b(place, stack):
    return [stack] + [place.turn(stack, "b", step) for step in place.steps("b")]


def gather_core(place, stacks):
    return stacks + [place.turn(stack, "core", 1) for stack in stacks]


def assemble(place, stacks, targets, turned=False):
    counts, dp_count, t_count = place.count, place.dp_count, place.count["t"]
    dtype = stacks[0].dtype
    shard_shape = stacks[0].shape[1:]
    rows, columns = shard_shape[-2:]
    shapes, copy_counts = [], 0
    for target in targets:
        if target[0] == "rows":
            shapes.append((target[2], target[3] * dp_count, columns * t_count))
            copy_counts += dp_count * t_count
        elif target[0] == "columns":
            aligned = columns % LANES == 0
            shape = (rows * t_count, columns * dp_count)
            shapes.append(shape if aligned else (dp_count, rows * t_count, columns))
            copy_counts += dp_count * t_count
        elif target[0] == "packed":
            aligned = rows % LANES == 0
            shape = (columns * t_count, rows * dp_count)
            shapes.append(shape if aligned else (dp_count, t_count, rows, columns))
            copy_counts += dp_count * t_count * (columns // rows if aligned else 1)
        else:
            shapes.append((dp_count, target[2], columns))
            copy_counts += dp_count

    def kernel(meta_ref, *refs):
        stack_refs = refs[: len(stacks)]
        out_refs = refs[len(stacks) : len(stacks) + len(targets)]
        sem = refs[-1]
        copies = []

        def send(source, target):
            copy = pltpu.make_async_copy(source, target, sem.at[len(copies)])
            copy.start()
            copies.append(copy)

        b_count = counts["b"]
        for number, stack_ref in enumerate(stack_refs):
            other, b_step = number // b_count, number % b_count
            core = lax.rem(meta_ref[2] + other, 2)
            for a_step in range(counts["a"]):
                y_spot = lax.rem(meta_ref[0] - b_step + counts["y"], counts["y"])
                x_spot = lax.rem(meta_ref[1] - a_step + counts["x"], counts["x"])
                if place.mixed:
                    y_other = lax.rem(meta_ref[0] - a_step + counts["y"], counts["y"])
                    x_other = lax.rem(meta_ref[1] - b_step + counts["x"], counts["x"])
                    y_spot = jnp.where(core == 1, y_other, y_spot)
                    x_spot = jnp.where(core == 1, x_other, x_spot)
                dp_spot = (y_spot * counts["x"] + x_spot) * 2 + core
                for t_step in range(t_count):
                    t_spot = lax.rem(meta_ref[3] - t_step + t_count, t_count) if turned else t_step
                    shard_ref = stack_ref.at[a_step * t_count + t_step]
                    for target, out_ref in zip(targets, out_refs):
                        t_columns = pl.ds(pl.multiple_of(t_spot * columns, columns), columns)
                        if target[0] == "rows":
                            first, depth, count = target[1:]
                            source = shard_ref.at[first : first + depth, 0:count, :]
                            here = pl.ds(pl.multiple_of(dp_spot * count, count), count)
                            send(source, out_ref.at[:, here, t_columns])
                        elif target[0] == "columns":
                            here = pl.ds(pl.multiple_of(t_spot * rows, rows), rows)
                            if columns % LANES == 0:
                                there = pl.ds(pl.multiple_of(dp_spot * columns, columns), columns)
                                send(shard_ref, out_ref.at[here, there])
                            else:
                                send(shard_ref, out_ref.at[dp_spot, here, :])
                        elif target[0] == "packed":
                            if rows % LANES == 0:
                                there = pl.ds(pl.multiple_of(dp_spot * rows, rows), rows)
                                for part in range(columns // rows):
                                    here = pl.ds(
                                        pl.multiple_of(t_spot * columns + part * rows, rows), rows
                                    )
                                    send(
                                        shard_ref.at[target[1], :, part * rows : (part + 1) * rows],
                                        out_ref.at[here, there],
                                    )
                            else:
                                send(shard_ref.at[target[1]], out_ref.at[dp_spot, t_spot])
                        elif t_step == 0:
                            first_row, count = target[1:]
                            send(shard_ref.at[0, first_row : first_row + count, :], out_ref.at[dp_spot])
        for copy in copies:
            copy.wait()

    meta = jnp.stack([place.index[axis] for axis in ("y", "x", "core", "t")]).astype(jnp.int32)
    results = pl.pallas_call(
        kernel,
        grid_spec=pltpu.PrefetchScalarGridSpec(
            num_scalar_prefetch=1,
            grid=(),
            in_specs=[pl.BlockSpec(memory_space=pl.ANY)] * len(stacks),
            out_specs=[pl.BlockSpec(memory_space=pltpu.VMEM)] * len(targets),
            scratch_shapes=[pltpu.SemaphoreType.DMA((copy_counts,))],
        ),
        out_shape=[jax.ShapeDtypeStruct(shape, dtype) for shape in shapes],
        compiler_params=pltpu.CompilerParams(vmem_limit_bytes=20 * 2**20),
        name="assemble",
    )(meta, *stacks)
    finished = []
    for target, whole in zip(targets, results):
        if target[0] == "columns" and columns % LANES:
            whole = whole.transpose(1, 0, 2).reshape(rows * t_count, columns * dp_count)
        if target[0] == "packed" and rows % LANES:
            whole = whole.reshape(dp_count, t_count, rows, columns // rows, rows)
            whole = whole.transpose(1, 3, 2, 0, 4).reshape(columns * t_count, rows * dp_count)
        finished.append(whole)
    return finished


def sent_order(place, width):
    core = place.index["core"]
    numbers = jnp.stack(place.blocks_for(1 - core) + place.blocks_for(core))
    block = width // place.dp_count
    sources = (numbers[:, None] * block + jnp.arange(block)[None, :]).reshape(1, width)
    return (jnp.arange(width)[:, None] == sources).astype(jnp.bfloat16)


def other_terms(place, pairs):
    result = []
    for inputs, grads in pairs:
        product = dot_f32(inputs[:, : inputs.shape[1] // 2], grads, TN).astype(jnp.bfloat16)
        result.append((inputs, grads, place.turn(product, "core", 1)))
    return result


def chip_terms(place, group):
    result = []
    for inputs, grads, other in group:
        half = inputs.shape[1] // 2
        step_rows = half // place.count["b"]
        terms = []
        for number in range(place.count["b"]):
            columns = slice(half + number * step_rows, half + (number + 1) * step_rows)
            rows = slice(number * step_rows, (number + 1) * step_rows)
            term = dot_f32(inputs[:, columns], grads, TN) + other[rows].astype(jnp.float32)
            terms.append(term.astype(jnp.bfloat16))
        result.append(terms)
    return result


def send_b(place, group):
    return [
        [place.turn(term, "b", step) for term, step in zip(terms, place.steps("b"))] + [terms[-1]]
        for terms in group
    ]


def added(arrays):
    total = arrays[0].astype(jnp.float32)
    for array in arrays[1:]:
        total = total + array.astype(jnp.float32)
    return total


def messages_a(place, group):
    result = []
    for arrived in group:
        step_rows = arrived[0].shape[0] // place.count["a"]
        messages = []
        for number in range(place.count["a"] - 1):
            rows = slice(number * step_rows, (number + 1) * step_rows)
            messages.append(added([one[rows] for one in arrived]).astype(jnp.bfloat16))
        result.append((messages, arrived))
    return result


def send_a(place, group):
    return [
        kept + [place.turn(message, "a", step) for message, step in zip(messages, place.steps("a"))]
        for messages, kept in group
    ]


def last_rows(kept):
    rows = kept[-1].shape[0]
    return added([one[-rows:] for one in kept])


def by_tensor(total, count):
    width = total.shape[1] // count
    return [total[:, number * width : (number + 1) * width] for number in range(count)]


def tensor_blocks(place, group):
    count = place.count["t"]
    blocks = [[] for _ in range(count)]
    for depth, kept in group:
        total = last_rows(kept).astype(jnp.bfloat16)
        for part in by_tensor(total, depth):
            for number, block in enumerate(by_tensor(part, count)):
                blocks[number].append(block)
    return jnp.stack([jnp.stack(block) for block in blocks])


def reduce_t(stack):
    return lax.psum_scatter(stack, TENSOR, scatter_dimension=0)


def reduce_t_vectors(place, kept, vectors):
    count = place.count["t"]
    total = last_rows(kept).astype(jnp.bfloat16)
    vector_count, columns = vectors.shape[0], total.shape[1] // count
    extra_rows = -(-vectors.size // (count * columns) // 16) * 16 if vectors.size else 0
    extra_rows = max(extra_rows, 16)
    width = vectors.shape[1] // count
    blocks = []
    for block, part in zip(by_tensor(total, count), by_tensor(vectors, count)):
        flat = part.astype(jnp.bfloat16).reshape(1, -1)
        flat = jnp.pad(flat, ((0, 0), (0, extra_rows * columns - flat.shape[1])))
        blocks.append(jnp.concatenate([block, flat.reshape(extra_rows, columns)]))
    result = lax.psum_scatter(jnp.stack(blocks), TENSOR, scatter_dimension=0)
    flat = result[-extra_rows:].reshape(-1)[: vector_count * width]
    return (result[:-extra_rows], flat.reshape(vector_count, width).astype(jnp.float32))


def reduce_vectors_core(place, columns):
    half = columns.shape[1] // 2
    total = columns[:, half:] + place.turn(columns[:, :half], "core", 1)
    return total


def reduce_vectors(place, total, axis):
    width = total.shape[1] // place.count[axis]
    arrived = total[:, -width:]
    for number, step in enumerate(place.steps(axis)):
        arrived = arrived + place.turn(total[:, number * width : (number + 1) * width], axis, step)
    return arrived


def clip_pairs(micro, z_count, step):
    return [
        (core * z_count + z, (z // micro) * z_count + micro * core + (step + z) % micro)
        for core in range(2)
        for z in range(z_count)
    ]


def clip_blocks(place, blocks):
    micro, z_here = blocks.shape[0], place.index["z"]
    return [
        lax.dynamic_index_in_dim(blocks, lax.rem(z_here + step, micro), 0, keepdims=False)
        for step in range(micro)
    ]


def to_clip(place, blocks):
    micro, z_count = len(blocks), place.count["z"]
    return [
        lax.ppermute(block, ("core", "z"), clip_pairs(micro, z_count, step))
        for step, block in enumerate(blocks)
    ]


def ordered_clip(place, arrived):
    micro, z_here = len(arrived), place.index["z"]
    stack = jnp.stack(arrived)
    ordered = [
        lax.dynamic_index_in_dim(stack, lax.rem(z_here - spot + micro, micro), 0, keepdims=False)
        for spot in range(micro)
    ]
    return jnp.concatenate(ordered, axis=0)


def own_blocks(place, rows_in, micro):
    z_here = place.index["z"]
    blocks = rows_in.reshape(micro, -1, rows_in.shape[-1])
    return [
        lax.dynamic_index_in_dim(blocks, lax.rem(z_here - step + micro, micro), 0, keepdims=False)
        for step in range(micro)
    ]


def from_clip(place, blocks):
    micro, z_count = len(blocks), place.count["z"]
    arrived = []
    for step, block in enumerate(blocks):
        pairs = [(end, start) for start, end in clip_pairs(micro, z_count, step)]
        arrived.append(lax.ppermute(block, ("core", "z"), pairs))
    return arrived


def own_clips(place, arrived):
    micro, z_here = len(arrived), place.index["z"]
    stack = jnp.stack(arrived)
    return jnp.stack(
        [
            lax.dynamic_index_in_dim(
                stack, lax.rem(number - lax.rem(z_here, micro) + micro, micro), 0, keepdims=False
            )
            for number in range(micro)
        ]
    )


def all_rows(place, own):
    return [own] + [place.turn(own, "seq", step) for step in place.steps("seq")]


def own_sum(place, parts):
    total = parts[0].astype(jnp.float32)
    for part, step in zip(parts[1:], place.steps("seq")):
        total = total + place.turn(part, "seq", step).astype(jnp.float32)
    return total


def neighbour_rows(place, rows_in, step):
    count = place.count["seq"]
    pairs = [
        place.seq_pair(start, start + step) for start in range(count) if 0 <= start + step < count
    ]
    return lax.ppermute(rows_in, place.names["seq"], pairs)


def feed_up(inputs, up_weight, up_bias, gain_row, shift_row):
    normed, normal, inverse = norm_rows(inputs, gain_row, shift_row)
    normed = normed.astype(jnp.bfloat16)
    upper_rows = matmul(normed, up_weight) + up_bias
    logistic = sigmoid(upper_rows)
    hidden = (upper_rows * logistic).astype(jnp.bfloat16)
    slope = swish_slope(upper_rows, logistic).astype(jnp.bfloat16)
    return (hidden, (normal, inverse, normed, slope))


def feed_back_down(grad_result, stored, down_weight):
    grad_low = grad_result.astype(jnp.bfloat16)
    grad_hidden = dot_f32(grad_low, down_weight, NT)
    grad_upper = (grad_hidden * stored[3].astype(jnp.float32)).astype(jnp.bfloat16)
    up_bias_grad = jnp.sum(grad_upper.astype(jnp.float32), axis=0)
    down_bias_grad = jnp.sum(grad_low.astype(jnp.float32), axis=0)
    return (grad_low, grad_upper, up_bias_grad, down_bias_grad)


def body(
    frames,
    cotangent,
    clip_valid,
    frame_counts,
    rel_rows,
    first_up,
    first_down,
    attend_in,
    attend_out,
    pointwise_in,
    pointwise_out,
    second_up,
    second_down,
    vectors,
    distance,
):
    place = Place()
    micro, _, width = frames.shape
    ratio_rows = FF // width
    attend_base = 3 + ratio_rows
    conv_base = attend_base + 5
    second_base = conv_base + 4
    final_base = second_base + 3 + ratio_rows
    taps_base = final_base + 2
    scale = HEAD_DIM ** (-0.5)
    order = sent_order(place, width)

    def sent(rows_low):
        return matmul(rows_low, order).astype(jnp.bfloat16)

    up_rows, up_columns = first_up.shape
    vector_rows = 16
    vector_parts = up_columns // vectors.shape[1]
    padded_vectors = jnp.pad(vectors, ((0, vector_rows * vector_parts - vectors.shape[0]), (0, 0)))
    vector_shard = (
        padded_vectors.reshape(vector_parts, vector_rows, -1).transpose(1, 0, 2).reshape(vector_rows, -1)
    )
    shard_up_one = jnp.concatenate([first_up, vector_shard], axis=0)[None]
    shard_mix = jnp.concatenate(
        [attend_in, packed(attend_out)[None], pointwise_in, packed(pointwise_out)[None]]
    )

    own_facts = jnp.stack([clip_valid, frame_counts])
    up_one = gather_t_turned(place, shard_up_one)
    up_one, first_down, own_facts = fence(up_one, first_down, own_facts)
    up_one = gather_a(place, up_one)
    down_one = gather_t(place, first_down)
    other_facts = place.turn(own_facts, "core", 1)
    up_one, frames, shard_mix = fence(up_one, frames, shard_mix)
    up_one = gather_b(place, up_one)
    rows_low = to_clip(place, clip_blocks(place, frames))
    down_one = gather_a(place, down_one)
    both_mix = gather_t(place, shard_mix)
    up_one, down_one, second_up = fence(up_one, down_one, second_up)
    up_one = gather_core(place, up_one)
    down_one = gather_b(place, down_one)
    up_one, down_one, second_up = fence(up_one, down_one, second_up)
    attend_mix = gather_a(place, both_mix[:, : attend_in.shape[0] + 1])
    point_mix = both_mix[:, attend_in.shape[0] + 1 :]
    up_two = gather_t(place, second_up[None])
    up_one, vector_slabs = assemble(
        place, up_one, [("rows", 0, 1, up_rows), ("slabs", up_rows, vector_rows)], turned=True
    )
    up_one = up_one[0]
    vector_wide = vector_slabs.reshape(place.dp_count, vector_rows, vector_parts, -1)
    vector_wide = vector_wide.transpose(2, 1, 0, 3).reshape(vector_rows * vector_parts, width)
    vector_wide = vector_wide[: vectors.shape[0]].astype(jnp.float32)

    rows_in = ordered_clip(place, rows_low).astype(jnp.float32)
    row_count = rows_in.shape[0]
    z_here = place.index["z"]
    facts = jnp.where(z_here // micro == place.index["core"], own_facts, other_facts)
    facts = lax.dynamic_index_in_dim(facts, lax.rem(z_here, micro), 1, keepdims=False)
    valid_flag = (facts[0] > 0).astype(jnp.float32)
    first_row = place.index["seq"] * row_count
    live = ((first_row + jnp.arange(row_count)) < facts[1]).astype(jnp.float32)[:, None]
    meta = jnp.stack([place.index["seq"] * (row_count // LANES), facts[1], place.index["seq"]])
    meta = meta.astype(jnp.int32)
    pick_rows = (rel_rows[:, None] == jnp.arange(OFFSETS)[None, :]).astype(jnp.bfloat16)
    table = wide_table(matmul(pick_rows, distance).astype(jnp.bfloat16))

    one_hidden, one_kept = feed_up(
        rows_in,
        up_one,
        vector_wide[2 : 2 + ratio_rows].reshape(FF),
        vector_wide[0],
        vector_wide[1],
    )
    (down_one, attend_mix, point_mix, second_down, one_hidden, one_kept, table) = fence(
        down_one, attend_mix, point_mix, second_down, one_hidden, one_kept, table
    )
    down_one = gather_core(place, down_one)
    attend_mix = gather_b(place, attend_mix)
    point_mix = gather_a(place, point_mix)
    down_two = gather_t(place, second_down)
    (down_one,) = assemble(place, down_one, [("columns",)])
    after_one = rows_in + 0.5 * (matmul(one_hidden, down_one) + vector_wide[2 + ratio_rows])
    attend_normed, attend_normal, attend_inverse = norm_rows(
        after_one, vector_wide[attend_base], vector_wide[attend_base + 1]
    )
    attend_normed = attend_normed.astype(jnp.bfloat16)
    (attend_mix, point_mix, up_two, after_one, attend_normed, attend_normal, attend_inverse) = fence(
        attend_mix, point_mix, up_two, after_one, attend_normed, attend_normal, attend_inverse
    )
    attend_mix = gather_core(place, attend_mix)
    point_mix = gather_b(place, point_mix)
    up_two = gather_a(place, up_two)
    attend_mix, attend_back_weight = assemble(place, attend_mix, [("rows", 0, 3, up_rows), ("packed", 3)])
    queries = (matmul(attend_normed, attend_mix[0]) + vector_wide[attend_base + 2]).astype(jnp.bfloat16)
    queries = (queries.astype(jnp.float32) * scale).astype(jnp.bfloat16)
    own_keys = matmul(attend_normed, attend_mix[1]).astype(jnp.bfloat16)
    own_values = (matmul(attend_normed, attend_mix[2]) + vector_wide[attend_base + 3]).astype(jnp.bfloat16)
    key_rows, value_rows = all_rows(place, own_keys), all_rows(place, own_values)
    (point_mix, up_two, down_two, cotangent, queries, key_rows, value_rows) = fence(
        point_mix, up_two, down_two, cotangent, queries, key_rows, value_rows
    )
    point_mix = gather_core(place, point_mix)
    up_two = gather_b(place, up_two)
    down_two = gather_a(place, down_two)
    cot_low = to_clip(place, clip_blocks(place, cotangent))
    context, levels = attend(meta, queries, key_rows, value_rows, table)
    (point_mix, up_two, down_two, context, levels, after_one) = fence(
        point_mix, up_two, down_two, context, levels, after_one
    )
    down_two = gather_b(place, down_two)
    up_two = gather_core(place, up_two)
    point_mix, point_back = assemble(place, point_mix, [("rows", 0, 2, up_rows), ("packed", 2)])
    after_two = after_one + matmul(context, attend_back_weight) + vector_wide[attend_base + 4]
    conv_normed, conv_normal, conv_inverse = norm_rows(
        after_two, vector_wide[conv_base], vector_wide[conv_base + 1]
    )
    conv_normed = conv_normed.astype(jnp.bfloat16)
    linear = matmul(conv_normed, point_mix[0])
    logistic = sigmoid(matmul(conv_normed, point_mix[1]))
    gated = linear * logistic * live
    taps = vector_wide[taps_base : taps_base + KERNEL]
    before = neighbour_rows(place, gated[-HALO:], 1)
    deep_gain, deep_shift = vector_wide[conv_base + 2], vector_wide[conv_base + 3]
    depth_out, activated = convolve(before, gated, taps, deep_gain, deep_shift)
    after_three = after_two + matmul(activated, point_back)
    (up_two, down_two, cot_low, after_three, depth_out, activated) = fence(
        up_two, down_two, cot_low, after_three, depth_out, activated
    )
    down_two = gather_core(place, down_two)
    (up_two,) = assemble(place, up_two, [("rows", 0, 1, up_rows)])
    up_two = up_two[0]
    two_hidden, two_kept = feed_up(
        after_three,
        up_two,
        vector_wide[second_base + 2 : second_base + 2 + ratio_rows].reshape(FF),
        vector_wide[second_base],
        vector_wide[second_base + 1],
    )
    (down_two, two_hidden, two_kept, up_two) = fence(down_two, two_hidden, two_kept, up_two)
    (down_two,) = assemble(place, down_two, [("columns",)])
    two_out = matmul(two_hidden, down_two) + vector_wide[second_base + 2 + ratio_rows]
    after_four = after_three + 0.5 * two_out
    final_rows, final_normal, final_inverse = norm_rows(
        after_four, vector_wide[final_base], vector_wide[final_base + 1]
    )
    row_out = jnp.where(valid_flag > 0, final_rows, rows_in).astype(jnp.bfloat16)
    rows_cot = ordered_clip(place, cot_low).astype(jnp.float32)
    grad_four, final_gain_grad, final_shift_grad = norm_back(
        rows_cot * valid_flag, final_normal, final_inverse, vector_wide[final_base]
    )
    grad_low, grad_upper, two_up_bias, two_down_bias = feed_back_down(
        0.5 * grad_four, two_kept, down_two
    )
    sum_down_two = other_terms(place, [(sent(grad_low), two_hidden)])
    (sum_down_two, grad_four, grad_upper, row_out) = fence(sum_down_two, grad_four, grad_upper, row_out)
    sum_down_two = send_b(place, chip_terms(place, sum_down_two))
    frames_out = from_clip(place, own_blocks(place, row_out, micro))
    sum_up_two = other_terms(place, [(sent(two_kept[2]), grad_upper)])
    grad_normed = dot_f32(grad_upper, up_two, NT)
    grad_two_in, two_gain, two_shift = norm_back(
        grad_normed, two_kept[0], two_kept[1], vector_wide[second_base]
    )
    grad_three = grad_four + grad_two_in
    conv_low = grad_three.astype(jnp.bfloat16)
    deep_norm, deep_normal, deep_inverse = norm_rows(depth_out, deep_gain, deep_shift)
    grad_deep = dot_f32(conv_low, point_back, NT) * swish_slope(deep_norm, sigmoid(deep_norm))
    grad_depth, deep_gain_grad, deep_shift_grad = norm_back(
        grad_deep, deep_normal, deep_inverse, deep_gain
    )
    after = neighbour_rows(place, grad_depth[:HALO], -1)
    (sum_down_two, sum_up_two, grad_three, conv_low, grad_depth, after, frames_out) = fence(
        sum_down_two, sum_up_two, grad_three, conv_low, grad_depth, after, frames_out
    )
    sum_down_two = send_a(place, messages_a(place, sum_down_two))
    sum_up_two = send_b(place, chip_terms(place, sum_up_two))
    grad_pair, tap_grads = convolve_back(
        meta, grad_depth, after, before, gated, taps, linear, logistic
    )
    (sum_down_two, sum_up_two, grad_pair) = fence(sum_down_two, sum_up_two, grad_pair)
    sum_down_two = reduce_t(tensor_blocks(place, [(1, sum_down_two[0])]))
    sum_up_two = send_a(place, messages_a(place, sum_up_two))
    sum_point = other_terms(
        place,
        [
            (sent(conv_normed), grad_pair),
            (sent(conv_low), activated),
        ],
    )
    grad_conv_normed = dot_f32(grad_pair[:, :width], point_mix[0], NT)
    grad_conv_normed = grad_conv_normed + dot_f32(grad_pair[:, width:], point_mix[1], NT)
    grad_conv_in, conv_gain_grad, conv_shift_grad = norm_back(
        grad_conv_normed, conv_normal, conv_inverse, vector_wide[conv_base]
    )
    grad_two = grad_three + grad_conv_in
    attend_low = grad_two.astype(jnp.bfloat16)
    grad_context = dot_f32(attend_low, attend_back_weight, NT).astype(jnp.bfloat16)
    (sum_up_two, sum_point, grad_two, attend_low, grad_context) = fence(
        sum_up_two, sum_point, grad_two, attend_low, grad_context
    )
    sum_up_two = reduce_t(tensor_blocks(place, [(1, sum_up_two[0])]))
    sum_point = send_b(place, chip_terms(place, sum_point))
    grad_queries, part_keys, part_values, grad_table = attend_back(
        meta, queries, key_rows, value_rows, table, grad_context, context, levels
    )
    (sum_point, grad_queries, part_keys, part_values, grad_table, sum_down_two) = fence(
        sum_point, grad_queries, part_keys, part_values, grad_table, sum_down_two
    )
    sum_point = send_a(place, messages_a(place, sum_point))
    grad_keys = own_sum(place, part_keys).astype(jnp.bfloat16)
    grad_values = own_sum(place, part_values).astype(jnp.bfloat16)
    sum_distance = jnp.dot(
        pick_rows.astype(jnp.float32).T, table_grad(grad_table), precision=lax.Precision.HIGHEST
    )
    sent_attend, sent_out = sent(attend_normed), sent(attend_low)
    (sum_point, sum_distance, grad_keys, grad_values, sum_up_two, sent_attend, sent_out) = fence(
        sum_point, sum_distance, grad_keys, grad_values, sum_up_two, sent_attend, sent_out
    )
    sum_attend = other_terms(
        place,
        [
            (sent_attend, jnp.concatenate([grad_queries, grad_keys, grad_values], axis=1)),
            (sent_out, context),
        ],
    )
    sum_distance = sum(
        [place.turn(sum_distance, "t", step) for step in place.steps("t")], sum_distance
    )
    sum_attend = chip_terms(place, sum_attend)
    sum_point = tensor_blocks(place, [(2, sum_point[0]), (1, sum_point[1])])
    grad_attend_normed = (
        dot_f32(grad_queries, attend_mix[0], NT)
        + dot_f32(grad_keys, attend_mix[1], NT)
        + dot_f32(grad_values, attend_mix[2], NT)
    )
    grad_attend_in, attend_gain_grad, attend_shift_grad = norm_back(
        grad_attend_normed, attend_normal, attend_inverse, vector_wide[attend_base]
    )
    grad_one = grad_two + grad_attend_in
    (sum_point, sum_attend, sum_distance, grad_one) = fence(sum_point, sum_attend, sum_distance, grad_one)
    sum_attend = send_b(place, sum_attend)
    sum_point = reduce_t(sum_point)
    grad_low, grad_upper, one_up_bias, one_down_bias = feed_back_down(0.5 * grad_one, one_kept, down_one)
    sent_low, sent_one = sent(grad_low), sent(one_kept[2])
    (sum_attend, grad_upper, sum_distance, sent_low, sent_one, one_up_bias) = fence(
        sum_attend, grad_upper, sum_distance, sent_low, sent_one, one_up_bias
    )
    sum_attend = send_a(place, messages_a(place, sum_attend))
    sum_down_one = other_terms(place, [(sent_low, one_hidden)])
    sum_up_one = other_terms(place, [(sent_one, grad_upper)])
    sum_down_one = chip_terms(place, sum_down_one)
    sum_distance = sum_distance + place.turn(sum_distance, "core", 1)
    sum_attend = tensor_blocks(place, [(3, sum_attend[0]), (1, sum_attend[1])])
    (sum_attend, sum_down_one, sum_up_one, grad_upper, sum_distance, sum_point) = fence(
        sum_attend, sum_down_one, sum_up_one, grad_upper, sum_distance, sum_point
    )
    sum_down_one = send_b(place, sum_down_one)
    sum_attend = reduce_t(sum_attend)
    sum_up_one = chip_terms(place, sum_up_one)
    sum_distance = sum(
        [place.turn(sum_distance, "b", step) for step in place.steps("b")], sum_distance
    )
    grad_normed = dot_f32(grad_upper, up_one, NT)
    grad_one_in, one_gain, one_shift = norm_back(grad_normed, one_kept[0], one_kept[1], vector_wide[0])
    grad_rows = grad_one + grad_one_in + (1.0 - valid_flag) * rows_cot

    grad_blocks = own_blocks(place, grad_rows.astype(jnp.bfloat16), micro)
    (sum_attend, sum_down_one, sum_up_one, grad_blocks, one_gain, one_shift, sum_distance) = fence(
        sum_attend, sum_down_one, sum_up_one, grad_blocks, one_gain, one_shift, sum_distance
    )
    sum_down_one = send_a(place, messages_a(place, sum_down_one))
    sum_up_one = send_b(place, sum_up_one)
    frames_grad = from_clip(place, grad_blocks)
    sum_distance = sum(
        [place.turn(sum_distance, "a", step) for step in place.steps("a")], sum_distance
    )

    def column_sum(rows):
        return jnp.sum(rows.astype(jnp.float32), axis=0)

    vector_part = jnp.concatenate(
        [
            jnp.stack([one_gain, one_shift]),
            one_up_bias.reshape(ratio_rows, width),
            jnp.stack(
                [
                    one_down_bias,
                    attend_gain_grad,
                    attend_shift_grad,
                    column_sum(grad_queries),
                    column_sum(grad_values),
                    column_sum(attend_low),
                    conv_gain_grad,
                    conv_shift_grad,
                    deep_gain_grad,
                    deep_shift_grad,
                    two_gain,
                    two_shift,
                ]
            ),
            two_up_bias.reshape(ratio_rows, width),
            jnp.stack([two_down_bias, final_gain_grad, final_shift_grad]),
            tap_grads[:KERNEL],
        ],
        axis=0,
    )
    vector_part = jnp.dot(vector_part, order.astype(jnp.float32), precision=lax.Precision.HIGHEST)
    sum_vectors = reduce_vectors_core(place, vector_part)
    (sum_up_one, sum_down_one, sum_vectors, frames_grad) = fence(
        sum_up_one, sum_down_one, sum_vectors, frames_grad
    )
    sum_up_one = send_a(place, messages_a(place, sum_up_one))
    sum_down_one = reduce_t(tensor_blocks(place, [(1, sum_down_one[0])]))
    sum_vectors = reduce_vectors(place, sum_vectors, "b")
    sum_vectors = reduce_vectors(place, sum_vectors, "a")
    (sum_up_one, sum_vectors) = fence(sum_up_one, sum_vectors)
    sum_up_one, grad_vectors = reduce_t_vectors(place, sum_up_one[0], sum_vectors)
    wide = jnp.float32
    return (
        own_clips(place, frames_out),
        own_clips(place, frames_grad),
        sum_up_one.astype(wide),
        sum_down_one[0].T.astype(wide),
        sum_attend[:3].astype(wide),
        sum_attend[3].T.astype(wide),
        sum_point[:2].astype(wide),
        sum_point[2].T.astype(wide),
        sum_up_two[0].astype(wide),
        sum_down_two[0].T.astype(wide),
        grad_vectors,
        sum_distance,
    )


def solution(mesh):
    dp_count, tensor_count = mesh.shape["dp"], mesh.shape["tensor"]

    def program(*arrays):
        group = 2 * (arrays[0].shape[0] // dp_count)
        parted = Mesh(
            mesh.devices.reshape(dp_count // 4, 2, 2, tensor_count // group, group),
            ("y", "x", "core", "far", "z"),
        )
        dp, tensor = ("y", "x", "core"), TENSOR
        return jax.shard_map(
            body,
            mesh=parted,
            in_specs=(
                P(dp, tensor, None),
                P(dp, tensor, None),
                P(dp),
                P(dp),
                P(),
                P(dp, tensor),
                P(tensor, dp),
                P(None, dp, tensor),
                P(tensor, dp),
                P(None, dp, tensor),
                P(tensor, dp),
                P(dp, tensor),
                P(tensor, dp),
                P(None, dp),
                P(),
            ),
            out_specs=(
                P(dp, tensor, None),
                P(dp, tensor, None),
                P(dp, tensor),
                P(tensor, dp),
                P(None, dp, tensor),
                P(tensor, dp),
                P(None, dp, tensor),
                P(tensor, dp),
                P(dp, tensor),
                P(tensor, dp),
                P(None, dp + tensor),
                P(),
            ),
            check_vma=False,
        )(*arrays)

    return program
```

```python
import functools

import jax
import jax.numpy as jnp
from jax import lax
from jax.experimental import pallas as pl
from jax.experimental.pallas import tpu as pltpu
from jax.sharding import Mesh
from jax.sharding import PartitionSpec as P

HEADS = 16
HEAD_DIM = 64
FF = 4096
KERNEL = 31
LEFT = 64
OFFSETS = 73
EPSILON = 1e-05

LANES = 128
SOFT_ROWS = 32
SLOPE_ROWS = 16
RIGHT = OFFSETS - 1 - LEFT
NT = (((1,), (1,)), ((), ()))
NN = (((1,), (0,)), ((), ()))
TN = (((0,), (0,)), ((), ()))


def dot_f32(left_side, right_side, dims):
    return lax.dot_general(left_side, right_side, dims, preferred_element_type=jnp.float32)


def band_distance():
    shape = (LANES, 3 * LANES)
    return (
        lax.broadcasted_iota(jnp.int32, shape, 1)
        - LANES
        - lax.broadcasted_iota(jnp.int32, shape, 0)
    )


LAST_ROWS = 8


def add_band(score_ref, half, source, distance, block, number):
    rows = slice(number * LANES, (number + 1) * LANES)
    own = source[rows]
    left_col = own[:, 2 * LANES - LEFT : 2 * LANES - LEFT + 1]
    right_col = own[:, RIGHT : RIGHT + 1]
    rolled = pltpu.roll(own - right_col, LANES, 1, stride=1, stride_axis=0)
    window = pl.multiple_of(block * LANES, LANES)
    near = rolled[:LEFT, :LANES] + (right_col - left_col)[:LEFT]
    near = jnp.where(distance[:LEFT, :LANES] > -LEFT, near, 0.0)
    score_ref[half, number * LANES : number * LANES + LEFT, pl.ds(window, LANES)] += near
    score_ref[half, rows, pl.ds(window + LANES, LANES)] += rolled[:, LANES:]
    last = LANES - LAST_ROWS
    after = jnp.where(distance[last:, 2 * LANES :] < RIGHT, rolled[last:, :LANES], 0.0)
    score_ref[half, number * LANES + last : (number + 1) * LANES, pl.ds(window + 2 * LANES, LANES)] += after


def in_half(shape, half):
    lanes = lax.broadcasted_iota(jnp.int32, shape, 1)
    return (lanes < HEAD_DIM) if half == 0 else (lanes >= HEAD_DIM)


def spare_lane(shape):
    return lax.rem(lax.broadcasted_iota(jnp.int32, shape, 1), HEAD_DIM)


def key_marks(meta_ref, key_count, blocks):
    shape = (key_count, LANES)
    spare, keys = spare_lane(shape), lax.broadcasted_iota(jnp.int32, shape, 0)
    before = keys < (meta_ref[0] + spare // 2) * LANES
    side = jnp.where(lax.rem(spare, 2) == 0, before.astype(jnp.float32), 1.0 - before.astype(jnp.float32))
    dead = jnp.where(keys < meta_ref[1], 0.0, -1e30)
    ones = (spare < 2 * blocks + 4).astype(jnp.float32)
    marks = jnp.where(spare < 2 * blocks, side, jnp.where(spare == 2 * blocks, dead, ones))
    return marks.astype(jnp.bfloat16)


def in_parts(column):
    parts = []
    for _ in range(3):
        part = column.astype(jnp.bfloat16).astype(jnp.float32)
        parts.append(part)
        column = column - part
    return parts


def with_marks(rows_half, half, columns_of):
    square = (LANES, LANES)
    spare, mine = spare_lane(square), in_half(square, half)
    parts = []
    for number in range(rows_half.shape[0] // LANES):
        own = rows_half[number * LANES : (number + 1) * LANES].astype(jnp.float32)
        marks = jnp.zeros(square, jnp.float32)
        for place, column in columns_of(number):
            marks = jnp.where(spare == place, column, marks)
        parts.append(jnp.where(mine, own, marks).astype(jnp.bfloat16))
    return jnp.concatenate(parts, axis=0)


def marked_queries(q_half, half, source, extra, blocks):
    def columns_of(number):
        rows = slice(number * LANES, (number + 1) * LANES)
        own = source[rows]
        columns = [
            (2 * number, own[:, 2 * LANES - LEFT : 2 * LANES - LEFT + 1]),
            (2 * number + 1, own[:, RIGHT : RIGHT + 1]),
            (2 * blocks, 1.0),
        ]
        return columns + [(2 * blocks + 1 + place, part[rows]) for place, part in enumerate(extra)]

    return with_marks(q_half, half, columns_of)


def key_spot(meta_ref, step, count, row_count):
    spot = lax.rem(meta_ref[2] - step + count, count)
    return pl.ds(pl.multiple_of(spot * row_count, row_count), row_count)


def attend_kernel(count, meta_ref, q_ref, e_ref, *refs):
    key_refs, value_refs = refs[:count], refs[count : 2 * count]
    c_ref, lse_ref, score_ref, share_ref, marks_ref, k_ref, v_ref = refs[2 * count :]
    row_count, key_count = q_ref.shape[0], k_ref.shape[0]
    for step in range(count):
        k_ref[key_spot(meta_ref, step, count, row_count)] = key_refs[step][...]
        v_ref[key_spot(meta_ref, step, count, row_count)] = value_refs[step][...]
    blocks = row_count // LANES
    pair = pl.program_id(0)
    lanes = lax.broadcasted_iota(jnp.int32, (row_count, LANES), 1)
    distance = band_distance()

    @pl.when(pair == 0)
    def _():
        marks_ref[...] = key_marks(meta_ref, key_count, blocks)

    sources = []
    for half in range(2):
        mine = in_half((row_count, LANES), half)
        q_half = jnp.where(mine, q_ref[...], 0)
        source = dot_f32(q_half, e_ref[...], NT).astype(jnp.bfloat16).astype(jnp.float32)
        sources.append(source)
        queries = marked_queries(q_half, half, source, [], blocks)
        keys = jnp.where(in_half((key_count, LANES), half), k_ref[...], marks_ref[...])
        score_ref[half, :, LANES : LANES + key_count] = dot_f32(queries, keys, NT)
    result = None
    for half in range(2):
        inverses = []
        for number in range(blocks):
            rows = slice(number * LANES, (number + 1) * LANES)
            add_band(score_ref, half, sources[half], distance, meta_ref[0] + number, number)
            for first in range(number * LANES, (number + 1) * LANES, SOFT_ROWS):
                few = slice(first, first + SOFT_ROWS)
                scores = score_ref[half, few, LANES : LANES + key_count]
                peak = jnp.max(scores, axis=1, keepdims=True)
                grown = jnp.exp(scores - peak)
                total = jnp.sum(grown, axis=1, keepdims=True)
                share_ref[half, few] = grown.astype(jnp.bfloat16)
                inverses.append(1.0 / total)
                lse_ref[few] = jnp.where(
                    lanes[few] == 2 * pair + half, peak + jnp.log(total), lse_ref[few]
                )
        context = dot_f32(share_ref[half], v_ref[...], NN) * jnp.concatenate(inverses, axis=0)
        result = context if half == 0 else jnp.where(in_half(context.shape, 1), context, result)
    c_ref[...] = result.astype(jnp.bfloat16)


def attend_back_kernel(count, meta_ref, q_ref, e_ref, dc_ref, c_ref, lse_ref, *refs):
    key_refs, value_refs = refs[:count], refs[count : 2 * count]
    dq_ref, de_ref = refs[2 * count : 2 * count + 2]
    dk_refs, dv_refs = refs[2 * count + 2 : 3 * count + 2], refs[3 * count + 2 : 4 * count + 2]
    score_ref, grad_ref, share_ref, slope_ref, source_ref, wide_ref, marks_ref, k_ref, v_ref, turn_ref = refs[
        4 * count + 2 :
    ]
    row_count, key_count = q_ref.shape[0], k_ref.shape[0]
    for step in range(count):
        k_ref[key_spot(meta_ref, step, count, row_count)] = key_refs[step][...]
        v_ref[key_spot(meta_ref, step, count, row_count)] = value_refs[step][...]
    key_blocks, blocks = key_count // LANES, row_count // LANES
    pair = pl.program_id(0)
    lanes = lax.broadcasted_iota(jnp.int32, (row_count, LANES), 1)
    distance = band_distance()
    square = (LANES, LANES)
    flip = (
        lax.broadcasted_iota(jnp.int32, square, 0) + lax.broadcasted_iota(jnp.int32, square, 1)
        == LANES - 1
    ).astype(jnp.float32).astype(jnp.bfloat16)
    spots = lax.broadcasted_iota(jnp.int32, square, 1)

    @pl.when(pair == 0)
    def _():
        shape = (key_count, LANES)
        place = lax.broadcasted_iota(jnp.int32, shape, 1)
        edge = (meta_ref[0] + place // 2) * LANES
        key = lax.broadcasted_iota(jnp.int32, shape, 0)
        before = (key < edge).astype(jnp.float32)
        after = (key >= edge + LANES).astype(jnp.float32)
        wide_ref[:, LANES:] = jnp.where(lax.rem(place, 2) == 0, before, after).astype(jnp.bfloat16)
        for half in range(2):
            slope_ref[half, :, :LANES] = jnp.zeros((row_count, LANES), jnp.bfloat16)
            slope_ref[half, :, LANES + key_count :] = jnp.zeros((row_count, LANES), jnp.bfloat16)
        de_ref[...] = jnp.zeros(de_ref.shape, jnp.float32)
        marks_ref[0] = key_marks(meta_ref, key_count, blocks)
        marks_ref[1] = (spare_lane(shape) < 3).astype(jnp.float32).astype(jnp.bfloat16)

    wide_ref[:, :LANES] = k_ref[...]
    inner_all = dc_ref[...].astype(jnp.float32) * c_ref[...].astype(jnp.float32)
    sources, q_halves, dc_halves = [], [], []
    for half in range(2):
        mine, mine_keys = in_half((row_count, LANES), half), in_half((key_count, LANES), half)
        q_half = jnp.where(mine, q_ref[...], 0)
        dc_half = jnp.where(mine, dc_ref[...], 0)
        source = dot_f32(q_half, e_ref[...], NT).astype(jnp.bfloat16).astype(jnp.float32)
        inner = jnp.sum(jnp.where(mine, inner_all, 0.0), axis=1, keepdims=True)
        level = jnp.sum(
            jnp.where(lanes == 2 * pair + half, lse_ref[...], 0.0), axis=1, keepdims=True
        )
        queries = marked_queries(q_half, half, source, in_parts(-level), blocks)
        keys = jnp.where(mine_keys, k_ref[...], marks_ref[0])
        score_ref[half, :, LANES : LANES + key_count] = dot_f32(queries, keys, NT)
        inner_parts = in_parts(-inner)
        grads = with_marks(
            dc_half,
            half,
            lambda number, parts=inner_parts: [
                (place, part[number * LANES : (number + 1) * LANES])
                for place, part in enumerate(parts)
            ],
        )
        values = jnp.where(mine_keys, v_ref[...], marks_ref[1])
        grad_ref[half] = dot_f32(grads, values, NT)
        sources.append(source)
        q_halves.append(q_half)
        dc_halves.append(dc_half)
    grad_q = grad_k = grad_v = None
    for half in range(2):
        for number in range(blocks):
            rows = slice(number * LANES, (number + 1) * LANES)
            add_band(score_ref, half, sources[half], distance, meta_ref[0] + number, number)
            for first in range(number * LANES, (number + 1) * LANES, SLOPE_ROWS):
                few = slice(first, first + SLOPE_ROWS)
                shares = jnp.exp(score_ref[half, few, LANES : LANES + key_count])
                share_ref[half, few] = shares.astype(jnp.bfloat16)
                slope_ref[half, few, LANES : LANES + key_count] = (
                    shares * grad_ref[half, few]
                ).astype(jnp.bfloat16)
    for half in range(2):
        mine = in_half((row_count, LANES), half)
        slopes = slope_ref[half, :, LANES : LANES + key_count]
        wide = dot_f32(slopes, wide_ref[...], NN)
        before = wide[:, LANES:]
        for number in range(blocks):
            rows = slice(number * LANES, (number + 1) * LANES)
            window = pl.multiple_of((meta_ref[0] + number) * LANES, LANES)
            first, last = number * LANES, (number + 1) * LANES - LAST_ROWS
            near = slope_ref[half, first : first + LEFT, pl.ds(window, LANES)].astype(jnp.float32)
            near = jnp.where(distance[:LEFT, :LANES] > -LEFT, near, 0.0)
            final = slope_ref[half, last - 8 : last + 8, pl.ds(window + 2 * LANES, LANES)]
            final = final.astype(jnp.float32)[8:]
            final = jnp.where(distance[LANES - LAST_ROWS :, 2 * LANES :] < RIGHT, final, 0.0)
            middle = slope_ref[half, rows, pl.ds(window + LANES, LANES)]
            gap = jnp.zeros((LANES - LEFT - LAST_ROWS, LANES), jnp.float32)
            edges = jnp.concatenate([near, gap, final], axis=0)
            inner_sum = jnp.sum(edges, axis=1, keepdims=True)
            first_rows = lax.broadcasted_iota(jnp.int32, (LANES, 1), 0) < LEFT
            far_left = before[rows, 2 * number : 2 * number + 1] - jnp.where(first_rows, inner_sum, 0.0)
            far_right = before[rows, 2 * number + 1 : 2 * number + 2] - jnp.where(
                first_rows, 0.0, inner_sum
            )
            band = jnp.concatenate([edges.astype(jnp.bfloat16), middle], axis=1)
            turned = dot_f32(flip, band, NN)
            turned = pltpu.roll(turned, 1, 1, stride=1, stride_axis=0)
            turned = dot_f32(flip, turned.astype(jnp.bfloat16), NN)
            turned = jnp.concatenate(
                [
                    turned[:, :LANES] + jnp.where(spots == RIGHT, far_right, 0.0),
                    turned[:, LANES:] + jnp.where(spots == 0, far_left, 0.0),
                ],
                axis=1,
            )
            source_ref[half, rows] = turned.astype(jnp.bfloat16)
        q_part = wide[:, :LANES] + dot_f32(source_ref[half], e_ref[...], NN)
        k_part = dot_f32(q_halves[half], slopes, TN)
        v_part = dot_f32(dc_halves[half], share_ref[half], TN)
        de_ref[...] += dot_f32(q_halves[half], source_ref[half], TN)
        grad_q = q_part if half == 0 else jnp.where(mine, q_part, grad_q)
        grad_k = k_part if half == 0 else grad_k + k_part
        grad_v = v_part if half == 0 else grad_v + v_part
    dq_ref[...] = (grad_q * HEAD_DIM ** (-0.5)).astype(jnp.bfloat16)
    for grad, grad_refs in ((grad_k, dk_refs), (grad_v, dv_refs)):
        turn_ref[...] = grad.T
        for step in range(count):
            rows = key_spot(meta_ref, -step, count, row_count)
            grad_refs[step][...] = turn_ref[rows].astype(jnp.bfloat16)


def pair_spec(row_count):
    return pl.BlockSpec((row_count, LANES), lambda pair, meta: (0, pair))


def fixed_spec(row_count, column_count):
    return pl.BlockSpec((row_count, column_count), lambda pair, meta: (0, 0))


def attend(meta, queries, key_rows, value_rows, table):
    row_count, width = queries.shape
    count = len(key_rows)
    key_count = row_count * count
    return pl.pallas_call(
        functools.partial(attend_kernel, count),
        grid_spec=pltpu.PrefetchScalarGridSpec(
            num_scalar_prefetch=1,
            grid=(width // LANES,),
            in_specs=[pair_spec(row_count), fixed_spec(2 * LANES, LANES)]
            + [pair_spec(row_count)] * (2 * count),
            out_specs=[pair_spec(row_count), fixed_spec(row_count, LANES)],
            scratch_shapes=[
                pltpu.VMEM((2, row_count, key_count + 2 * LANES), jnp.float32),
                pltpu.VMEM((2, row_count, key_count), jnp.bfloat16),
                pltpu.VMEM((key_count, LANES), jnp.bfloat16),
                pltpu.VMEM((key_count, LANES), jnp.bfloat16),
                pltpu.VMEM((key_count, LANES), jnp.bfloat16),
            ],
        ),
        out_shape=[
            jax.ShapeDtypeStruct((row_count, width), jnp.bfloat16),
            jax.ShapeDtypeStruct((row_count, LANES), jnp.float32),
        ],
        compiler_params=pltpu.CompilerParams(vmem_limit_bytes=48 * 2**20),
        name="attend",
    )(meta, queries, table, *key_rows, *value_rows)


def attend_back(meta, queries, key_rows, value_rows, table, grad_context, context, levels):
    row_count, width = queries.shape
    count = len(key_rows)
    key_count = row_count * count
    rows_out = jax.ShapeDtypeStruct((row_count, width), jnp.bfloat16)
    results = pl.pallas_call(
        functools.partial(attend_back_kernel, count),
        grid_spec=pltpu.PrefetchScalarGridSpec(
            num_scalar_prefetch=1,
            grid=(width // LANES,),
            in_specs=[
                pair_spec(row_count),
                fixed_spec(2 * LANES, LANES),
                pair_spec(row_count),
                pair_spec(row_count),
                fixed_spec(row_count, LANES),
            ]
            + [pair_spec(row_count)] * (2 * count),
            out_specs=[pair_spec(row_count), fixed_spec(LANES, 2 * LANES)]
            + [pair_spec(row_count)] * (2 * count),
            scratch_shapes=[
                pltpu.VMEM((2, row_count, key_count + 2 * LANES), jnp.float32),
                pltpu.VMEM((2, row_count, key_count), jnp.float32),
                pltpu.VMEM((2, row_count, key_count), jnp.bfloat16),
                pltpu.VMEM((2, row_count, key_count + 2 * LANES), jnp.bfloat16),
                pltpu.VMEM((2, row_count, 2 * LANES), jnp.bfloat16),
                pltpu.VMEM((key_count, 2 * LANES), jnp.bfloat16),
                pltpu.VMEM((2, key_count, LANES), jnp.bfloat16),
                pltpu.VMEM((key_count, LANES), jnp.bfloat16),
                pltpu.VMEM((key_count, LANES), jnp.bfloat16),
                pltpu.VMEM((key_count, LANES), jnp.float32),
            ],
        ),
        out_shape=[rows_out, jax.ShapeDtypeStruct((LANES, 2 * LANES), jnp.float32)]
        + [rows_out] * (2 * count),
        compiler_params=pltpu.CompilerParams(vmem_limit_bytes=48 * 2**20),
        name="attend_back",
    )(meta, queries, table, grad_context, context, levels, *key_rows, *value_rows)
    return results[0], results[2 : 2 + count], results[2 + count :], results[1]


def wide_table(table_low):
    places = jnp.arange(2 * LANES)
    offsets = jnp.clip(jnp.where(places < LANES, places, places - 2 * LANES) + LEFT, 0, OFFSETS - 1)
    rows = table_low[offsets]
    return jnp.concatenate([rows, rows], axis=1)


def table_grad(wide_grad):
    folded = (wide_grad[:HEAD_DIM] + wide_grad[HEAD_DIM:]).T
    first = jnp.sum(folded[LANES : 2 * LANES - LEFT + 1], axis=0, keepdims=True)
    last = jnp.sum(folded[RIGHT:LANES], axis=0, keepdims=True)
    return jnp.concatenate([first, folded[2 * LANES - LEFT + 1 :], folded[:RIGHT], last], axis=0)


def sigmoid(values):
    return 0.5 * jnp.tanh(0.5 * values) + 0.5


def swish_slope(values, logistic):
    return logistic + values * logistic * (1.0 - logistic)


def matmul(left_side, right_side):
    return dot_f32(left_side, right_side, NN)


def norm_rows(values, gain_row, shift_row):
    centred = values - jnp.mean(values, axis=-1, keepdims=True)
    variance = jnp.mean(centred * centred, axis=-1, keepdims=True)
    inverse = lax.rsqrt(variance + EPSILON)
    normal = centred * inverse
    return (normal * gain_row + shift_row, normal, inverse)


def norm_back(grad_out, normal, inverse, gain_row):
    grad_normal = grad_out * gain_row
    grad_in = inverse * (
        grad_normal
        - jnp.mean(grad_normal, axis=-1, keepdims=True)
        - normal * jnp.mean(grad_normal * normal, axis=-1, keepdims=True)
    )
    return (grad_in, jnp.sum(grad_out * normal, axis=0), jnp.sum(grad_out, axis=0))


CHUNK = 64
HALO = 32


def tap_slices(window, offsets):
    length = window.shape[0]
    slices = {}
    for rest in range(8):
        wanted = [offset for offset in offsets if offset % 8 == rest]
        if wanted:
            turned = pltpu.roll(window, length - rest, 0) if rest else window
            for offset in wanted:
                slices[offset] = turned[offset - rest : offset - rest + CHUNK]
    return slices


def convolve_kernel(before_ref, gated_ref, taps_ref, gain_ref, shift_ref, deep_ref, low_ref, padded_ref):
    row_count, width = gated_ref.shape
    lead = HALO - (KERNEL - 1)
    padded_ref[:HALO] = before_ref[...]
    padded_ref[HALO:] = gated_ref[...]

    @pl.loop(0, width // LANES)
    def _(column):
        lanes = pl.ds(pl.multiple_of(column * LANES, LANES), LANES)
        taps = [taps_ref[tap : tap + 1, lanes] for tap in range(KERNEL)]

        @pl.loop(0, row_count // CHUNK)
        def _(chunk):
            first = pl.multiple_of(chunk * CHUNK, CHUNK)
            window = padded_ref[pl.ds(first, CHUNK + HALO), lanes]
            slices = tap_slices(window, [tap + lead for tap in range(KERNEL)])
            total = taps[0] * slices[lead]
            for tap in range(1, KERNEL):
                total = total + taps[tap] * slices[tap + lead]
            deep_ref[pl.ds(first, CHUNK), lanes] = total

    @pl.loop(0, row_count // CHUNK)
    def _(chunk):
        rows = pl.ds(pl.multiple_of(chunk * CHUNK, CHUNK), CHUNK)
        deep_norm, _, _ = norm_rows(deep_ref[rows, :], gain_ref[...], shift_ref[...])
        low_ref[rows, :] = (deep_norm * sigmoid(deep_norm)).astype(jnp.bfloat16)


def convolve(before, gated, taps, gain_row, shift_row):
    shape = gated.shape
    return pl.pallas_call(
        convolve_kernel,
        in_specs=[pl.BlockSpec(memory_space=pltpu.VMEM)] * 5,
        out_specs=[pl.BlockSpec(memory_space=pltpu.VMEM)] * 2,
        out_shape=[
            jax.ShapeDtypeStruct(shape, jnp.float32),
            jax.ShapeDtypeStruct(shape, jnp.bfloat16),
        ],
        scratch_shapes=[pltpu.VMEM((shape[0] + HALO, shape[1]), jnp.float32)],
        compiler_params=pltpu.CompilerParams(vmem_limit_bytes=32 * 2**20),
        name="convolve",
    )(before, gated, taps, gain_row[None], shift_row[None])


def convolve_back_kernel(
    meta_ref, grad_ref, after_ref, before_ref, gated_ref, taps_ref, linear_ref, logistic_ref,
    pair_ref, tap_grad_ref, padded_ref, extended_ref,
):
    row_count, width = gated_ref.shape
    lead = HALO - (KERNEL - 1)
    padded_ref[:HALO] = before_ref[...]
    padded_ref[HALO:] = gated_ref[...]
    extended_ref[:row_count] = grad_ref[...]
    extended_ref[row_count:] = after_ref[...]
    live_rows = meta_ref[1] - meta_ref[0] * LANES

    @pl.loop(0, width // LANES)
    def _(column):
        start = pl.multiple_of(column * LANES, LANES)
        lanes = pl.ds(start, LANES)
        taps = [taps_ref[tap : tap + 1, lanes] for tap in range(KERNEL)]

        @pl.loop(0, row_count // CHUNK)
        def _(chunk):
            first = pl.multiple_of(chunk * CHUNK, CHUNK)
            rows = pl.ds(first, CHUNK)
            window = extended_ref[pl.ds(first, CHUNK + HALO), lanes]
            slices = tap_slices(window, [KERNEL - 1 - tap for tap in range(KERNEL)])
            total = taps[0] * slices[KERNEL - 1]
            for tap in range(1, KERNEL):
                total = total + taps[tap] * slices[KERNEL - 1 - tap]
            places = first + lax.broadcasted_iota(jnp.int32, (CHUNK, LANES), 0)
            logistic = logistic_ref[rows, lanes]
            grad_linear = jnp.where(places < live_rows, total, 0.0) * logistic
            pair_ref[rows, lanes] = grad_linear.astype(jnp.bfloat16)
            grad_gate = grad_linear * linear_ref[rows, lanes] * (1.0 - logistic)
            gate_lanes = pl.ds(pl.multiple_of(width + start, LANES), LANES)
            pair_ref[rows, gate_lanes] = grad_gate.astype(jnp.bfloat16)

        def tap_step(chunk, totals):
            first = pl.multiple_of(chunk * CHUNK, CHUNK)
            window = padded_ref[pl.ds(first, CHUNK + HALO), lanes]
            slices = tap_slices(window, [tap + lead for tap in range(KERNEL)])
            grad = extended_ref[pl.ds(first, CHUNK), lanes]
            added_up = []
            for tap in range(KERNEL):
                product = slices[tap + lead] * grad
                part = product[:8]
                for piece in range(1, CHUNK // 8):
                    part = part + product[8 * piece : 8 * piece + 8]
                added_up.append(totals[tap] + part)
            return tuple(added_up)

        zero = jnp.zeros((8, LANES), jnp.float32)
        totals = lax.fori_loop(0, row_count // CHUNK, tap_step, (zero,) * KERNEL)
        for tap in range(KERNEL):
            tap_grad_ref[tap : tap + 1, lanes] = jnp.sum(totals[tap], axis=0, keepdims=True)


def convolve_back(meta, grad_depth, after, before, gated, taps, linear, logistic):
    row_count, width = gated.shape
    vmem = pl.BlockSpec(memory_space=pltpu.VMEM)
    return pl.pallas_call(
        convolve_back_kernel,
        grid_spec=pltpu.PrefetchScalarGridSpec(
            num_scalar_prefetch=1,
            grid=(),
            in_specs=[vmem] * 7,
            out_specs=[vmem] * 2,
            scratch_shapes=[pltpu.VMEM((row_count + HALO, width), jnp.float32)] * 2,
        ),
        out_shape=[
            jax.ShapeDtypeStruct((row_count, 2 * width), jnp.bfloat16),
            jax.ShapeDtypeStruct(taps.shape, jnp.float32),
        ],
        compiler_params=pltpu.CompilerParams(vmem_limit_bytes=40 * 2**20),
        name="convolve_back",
    )(meta, grad_depth, after, before, gated, taps, linear, logistic)


def fence(*values):
    return lax.optimization_barrier(values)


TENSOR = ("far", "z")


class Place:
    def __init__(self):
        axes = ("y", "x", "core", "far", "z")
        self.count = {axis: lax.axis_size(axis) for axis in axes}
        self.index = {axis: lax.axis_index(axis) for axis in axes}
        count, index = self.count, self.index
        count["t"] = count["far"] * count["z"]
        index["t"] = index["far"] * count["z"] + index["z"]
        count["seq"] = count["far"] * 2
        index["seq"] = index["far"] * 2 + index["core"]
        count["a"], count["b"] = count["x"], count["y"]
        self.mixed = count["x"] == count["y"]
        self.names = {"t": TENSOR, "seq": ("core", "far")}
        self.dp_count = count["y"] * count["x"] * 2

    def seq_pair(self, start, end):
        far = self.count["far"]
        return ((start % 2) * far + start // 2, (end % 2) * far + end // 2)

    def turn(self, block, axis, step):
        size = self.count[axis]
        pairs = [(start, (start + step) % size) for start in range(size)]
        if axis == "seq":
            pairs = [self.seq_pair(*pair) for pair in pairs]
        if axis in ("a", "b"):
            y_count, x_count = self.count["y"], self.count["x"]
            pairs = []
            for y in range(y_count):
                for x in range(x_count):
                    for core in range(2):
                        along_x = (axis == "a") != (self.mixed and core == 1)
                        new_y = y if along_x else (y + step) % y_count
                        new_x = (x + step) % x_count if along_x else x
                        pairs.append(
                            ((y * x_count + x) * 2 + core, (new_y * x_count + new_x) * 2 + core)
                        )
            return lax.ppermute(block, ("y", "x", "core"), pairs)
        return lax.ppermute(block, self.names.get(axis, axis), pairs)

    def after(self, axis, step):
        return lax.rem(self.index[axis] + step, self.count[axis])

    def blocks_for(self, core):
        y_count, x_count = self.count["y"], self.count["x"]
        numbers = []
        for b_step in [*self.steps("b"), 0]:
            for a_step in [*self.steps("a"), 0]:
                y = lax.rem(self.index["y"] + b_step, y_count)
                x = lax.rem(self.index["x"] + a_step, x_count)
                if self.mixed:
                    y = jnp.where(core == 1, lax.rem(self.index["y"] + a_step, y_count), y)
                    x = jnp.where(core == 1, lax.rem(self.index["x"] + b_step, x_count), x)
                numbers.append((y * x_count + x) * 2 + core)
        return numbers

    def steps(self, axis):
        return range(1, self.count[axis])


def packed(shard):
    rows, columns = shard.shape
    blocks = shard.reshape(rows // columns, columns, columns)
    return blocks.transpose(1, 0, 2).reshape(columns, rows)


def gather_t_turned(place, shard):
    return jnp.stack([shard] + [place.turn(shard, "t", step) for step in place.steps("t")])


def gather_t(place, shard):
    return lax.all_gather(shard, TENSOR, axis=0)


def gather_a(place, stack):
    return jnp.concatenate([stack] + [place.turn(stack, "a", step) for step in place.steps("a")])


def gather_b(place, stack):
    return [stack] + [place.turn(stack, "b", step) for step in place.steps("b")]


def gather_core(place, stacks):
    return stacks + [place.turn(stack, "core", 1) for stack in stacks]


def assemble(place, stacks, targets, turned=False):
    counts, dp_count, t_count = place.count, place.dp_count, place.count["t"]
    dtype = stacks[0].dtype
    shard_shape = stacks[0].shape[1:]
    rows, columns = shard_shape[-2:]
    shapes, copy_counts = [], 0
    for target in targets:
        if target[0] == "rows":
            shapes.append((target[2], target[3] * dp_count, columns * t_count))
            copy_counts += dp_count * t_count
        elif target[0] == "columns":
            aligned = columns % LANES == 0
            shape = (rows * t_count, columns * dp_count)
            shapes.append(shape if aligned else (dp_count, rows * t_count, columns))
            copy_counts += dp_count * t_count
        elif target[0] == "packed":
            aligned = rows % LANES == 0
            shape = (columns * t_count, rows * dp_count)
            shapes.append(shape if aligned else (dp_count, t_count, rows, columns))
            copy_counts += dp_count * t_count * (columns // rows if aligned else 1)
        else:
            shapes.append((dp_count, target[2], columns))
            copy_counts += dp_count

    def kernel(meta_ref, *refs):
        stack_refs = refs[: len(stacks)]
        out_refs = refs[len(stacks) : len(stacks) + len(targets)]
        sem = refs[-1]
        copies = []

        def send(source, target):
            copy = pltpu.make_async_copy(source, target, sem.at[len(copies)])
            copy.start()
            copies.append(copy)

        b_count = counts["b"]
        for number, stack_ref in enumerate(stack_refs):
            other, b_step = number // b_count, number % b_count
            core = lax.rem(meta_ref[2] + other, 2)
            for a_step in range(counts["a"]):
                y_spot = lax.rem(meta_ref[0] - b_step + counts["y"], counts["y"])
                x_spot = lax.rem(meta_ref[1] - a_step + counts["x"], counts["x"])
                if place.mixed:
                    y_other = lax.rem(meta_ref[0] - a_step + counts["y"], counts["y"])
                    x_other = lax.rem(meta_ref[1] - b_step + counts["x"], counts["x"])
                    y_spot = jnp.where(core == 1, y_other, y_spot)
                    x_spot = jnp.where(core == 1, x_other, x_spot)
                dp_spot = (y_spot * counts["x"] + x_spot) * 2 + core
                for t_step in range(t_count):
                    t_spot = lax.rem(meta_ref[3] - t_step + t_count, t_count) if turned else t_step
                    shard_ref = stack_ref.at[a_step * t_count + t_step]
                    for target, out_ref in zip(targets, out_refs):
                        t_columns = pl.ds(pl.multiple_of(t_spot * columns, columns), columns)
                        if target[0] == "rows":
                            first, depth, count = target[1:]
                            source = shard_ref.at[first : first + depth, 0:count, :]
                            here = pl.ds(pl.multiple_of(dp_spot * count, count), count)
                            send(source, out_ref.at[:, here, t_columns])
                        elif target[0] == "columns":
                            here = pl.ds(pl.multiple_of(t_spot * rows, rows), rows)
                            if columns % LANES == 0:
                                there = pl.ds(pl.multiple_of(dp_spot * columns, columns), columns)
                                send(shard_ref, out_ref.at[here, there])
                            else:
                                send(shard_ref, out_ref.at[dp_spot, here, :])
                        elif target[0] == "packed":
                            if rows % LANES == 0:
                                there = pl.ds(pl.multiple_of(dp_spot * rows, rows), rows)
                                for part in range(columns // rows):
                                    here = pl.ds(
                                        pl.multiple_of(t_spot * columns + part * rows, rows), rows
                                    )
                                    send(
                                        shard_ref.at[target[1], :, part * rows : (part + 1) * rows],
                                        out_ref.at[here, there],
                                    )
                            else:
                                send(shard_ref.at[target[1]], out_ref.at[dp_spot, t_spot])
                        elif t_step == 0:
                            first_row, count = target[1:]
                            send(shard_ref.at[0, first_row : first_row + count, :], out_ref.at[dp_spot])
        for copy in copies:
            copy.wait()

    meta = jnp.stack([place.index[axis] for axis in ("y", "x", "core", "t")]).astype(jnp.int32)
    results = pl.pallas_call(
        kernel,
        grid_spec=pltpu.PrefetchScalarGridSpec(
            num_scalar_prefetch=1,
            grid=(),
            in_specs=[pl.BlockSpec(memory_space=pl.ANY)] * len(stacks),
            out_specs=[pl.BlockSpec(memory_space=pltpu.VMEM)] * len(targets),
            scratch_shapes=[pltpu.SemaphoreType.DMA((copy_counts,))],
        ),
        out_shape=[jax.ShapeDtypeStruct(shape, dtype) for shape in shapes],
        compiler_params=pltpu.CompilerParams(vmem_limit_bytes=20 * 2**20),
        name="assemble",
    )(meta, *stacks)
    finished = []
    for target, whole in zip(targets, results):
        if target[0] == "columns" and columns % LANES:
            whole = whole.transpose(1, 0, 2).reshape(rows * t_count, columns * dp_count)
        if target[0] == "packed" and rows % LANES:
            whole = whole.reshape(dp_count, t_count, rows, columns // rows, rows)
            whole = whole.transpose(1, 3, 2, 0, 4).reshape(columns * t_count, rows * dp_count)
        finished.append(whole)
    return finished


def sent_order(place, width):
    core = place.index["core"]
    numbers = jnp.stack(place.blocks_for(1 - core) + place.blocks_for(core))
    block = width // place.dp_count
    sources = (numbers[:, None] * block + jnp.arange(block)[None, :]).reshape(1, width)
    return (jnp.arange(width)[:, None] == sources).astype(jnp.bfloat16)


def other_products(pairs):
    result = []
    for inputs, grads in pairs:
        product = dot_f32(inputs[:, : inputs.shape[1] // 2], grads, TN).astype(jnp.bfloat16)
        result.append((inputs, grads, product))
    return result


def send_core(place, group):
    return [(inputs, grads, place.turn(product, "core", 1)) for inputs, grads, product in group]


def other_terms(place, pairs):
    return send_core(place, other_products(pairs))


def chip_terms(place, group):
    result = []
    for inputs, grads, other in group:
        half = inputs.shape[1] // 2
        step_rows = half // place.count["b"]
        terms = []
        for number in range(place.count["b"]):
            columns = slice(half + number * step_rows, half + (number + 1) * step_rows)
            rows = slice(number * step_rows, (number + 1) * step_rows)
            term = dot_f32(inputs[:, columns], grads, TN) + other[rows].astype(jnp.float32)
            terms.append(term.astype(jnp.bfloat16))
        result.append(terms)
    return result


def send_b(place, group):
    return [
        [place.turn(term, "b", step) for term, step in zip(terms, place.steps("b"))] + [terms[-1]]
        for terms in group
    ]


def added(arrays):
    total = arrays[0].astype(jnp.float32)
    for array in arrays[1:]:
        total = total + array.astype(jnp.float32)
    return total


def messages_a(place, group):
    result = []
    for arrived in group:
        step_rows = arrived[0].shape[0] // place.count["a"]
        messages = []
        for number in range(place.count["a"] - 1):
            rows = slice(number * step_rows, (number + 1) * step_rows)
            messages.append(added([one[rows] for one in arrived]).astype(jnp.bfloat16))
        result.append((messages, arrived))
    return result


def send_a(place, group):
    return [
        kept + [place.turn(message, "a", step) for message, step in zip(messages, place.steps("a"))]
        for messages, kept in group
    ]


def last_rows(kept):
    rows = kept[-1].shape[0]
    return added([one[-rows:] for one in kept])


def by_tensor(total, count):
    width = total.shape[1] // count
    return [total[:, number * width : (number + 1) * width] for number in range(count)]


def tensor_blocks(place, group):
    count = place.count["t"]
    blocks = [[] for _ in range(count)]
    for depth, kept in group:
        total = last_rows(kept).astype(jnp.bfloat16)
        for part in by_tensor(total, depth):
            for number, block in enumerate(by_tensor(part, count)):
                blocks[number].append(block)
    return jnp.stack([jnp.stack(block) for block in blocks])


def reduce_t(stack):
    return lax.psum_scatter(stack, TENSOR, scatter_dimension=0)


def reduce_t_vectors(place, kept, vectors):
    count = place.count["t"]
    total = last_rows(kept).astype(jnp.bfloat16)
    vector_count, columns = vectors.shape[0], total.shape[1] // count
    extra_rows = -(-vectors.size // (count * columns) // 16) * 16 if vectors.size else 0
    extra_rows = max(extra_rows, 16)
    width = vectors.shape[1] // count
    blocks = []
    for block, part in zip(by_tensor(total, count), by_tensor(vectors, count)):
        flat = part.astype(jnp.bfloat16).reshape(1, -1)
        flat = jnp.pad(flat, ((0, 0), (0, extra_rows * columns - flat.shape[1])))
        blocks.append(jnp.concatenate([block, flat.reshape(extra_rows, columns)]))
    result = lax.psum_scatter(jnp.stack(blocks), TENSOR, scatter_dimension=0)
    flat = result[-extra_rows:].reshape(-1)[: vector_count * width]
    return (result[:-extra_rows], flat.reshape(vector_count, width).astype(jnp.float32))


def reduce_vectors_core(place, columns):
    half = columns.shape[1] // 2
    total = columns[:, half:] + place.turn(columns[:, :half], "core", 1)
    return total


def reduce_vectors(place, total, axis):
    width = total.shape[1] // place.count[axis]
    arrived = total[:, -width:]
    for number, step in enumerate(place.steps(axis)):
        arrived = arrived + place.turn(total[:, number * width : (number + 1) * width], axis, step)
    return arrived


def clip_pairs(micro, z_count, step):
    return [
        (core * z_count + z, (z // micro) * z_count + micro * core + (step + z) % micro)
        for core in range(2)
        for z in range(z_count)
    ]


def clip_blocks(place, blocks):
    micro, z_here = blocks.shape[0], place.index["z"]
    return [
        lax.dynamic_index_in_dim(blocks, lax.rem(z_here + step, micro), 0, keepdims=False)
        for step in range(micro)
    ]


def to_clip(place, blocks):
    micro, z_count = len(blocks), place.count["z"]
    return [
        lax.ppermute(block, ("core", "z"), clip_pairs(micro, z_count, step))
        for step, block in enumerate(blocks)
    ]


def ordered_clip(place, arrived):
    micro, z_here = len(arrived), place.index["z"]
    stack = jnp.stack(arrived)
    ordered = [
        lax.dynamic_index_in_dim(stack, lax.rem(z_here - spot + micro, micro), 0, keepdims=False)
        for spot in range(micro)
    ]
    return jnp.concatenate(ordered, axis=0)


def own_blocks(place, rows_in, micro):
    z_here = place.index["z"]
    blocks = rows_in.reshape(micro, -1, rows_in.shape[-1])
    return [
        lax.dynamic_index_in_dim(blocks, lax.rem(z_here - step + micro, micro), 0, keepdims=False)
        for step in range(micro)
    ]


def from_clip(place, blocks):
    micro, z_count = len(blocks), place.count["z"]
    arrived = []
    for step, block in enumerate(blocks):
        pairs = [(end, start) for start, end in clip_pairs(micro, z_count, step)]
        arrived.append(lax.ppermute(block, ("core", "z"), pairs))
    return arrived


def own_clips(place, arrived):
    micro, z_here = len(arrived), place.index["z"]
    stack = jnp.stack(arrived)
    return jnp.stack(
        [
            lax.dynamic_index_in_dim(
                stack, lax.rem(number - lax.rem(z_here, micro) + micro, micro), 0, keepdims=False
            )
            for number in range(micro)
        ]
    )


def all_rows(place, own):
    return [own] + [place.turn(own, "seq", step) for step in place.steps("seq")]


def own_sum(place, parts):
    total = parts[0].astype(jnp.float32)
    for part, step in zip(parts[1:], place.steps("seq")):
        total = total + place.turn(part, "seq", step).astype(jnp.float32)
    return total


def neighbour_rows(place, rows_in, step):
    count = place.count["seq"]
    pairs = [
        place.seq_pair(start, start + step) for start in range(count) if 0 <= start + step < count
    ]
    return lax.ppermute(rows_in, place.names["seq"], pairs)


def feed_up(inputs, up_weight, up_bias, gain_row, shift_row):
    normed, normal, inverse = norm_rows(inputs, gain_row, shift_row)
    normed = normed.astype(jnp.bfloat16)
    upper_rows = matmul(normed, up_weight) + up_bias
    logistic = sigmoid(upper_rows)
    hidden = (upper_rows * logistic).astype(jnp.bfloat16)
    slope = swish_slope(upper_rows, logistic).astype(jnp.bfloat16)
    return (hidden, (normal, inverse, normed, slope))


def feed_back_down(grad_result, stored, down_weight):
    grad_low = grad_result.astype(jnp.bfloat16)
    grad_hidden = dot_f32(grad_low, down_weight, NT)
    grad_upper = (grad_hidden * stored[3].astype(jnp.float32)).astype(jnp.bfloat16)
    up_bias_grad = jnp.sum(grad_upper.astype(jnp.float32), axis=0)
    down_bias_grad = jnp.sum(grad_low.astype(jnp.float32), axis=0)
    return (grad_low, grad_upper, up_bias_grad, down_bias_grad)


def body(
    frames,
    cotangent,
    clip_valid,
    frame_counts,
    rel_rows,
    first_up,
    first_down,
    attend_in,
    attend_out,
    pointwise_in,
    pointwise_out,
    second_up,
    second_down,
    vectors,
    distance,
):
    place = Place()
    micro, _, width = frames.shape
    ratio_rows = FF // width
    attend_base = 3 + ratio_rows
    conv_base = attend_base + 5
    second_base = conv_base + 4
    final_base = second_base + 3 + ratio_rows
    taps_base = final_base + 2
    scale = HEAD_DIM ** (-0.5)
    order = sent_order(place, width)

    def sent(rows_low):
        return matmul(rows_low, order).astype(jnp.bfloat16)

    up_rows, up_columns = first_up.shape
    vector_rows = 16
    vector_parts = up_columns // vectors.shape[1]
    padded_vectors = jnp.pad(vectors, ((0, vector_rows * vector_parts - vectors.shape[0]), (0, 0)))
    vector_shard = (
        padded_vectors.reshape(vector_parts, vector_rows, -1).transpose(1, 0, 2).reshape(vector_rows, -1)
    )
    shard_up_one = jnp.concatenate([first_up, vector_shard], axis=0)[None]
    shard_mix = jnp.concatenate(
        [attend_in, packed(attend_out)[None], pointwise_in, packed(pointwise_out)[None]]
    )

    own_facts = jnp.stack([clip_valid, frame_counts])
    up_one = gather_t_turned(place, shard_up_one)
    up_one, first_down, own_facts = fence(up_one, first_down, own_facts)
    up_one = gather_a(place, up_one)
    down_one = gather_t(place, first_down)
    other_facts = place.turn(own_facts, "core", 1)
    up_one, frames, shard_mix, other_facts = fence(up_one, frames, shard_mix, other_facts)
    up_one = gather_b(place, up_one)
    rows_low = to_clip(place, clip_blocks(place, frames))
    down_one = gather_a(place, down_one)
    both_mix = gather_t(place, shard_mix)
    up_one, down_one, second_up = fence(up_one, down_one, second_up)
    up_one = gather_core(place, up_one)
    down_one = gather_b(place, down_one)
    up_one, down_one, second_up = fence(up_one, down_one, second_up)
    attend_mix = gather_a(place, both_mix[:, : attend_in.shape[0] + 1])
    point_mix = both_mix[:, attend_in.shape[0] + 1 :]
    up_two = gather_t(place, second_up[None])
    up_one, vector_slabs = assemble(
        place, up_one, [("rows", 0, 1, up_rows), ("slabs", up_rows, vector_rows)], turned=True
    )
    up_one = up_one[0]
    vector_wide = vector_slabs.reshape(place.dp_count, vector_rows, vector_parts, -1)
    vector_wide = vector_wide.transpose(2, 1, 0, 3).reshape(vector_rows * vector_parts, width)
    vector_wide = vector_wide[: vectors.shape[0]].astype(jnp.float32)

    rows_in = ordered_clip(place, rows_low).astype(jnp.float32)
    row_count = rows_in.shape[0]
    z_here = place.index["z"]
    facts = jnp.where(z_here // micro == place.index["core"], own_facts, other_facts)
    facts = lax.dynamic_index_in_dim(facts, lax.rem(z_here, micro), 1, keepdims=False)
    valid_flag = (facts[0] > 0).astype(jnp.float32)
    first_row = place.index["seq"] * row_count
    live = ((first_row + jnp.arange(row_count)) < facts[1]).astype(jnp.float32)[:, None]
    meta = jnp.stack([place.index["seq"] * (row_count // LANES), facts[1], place.index["seq"]])
    meta = meta.astype(jnp.int32)
    pick_rows = (rel_rows[:, None] == jnp.arange(OFFSETS)[None, :]).astype(jnp.bfloat16)
    table = wide_table(matmul(pick_rows, distance).astype(jnp.bfloat16))

    one_hidden, one_kept = feed_up(
        rows_in,
        up_one,
        vector_wide[2 : 2 + ratio_rows].reshape(FF),
        vector_wide[0],
        vector_wide[1],
    )
    (down_one, attend_mix, point_mix, second_down, one_hidden, one_kept, table) = fence(
        down_one, attend_mix, point_mix, second_down, one_hidden, one_kept, table
    )
    down_one = gather_core(place, down_one)
    attend_mix = gather_b(place, attend_mix)
    point_mix = gather_a(place, point_mix)
    down_two = gather_t(place, second_down)
    (down_one,) = assemble(place, down_one, [("columns",)])
    after_one = rows_in + 0.5 * (matmul(one_hidden, down_one) + vector_wide[2 + ratio_rows])
    attend_normed, attend_normal, attend_inverse = norm_rows(
        after_one, vector_wide[attend_base], vector_wide[attend_base + 1]
    )
    attend_normed = attend_normed.astype(jnp.bfloat16)
    (attend_mix, point_mix, up_two, after_one, attend_normed, attend_normal, attend_inverse) = fence(
        attend_mix, point_mix, up_two, after_one, attend_normed, attend_normal, attend_inverse
    )
    attend_mix = gather_core(place, attend_mix)
    point_mix = gather_b(place, point_mix)
    up_two = gather_a(place, up_two)
    attend_mix, attend_back_weight = assemble(place, attend_mix, [("rows", 0, 3, up_rows), ("packed", 3)])
    queries = (matmul(attend_normed, attend_mix[0]) + vector_wide[attend_base + 2]).astype(jnp.bfloat16)
    queries = (queries.astype(jnp.float32) * scale).astype(jnp.bfloat16)
    own_keys = matmul(attend_normed, attend_mix[1]).astype(jnp.bfloat16)
    own_values = (matmul(attend_normed, attend_mix[2]) + vector_wide[attend_base + 3]).astype(jnp.bfloat16)
    key_rows, value_rows = all_rows(place, own_keys), all_rows(place, own_values)
    (point_mix, up_two, down_two, cotangent, queries, key_rows, value_rows) = fence(
        point_mix, up_two, down_two, cotangent, queries, key_rows, value_rows
    )
    point_mix = gather_core(place, point_mix)
    up_two = gather_b(place, up_two)
    down_two = gather_a(place, down_two)
    cot_low = to_clip(place, clip_blocks(place, cotangent))
    context, levels = attend(meta, queries, key_rows, value_rows, table)
    (point_mix, up_two, down_two, context, levels, after_one) = fence(
        point_mix, up_two, down_two, context, levels, after_one
    )
    down_two = gather_b(place, down_two)
    up_two = gather_core(place, up_two)
    point_mix, point_back = assemble(place, point_mix, [("rows", 0, 2, up_rows), ("packed", 2)])
    after_two = after_one + matmul(context, attend_back_weight) + vector_wide[attend_base + 4]
    conv_normed, conv_normal, conv_inverse = norm_rows(
        after_two, vector_wide[conv_base], vector_wide[conv_base + 1]
    )
    conv_normed = conv_normed.astype(jnp.bfloat16)
    linear = matmul(conv_normed, point_mix[0])
    logistic = sigmoid(matmul(conv_normed, point_mix[1]))
    gated = linear * logistic * live
    taps = vector_wide[taps_base : taps_base + KERNEL]
    before = neighbour_rows(place, gated[-HALO:], 1)
    deep_gain, deep_shift = vector_wide[conv_base + 2], vector_wide[conv_base + 3]
    depth_out, activated = convolve(before, gated, taps, deep_gain, deep_shift)
    after_three = after_two + matmul(activated, point_back)
    (up_two, down_two, cot_low, after_three, depth_out, activated) = fence(
        up_two, down_two, cot_low, after_three, depth_out, activated
    )
    down_two = gather_core(place, down_two)
    (up_two,) = assemble(place, up_two, [("rows", 0, 1, up_rows)])
    up_two = up_two[0]
    two_hidden, two_kept = feed_up(
        after_three,
        up_two,
        vector_wide[second_base + 2 : second_base + 2 + ratio_rows].reshape(FF),
        vector_wide[second_base],
        vector_wide[second_base + 1],
    )
    (down_two, two_hidden, two_kept, up_two) = fence(down_two, two_hidden, two_kept, up_two)
    (down_two,) = assemble(place, down_two, [("columns",)])
    two_out = matmul(two_hidden, down_two) + vector_wide[second_base + 2 + ratio_rows]
    after_four = after_three + 0.5 * two_out
    final_rows, final_normal, final_inverse = norm_rows(
        after_four, vector_wide[final_base], vector_wide[final_base + 1]
    )
    row_out = jnp.where(valid_flag > 0, final_rows, rows_in).astype(jnp.bfloat16)
    rows_cot = ordered_clip(place, cot_low).astype(jnp.float32)
    grad_four, final_gain_grad, final_shift_grad = norm_back(
        rows_cot * valid_flag, final_normal, final_inverse, vector_wide[final_base]
    )
    grad_low, grad_upper, two_up_bias, two_down_bias = feed_back_down(
        0.5 * grad_four, two_kept, down_two
    )
    sum_down_two = other_terms(place, [(sent(grad_low), two_hidden)])
    (sum_down_two, grad_four, grad_upper, row_out) = fence(sum_down_two, grad_four, grad_upper, row_out)
    sum_down_two = send_b(place, chip_terms(place, sum_down_two))
    frames_out = from_clip(place, own_blocks(place, row_out, micro))
    sum_up_two = other_terms(place, [(sent(two_kept[2]), grad_upper)])
    grad_normed = dot_f32(grad_upper, up_two, NT)
    grad_two_in, two_gain, two_shift = norm_back(
        grad_normed, two_kept[0], two_kept[1], vector_wide[second_base]
    )
    grad_three = grad_four + grad_two_in
    conv_low = grad_three.astype(jnp.bfloat16)
    deep_norm, deep_normal, deep_inverse = norm_rows(depth_out, deep_gain, deep_shift)
    grad_deep = dot_f32(conv_low, point_back, NT) * swish_slope(deep_norm, sigmoid(deep_norm))
    grad_depth, deep_gain_grad, deep_shift_grad = norm_back(
        grad_deep, deep_normal, deep_inverse, deep_gain
    )
    after = neighbour_rows(place, grad_depth[:HALO], -1)
    (sum_down_two, sum_up_two, grad_three, conv_low, grad_depth, after, frames_out) = fence(
        sum_down_two, sum_up_two, grad_three, conv_low, grad_depth, after, frames_out
    )
    sum_down_two = send_a(place, messages_a(place, sum_down_two))
    sum_up_two = send_b(place, chip_terms(place, sum_up_two))
    grad_pair, tap_grads = convolve_back(
        meta, grad_depth, after, before, gated, taps, linear, logistic
    )
    (sum_down_two, sum_up_two, grad_pair) = fence(sum_down_two, sum_up_two, grad_pair)
    sum_down_two = reduce_t(tensor_blocks(place, [(1, sum_down_two[0])]))
    sum_up_two = send_a(place, messages_a(place, sum_up_two))
    sum_point = other_terms(
        place,
        [
            (sent(conv_normed), grad_pair),
            (sent(conv_low), activated),
        ],
    )
    grad_conv_normed = dot_f32(grad_pair[:, :width], point_mix[0], NT)
    grad_conv_normed = grad_conv_normed + dot_f32(grad_pair[:, width:], point_mix[1], NT)
    grad_conv_in, conv_gain_grad, conv_shift_grad = norm_back(
        grad_conv_normed, conv_normal, conv_inverse, vector_wide[conv_base]
    )
    grad_two = grad_three + grad_conv_in
    attend_low = grad_two.astype(jnp.bfloat16)
    grad_context = dot_f32(attend_low, attend_back_weight, NT).astype(jnp.bfloat16)
    (sum_up_two, sum_point, grad_two, attend_low, grad_context) = fence(
        sum_up_two, sum_point, grad_two, attend_low, grad_context
    )
    sum_up_two = reduce_t(tensor_blocks(place, [(1, sum_up_two[0])]))
    sum_point = send_b(place, chip_terms(place, sum_point))
    grad_queries, part_keys, part_values, grad_table = attend_back(
        meta, queries, key_rows, value_rows, table, grad_context, context, levels
    )
    (sum_point, grad_queries, part_keys, part_values, grad_table, sum_down_two) = fence(
        sum_point, grad_queries, part_keys, part_values, grad_table, sum_down_two
    )
    sum_point = send_a(place, messages_a(place, sum_point))
    grad_keys = own_sum(place, part_keys).astype(jnp.bfloat16)
    grad_values = own_sum(place, part_values).astype(jnp.bfloat16)
    sum_distance = jnp.dot(
        pick_rows.astype(jnp.float32).T, table_grad(grad_table), precision=lax.Precision.HIGHEST
    )
    sent_attend, sent_out = sent(attend_normed), sent(attend_low)
    (sum_point, sum_distance, grad_keys, grad_values, sum_up_two, sent_attend, sent_out) = fence(
        sum_point, sum_distance, grad_keys, grad_values, sum_up_two, sent_attend, sent_out
    )
    sum_attend = other_terms(
        place,
        [
            (sent_attend, jnp.concatenate([grad_queries, grad_keys, grad_values], axis=1)),
            (sent_out, context),
        ],
    )
    sum_distance = sum(
        [place.turn(sum_distance, "t", step) for step in place.steps("t")], sum_distance
    )
    sum_attend = chip_terms(place, sum_attend)
    sum_point = tensor_blocks(place, [(2, sum_point[0]), (1, sum_point[1])])
    grad_attend_normed = (
        dot_f32(grad_queries, attend_mix[0], NT)
        + dot_f32(grad_keys, attend_mix[1], NT)
        + dot_f32(grad_values, attend_mix[2], NT)
    )
    grad_attend_in, attend_gain_grad, attend_shift_grad = norm_back(
        grad_attend_normed, attend_normal, attend_inverse, vector_wide[attend_base]
    )
    grad_one = grad_two + grad_attend_in
    (sum_point, sum_attend, sum_distance, grad_one) = fence(sum_point, sum_attend, sum_distance, grad_one)
    sum_attend = send_b(place, sum_attend)
    sum_point = reduce_t(sum_point)
    grad_low, grad_upper, one_up_bias, one_down_bias = feed_back_down(0.5 * grad_one, one_kept, down_one)
    sum_down_one = other_products([(sent(grad_low), one_hidden)])
    sum_up_one = other_products([(sent(one_kept[2]), grad_upper)])
    (sum_attend, grad_upper, sum_distance, sum_down_one, sum_up_one, one_up_bias) = fence(
        sum_attend, grad_upper, sum_distance, sum_down_one, sum_up_one, one_up_bias
    )
    sum_attend = send_a(place, messages_a(place, sum_attend))
    sum_down_one = send_core(place, sum_down_one)
    sum_up_one = send_core(place, sum_up_one)
    sum_down_one = chip_terms(place, sum_down_one)
    sum_distance = sum_distance + place.turn(sum_distance, "core", 1)
    sum_attend = tensor_blocks(place, [(3, sum_attend[0]), (1, sum_attend[1])])
    (sum_attend, sum_down_one, sum_up_one, grad_upper, sum_distance, sum_point) = fence(
        sum_attend, sum_down_one, sum_up_one, grad_upper, sum_distance, sum_point
    )
    sum_down_one = send_b(place, sum_down_one)
    sum_attend = reduce_t(sum_attend)
    sum_up_one = chip_terms(place, sum_up_one)
    sum_distance = sum(
        [place.turn(sum_distance, "b", step) for step in place.steps("b")], sum_distance
    )
    grad_normed = dot_f32(grad_upper, up_one, NT)
    grad_one_in, one_gain, one_shift = norm_back(grad_normed, one_kept[0], one_kept[1], vector_wide[0])
    grad_rows = grad_one + grad_one_in + (1.0 - valid_flag) * rows_cot

    grad_blocks = own_blocks(place, grad_rows.astype(jnp.bfloat16), micro)
    (sum_attend, sum_down_one, sum_up_one, grad_blocks, one_gain, one_shift, sum_distance) = fence(
        sum_attend, sum_down_one, sum_up_one, grad_blocks, one_gain, one_shift, sum_distance
    )
    sum_down_one = send_a(place, messages_a(place, sum_down_one))
    sum_up_one = send_b(place, sum_up_one)
    frames_grad = from_clip(place, grad_blocks)
    sum_distance = sum(
        [place.turn(sum_distance, "a", step) for step in place.steps("a")], sum_distance
    )

    def column_sum(rows):
        return jnp.sum(rows.astype(jnp.float32), axis=0)

    vector_part = jnp.concatenate(
        [
            jnp.stack([one_gain, one_shift]),
            one_up_bias.reshape(ratio_rows, width),
            jnp.stack(
                [
                    one_down_bias,
                    attend_gain_grad,
                    attend_shift_grad,
                    column_sum(grad_queries),
                    column_sum(grad_values),
                    column_sum(attend_low),
                    conv_gain_grad,
                    conv_shift_grad,
                    deep_gain_grad,
                    deep_shift_grad,
                    two_gain,
                    two_shift,
                ]
            ),
            two_up_bias.reshape(ratio_rows, width),
            jnp.stack([two_down_bias, final_gain_grad, final_shift_grad]),
            tap_grads[:KERNEL],
        ],
        axis=0,
    )
    vector_part = jnp.dot(vector_part, order.astype(jnp.float32), precision=lax.Precision.HIGHEST)
    sum_vectors = reduce_vectors_core(place, vector_part)
    (sum_up_one, sum_down_one, sum_vectors, frames_grad) = fence(
        sum_up_one, sum_down_one, sum_vectors, frames_grad
    )
    sum_up_one = send_a(place, messages_a(place, sum_up_one))
    sum_down_one = reduce_t(tensor_blocks(place, [(1, sum_down_one[0])]))
    sum_vectors = reduce_vectors(place, sum_vectors, "b")
    sum_vectors = reduce_vectors(place, sum_vectors, "a")
    (sum_up_one, sum_vectors) = fence(sum_up_one, sum_vectors)
    sum_up_one, grad_vectors = reduce_t_vectors(place, sum_up_one[0], sum_vectors)
    wide = jnp.float32
    return (
        own_clips(place, frames_out),
        own_clips(place, frames_grad),
        sum_up_one.astype(wide),
        sum_down_one[0].T.astype(wide),
        sum_attend[:3].astype(wide),
        sum_attend[3].T.astype(wide),
        sum_point[:2].astype(wide),
        sum_point[2].T.astype(wide),
        sum_up_two[0].astype(wide),
        sum_down_two[0].T.astype(wide),
        grad_vectors,
        sum_distance,
    )


def solution(mesh):
    dp_count, tensor_count = mesh.shape["dp"], mesh.shape["tensor"]

    def program(*arrays):
        group = 2 * (arrays[0].shape[0] // dp_count)
        parted = Mesh(
            mesh.devices.reshape(dp_count // 4, 2, 2, tensor_count // group, group),
            ("y", "x", "core", "far", "z"),
        )
        dp, tensor = ("y", "x", "core"), TENSOR
        return jax.shard_map(
            body,
            mesh=parted,
            in_specs=(
                P(dp, tensor, None),
                P(dp, tensor, None),
                P(dp),
                P(dp),
                P(),
                P(dp, tensor),
                P(tensor, dp),
                P(None, dp, tensor),
                P(tensor, dp),
                P(None, dp, tensor),
                P(tensor, dp),
                P(dp, tensor),
                P(tensor, dp),
                P(None, dp),
                P(),
            ),
            out_specs=(
                P(dp, tensor, None),
                P(dp, tensor, None),
                P(dp, tensor),
                P(tensor, dp),
                P(None, dp, tensor),
                P(tensor, dp),
                P(None, dp, tensor),
                P(tensor, dp),
                P(dp, tensor),
                P(tensor, dp),
                P(None, dp + tensor),
                P(),
            ),
            check_vma=False,
        )(*arrays)

    return program
```
